256 devices in a mesh: expert: 32 (over x, z), dp: 8 (over y, core).
Axes of the slice: x: 4, y: 4, z: 8, core: 2. Of those that a mesh axis runs over, the one named last changes fastest.
Arguments:
- incoming_elements: bfloat16 [33792, 768], P(('expert', 'dp')), may hold values from -6 to 6
- assigned_specialist: int32 [33792, 1], P(('expert', 'dp')), may hold values from 0 to 31; in each aligned block of 132 rows (0 to 131, 132 to 263, ...) at most 9 rows name the same one
- element_couple_kind: int32 [33792], P(('expert', 'dp')), may hold values from 0 to 3, as said below
- chosen_specialist_chance: float32 [33792], P(('expert', 'dp')), may hold values from 0.2 to 1
- specialist_layernorm_multiplier: float32 [768], replicated, may hold values from 0.5 to 1.5
- final_layernorm_multiplier_vec: float32 [768], replicated, may hold values from 0.5 to 1.5
- specialist_first_matrix: bfloat16 [32, 768, 3072], P('expert'), may hold values from -0.21875 to 0.21875
- specialist_second_matrix: bfloat16 [32, 3072, 768], P('expert'), may hold values from -0.109375 to 0.109375
- sharpness_factor: float32 [1], replicated, may hold values from 16 to 48
- similarity_shift_term: float32 [1], replicated, may hold values from -4 to -1
- objective_adjoint_factor: float32 [1], replicated, may hold values from 12288 to 49152
Outputs:
- token_grads: bfloat16 [33792, 768], P(('expert', 'dp'))
- grad_in: bfloat16 [32, 768, 3072], P('expert', None, 'dp')
- grad_out: bfloat16 [32, 3072, 768], P('expert', 'dp')
The draws below stay inside these ranges and needn't reach their ends.
Inputs may be any that keep to these rules, and one draw needn't show every extreme that they name: `assigned_specialist`: no expert is named by more than 9 rows of one device (aligned blocks of 132 rows), and in some device's rows one expert is named exactly 9 times. `element_couple_kind`: within the rows of one device (aligned blocks of 132 rows), each value k below 2 marks the image tokens of local pair k and appears exactly 50 times; each value k from 2 on marks the text tokens of local pair k - 2 and appears exactly 16 times; the order within a block is arbitrary.
All inputs are finite; a program needn't handle non-finite values.
Results may differ from the reference program's by a relative error of at most 0.019.
Values may be sent and summed in bfloat16 or wider, within the bound.
No kernel may reach another device: no remote copies, remote signals or barrier semaphores. Data moves between devices by JAX's collectives and lax.ppermute only.
A program may use at most 128 MiB of HBM per device.

```python
import math
import jax
import jax.numpy as jnp
import numpy as np
from jax import lax

D = 768
H = 3072
IMG = 50
TXT = 16
E = 32
PAIRS_DEV = 2
TOK_DEV = 132
CAP = 9
PAIRS = 512
TOKENS = 33792
N_EXPERT = 32
N_DP = 8


def couple_kinds(key):
    key = jax.random.fold_in(key, 11)
    index = jnp.arange(TOK_DEV, dtype=jnp.int32)
    split = PAIRS_DEV * IMG
    base = jnp.where(index < split, index // IMG, PAIRS_DEV + (index - split) // TXT).astype(jnp.int32)
    blocks = TOKENS // TOK_DEV
    keys = jax.random.split(key, blocks)
    shuffled = jax.vmap(lambda single: jax.random.permutation(single, base))(keys)
    return shuffled.reshape(TOKENS).astype(jnp.int32)


def draw_element_couple_kind(key, part):
    return couple_kinds(key)


def draw_incoming_elements(key, part):
    kinds = couple_kinds(key)
    key = jax.random.fold_in(key, 5)
    noise_key, latent_key = jax.random.split(key)
    block = (jnp.arange(TOKENS, dtype=jnp.int32) // TOK_DEV).astype(jnp.int32)
    local_pair = jnp.where(kinds < PAIRS_DEV, kinds, kinds - PAIRS_DEV).astype(jnp.int32)
    pair_index = (block * PAIRS_DEV + local_pair).astype(jnp.int32)
    half = PAIRS // 2
    latent_index = (pair_index % half).astype(jnp.int32)
    latent = jax.random.normal(latent_key, (half, D), jnp.float32)
    noise = jax.random.normal(noise_key, (TOKENS, D), jnp.float32)
    values = 0.6 * noise + 0.8 * latent[latent_index]
    return jnp.clip(values, -6.0, 6.0).astype(jnp.bfloat16)


def level_of(rng, shape, cuts, smallest, largest):
    def one(dim, shards_of):
        steps = jax.random.uniform(jax.random.fold_in(jax.random.fold_in(rng, 6), dim), (shards_of,), jnp.float32, smallest / len(cuts), largest / len(cuts))
        return jnp.repeat(jnp.exp(steps), shape[dim] // shards_of).reshape((-1,) + (1,) * (len(shape) - dim - 1))

    factor_of = one(*cuts[0])
    for cut in cuts[1:]:
        factor_of = factor_of * one(*cut)
    return factor_of


def routed_block(key, own, number, rows, amount, top, reach, skew):
    sequence = jax.random.permutation(key, amount)
    crowded, usual = portions_of(amount, rows * top, reach, skew, True), portions_of(amount, rows * top, reach, skew, False)
    places = jnp.arange(amount)

    def named(lengths, offset_by):
        used = int((lengths > 0).sum())
        fixed = max(1, used // 4)
        passed = fixed + (places - fixed + offset_by * (used - fixed)) % max(1, amount - fixed)
        return jnp.zeros((amount,), jnp.int32).at[sequence[jnp.where(places < fixed, places, passed)]].set(jnp.asarray(lengths, jnp.int32))

    lengths = jnp.where(number % 4 == 0, named(crowded, number // 4), named(usual, number - number // 4 - 1))
    mixed = jax.random.permutation(jax.random.fold_in(own, 3), amount)
    donor, receiver = mixed[0:amount // 2 * 2:2], mixed[1:amount // 2 * 2:2]
    room = jnp.minimum(lengths[donor] - 1, reach - lengths[receiver]) // 2
    room = jnp.where((donor == sequence[0]) | (receiver == sequence[0]) | (lengths[receiver] == 0), 0, jnp.maximum(room, 0))
    passed = jax.random.randint(jax.random.fold_in(own, 4), (amount // 2,), 0, 1 << 20) % (room + 1)
    lengths = lengths.at[donor].add(-passed).at[receiver].add(passed)
    items = jnp.searchsorted(jnp.cumsum(lengths), jnp.arange(rows * top), side="right").astype(jnp.int32)
    listing = items.reshape(top, rows).T
    listing = listing[jax.random.permutation(jax.random.fold_in(own, 1), rows)]
    offset_by = jax.random.randint(jax.random.fold_in(own, 2), (rows, 1), 0, top)
    return jnp.take_along_axis(listing, (jnp.arange(top)[None, :] + offset_by) % top, axis=1)


def portions_of(amount, total, limit, skew, full):
    loads = [(1 << 20) // math.isqrt(rank ** skew) + 1 for rank in range(1, amount + 1)]
    largest = limit if full else min(limit, max(-(-total // amount), total * loads[0] // sum(loads)))
    least = 1 if total - largest >= amount - 1 else 0
    given, spare = [largest] + [least] * (amount - 1), total - largest - least * (amount - 1)
    while spare > 0:
        candidates = [i for i in range(1, amount) if given[i] < largest] or [i for i in range(1, amount) if given[i] < limit]
        pool, left = sum([loads[i] for i in candidates]), spare
        for i in candidates:
            more = min(limit - given[i], max(1, left * loads[i] // pool), spare)
            given[i] = given[i] + more
            spare = spare - more
    return np.array(given)


def scatter_about(own_key, dims, scale, most, cuts=(), kind=jnp.bfloat16):
    factor_of = level_of(own_key, dims, cuts, -0.22, 0.18) if cuts else 1.0
    entries = jax.random.normal(own_key, dims, jnp.float32) * scale * factor_of
    return jnp.minimum(jnp.maximum(entries, -most), most).astype(kind)


def setup_inputs(seed: int = 0) -> dict:
    seeds = jax.random.split(jax.random.key(seed), 12)
    incoming_elements = draw_incoming_elements(jax.random.fold_in(seeds[11], 71), 0)
    assigned_specialist_keys = jax.random.split(jax.random.fold_in(seeds[1], 1), TOKENS // TOK_DEV)
    assigned_specialist_turns = jax.random.permutation(jax.random.fold_in(seeds[1], 3), TOKENS // TOK_DEV)
    assigned_specialist = jax.vmap(lambda own, number: routed_block(jax.random.fold_in(seeds[1], 2), own, number, TOK_DEV, E, 1, CAP, 2))(assigned_specialist_keys, assigned_specialist_turns).reshape((TOKENS, 1))
    element_couple_kind = draw_element_couple_kind(jax.random.fold_in(seeds[11], 71), 0)
    chosen_specialist_chance = jnp.clip(0.2 + 0.8 * jax.random.uniform(seeds[3], (TOKENS,), jnp.float32) ** level_of(seeds[3], (TOKENS,), ((0, 256),), -0.2, 0.2), 0.2, 1.0)
    specialist_layernorm_multiplier = jnp.clip(1.0 + 0.1 * jax.random.normal(seeds[4], (D,), jnp.float32), 0.5, 1.5)
    final_layernorm_multiplier_vec = jnp.clip(1.0 + 0.1 * jax.random.normal(seeds[5], (D,), jnp.float32), 0.5, 1.5)
    specialist_first_matrix = scatter_about(seeds[6], (E, D, H), D ** -0.5, 0.21875, ((0, 32),))
    specialist_second_matrix = scatter_about(seeds[7], (E, H, D), H ** -0.5, 0.109375, ((0, 32),))
    sharpness_factor = jnp.clip(jnp.exp(jax.random.uniform(seeds[8], (1,), jnp.float32, math.log(16.0), math.log(48.0))), 16.0, 48.0)
    similarity_shift_term = jnp.clip(jax.random.uniform(seeds[9], (1,), jnp.float32, -4.0, -1.0), -4.0, -1.0)
    objective_adjoint_factor = jnp.clip(jnp.exp(jax.random.uniform(seeds[10], (1,), jnp.float32, math.log(12288.0), math.log(49152.0))), 12288.0, 49152.0)
    return dict(incoming_elements=incoming_elements, assigned_specialist=assigned_specialist, element_couple_kind=element_couple_kind, chosen_specialist_chance=chosen_specialist_chance, specialist_layernorm_multiplier=specialist_layernorm_multiplier, final_layernorm_multiplier_vec=final_layernorm_multiplier_vec, specialist_first_matrix=specialist_first_matrix, specialist_second_matrix=specialist_second_matrix, sharpness_factor=sharpness_factor, similarity_shift_term=similarity_shift_term, objective_adjoint_factor=objective_adjoint_factor)


epsilon = 1e-06
maximal_accuracy = lax.Precision.HIGHEST
root_half = 0.7071067811865476
inverse_root_tau = 0.3989422804014327

def layer_norm(values, gain):
    center = values - lax.optimization_barrier(jnp.mean(values, axis=1, keepdims=True))
    inverse = lax.rsqrt(lax.optimization_barrier(jnp.mean(center * center, axis=1, keepdims=True)) + epsilon)
    scaled = center * inverse
    return (scaled * gain[None, :], scaled, inverse)

def norm_back(upstream, gain, scaled, inverse):
    grad_hat = upstream * gain[None, :]
    return inverse * (grad_hat - lax.optimization_barrier(jnp.mean(grad_hat, axis=1, keepdims=True)) - scaled * lax.optimization_barrier(jnp.mean(grad_hat * scaled, axis=1, keepdims=True)))

def gelu_exact(values):
    return 0.5 * values * (1.0 + lax.erf(values * root_half))

def gelu_slope(values):
    return 0.5 * (1.0 + lax.erf(values * root_half)) + values * jnp.exp(-0.5 * values * values) * inverse_root_tau

def pair_slope(similarity_scores, labels, multiplier, count):
    signs = 2.0 * labels - 1.0
    return -(multiplier / count) * signs * jax.nn.sigmoid(-signs * similarity_scores)

def reference(incoming_elements, assigned_specialist, element_couple_kind, chosen_specialist_chance, specialist_layernorm_multiplier, final_layernorm_multiplier_vec, specialist_first_matrix, specialist_second_matrix, sharpness_factor, similarity_shift_term, objective_adjoint_factor):
    blocks = N_EXPERT * N_DP
    inputs = incoming_elements.astype(jnp.float32)
    normed, scaled_in, inverse_in = layer_norm(inputs, specialist_layernorm_multiplier)
    normed_b = normed.astype(jnp.bfloat16)
    route = assigned_specialist[:, 0].astype(jnp.int32)
    owner = (jnp.arange(TOKENS, dtype=jnp.int32) // TOK_DEV).astype(jnp.int32)
    onehot = (route[:, None] == jnp.arange(E, dtype=jnp.int32)[None, :]).astype(jnp.int32)
    running = jnp.cumsum(onehot.reshape(blocks, TOK_DEV, E), axis=1).reshape(TOKENS, E)
    position = lax.optimization_barrier(jnp.sum((running - 1) * onehot, axis=1)).astype(jnp.int32)

    def dispatch(values):
        buffer = jnp.zeros((E, blocks, CAP, D), values.dtype)
        return buffer.at[route, owner, position].set(values).reshape(E, blocks * CAP, D)

    def collect(buffer):
        return buffer.reshape(E, blocks, CAP, D)[route, owner, position]
    sent = dispatch(normed_b)

    def forward_expert(items):
        rows_in, first_w, second_w = items
        pre_act = jnp.dot(rows_in.astype(jnp.float32), first_w.astype(jnp.float32), precision=maximal_accuracy)
        hidden = gelu_exact(pre_act).astype(jnp.bfloat16)
        return jnp.dot(hidden.astype(jnp.float32), second_w.astype(jnp.float32), precision=maximal_accuracy).astype(jnp.bfloat16)
    returned = lax.map(forward_expert, (sent, specialist_first_matrix, specialist_second_matrix))
    expert_rows = collect(returned).astype(jnp.float32)
    mixed = inputs + chosen_specialist_chance[:, None] * expert_rows
    final, scaled_out, inverse_out = layer_norm(mixed, final_layernorm_multiplier_vec)
    group = (owner * (2 * PAIRS_DEV) + element_couple_kind).astype(jnp.int32)
    sums = jax.ops.segment_sum(final, group, num_segments=blocks * 2 * PAIRS_DEV)
    counts = jnp.where(jnp.arange(2 * PAIRS_DEV) < PAIRS_DEV, IMG, TXT).astype(jnp.float32)
    counts_all = jnp.tile(counts, blocks)
    pooled = sums / counts_all[:, None]
    inverse_norm = lax.rsqrt(lax.optimization_barrier(jnp.sum(pooled * pooled, axis=1)) + epsilon)
    unit = (pooled * inverse_norm[:, None]).astype(jnp.bfloat16)
    arranged = unit.reshape(blocks, 2, PAIRS_DEV, D)
    picture_vectors = arranged[:, 0].reshape(PAIRS, D)
    caption_vectors = arranged[:, 1].reshape(PAIRS, D)
    similarity_sharpness = sharpness_factor[0]
    starting_shift = similarity_shift_term[0]
    multiplier = objective_adjoint_factor[0]
    similarity_scores = similarity_sharpness * jnp.dot(picture_vectors, caption_vectors.T, preferred_element_type=jnp.float32) + starting_shift
    labels = jnp.eye(PAIRS, dtype=jnp.float32)
    derivative_factor = pair_slope(similarity_scores, labels, multiplier, PAIRS)
    picture_vector_derivs = similarity_sharpness * jnp.dot(derivative_factor, caption_vectors.astype(jnp.float32), precision=maximal_accuracy)
    caption_vector_derivs = similarity_sharpness * jnp.dot(derivative_factor.T, picture_vectors.astype(jnp.float32), precision=maximal_accuracy)
    grad_unit = jnp.stack([picture_vector_derivs.reshape(blocks, PAIRS_DEV, D), caption_vector_derivs.reshape(blocks, PAIRS_DEV, D)], axis=1)
    grad_unit = grad_unit.reshape(blocks * 2 * PAIRS_DEV, D)
    inner = lax.optimization_barrier(jnp.sum(pooled * grad_unit, axis=1))
    grad_pooled = grad_unit * inverse_norm[:, None] - pooled * (inverse_norm ** 3 * inner)[:, None]
    grad_final = (grad_pooled / counts_all[:, None])[group]
    grad_mixed = norm_back(grad_final, final_layernorm_multiplier_vec, scaled_out, inverse_out)
    grad_rows = (chosen_specialist_chance[:, None] * grad_mixed).astype(jnp.bfloat16)
    grad_sent = dispatch(grad_rows)

    def backward_expert(items):
        rows_in, rows_grad, first_w, second_w = items
        first_f = first_w.astype(jnp.float32)
        second_f = second_w.astype(jnp.float32)
        pre_act = jnp.dot(rows_in.astype(jnp.float32), first_f, precision=maximal_accuracy)
        hidden = gelu_exact(pre_act).astype(jnp.bfloat16)
        grad_hidden = (jnp.dot(rows_grad.astype(jnp.float32), second_f.T, precision=maximal_accuracy) * gelu_slope(pre_act)).astype(jnp.bfloat16)
        grad_back = jnp.dot(grad_hidden.astype(jnp.float32), first_f.T, precision=maximal_accuracy).astype(jnp.bfloat16)
        groups_in = rows_in.reshape(N_EXPERT, N_DP, CAP, D).astype(jnp.float32)
        groups_grad = rows_grad.reshape(N_EXPERT, N_DP, CAP, D).astype(jnp.float32)
        groups_hidden = grad_hidden.reshape(N_EXPERT, N_DP, CAP, H).astype(jnp.float32)
        groups_act = hidden.reshape(N_EXPERT, N_DP, CAP, H).astype(jnp.float32)
        part_in = jnp.einsum('adch,adcm->dhm', groups_hidden, groups_in, precision=maximal_accuracy)
        part_out = jnp.einsum('adch,adcm->dhm', groups_act, groups_grad, precision=maximal_accuracy)
        total_in = lax.optimization_barrier(jnp.sum(lax.optimization_barrier(part_in.astype(jnp.bfloat16)).astype(jnp.float32), axis=0))
        total_out = lax.optimization_barrier(jnp.sum(lax.optimization_barrier(part_out.astype(jnp.bfloat16)).astype(jnp.float32), axis=0))
        return (grad_back, total_in.T.astype(jnp.bfloat16), total_out.astype(jnp.bfloat16))
    grad_back_all, grad_in, grad_out = lax.map(backward_expert, (sent, grad_sent, specialist_first_matrix, specialist_second_matrix))
    grad_normed = collect(grad_back_all).astype(jnp.float32)
    token_grads = (grad_mixed + norm_back(grad_normed, specialist_layernorm_multiplier, scaled_in, inverse_in)).astype(jnp.bfloat16)
    return (token_grads, grad_in, grad_out)
```

```python
import functools

import jax
import jax.numpy as jnp
from jax import lax
from jax.experimental import pallas as pl
from jax.experimental.pallas import tpu as pltpu
from jax.sharding import PartitionSpec as P

D = 768
H = 3072
IMG = 50
TXT = 16
E = 32
DP = 8
NX = 4
NZ = 8
TOK = 132
CAP = 9
PAIRS = 512
ROWS = E * CAP
LANES = 128
CHUNKS = D // LANES
SLAB = 56
META = CAP * CHUNKS
PACKED = E * SLAB
HB = 512
HS = H // DP
GROUP = 4 * E

EPS = 1e-06
ROOT_HALF = 0.7071067811865476
INV_ROOT_TAU = 0.3989422804014327
BF = jnp.bfloat16
F32 = jnp.float32


def params(mib):
    return pltpu.CompilerParams(vmem_limit_bytes=mib * 1024 * 1024)


def cost(flops, moved, trans=0):
    return pl.CostEstimate(flops=int(flops), bytes_accessed=int(moved), transcendentals=int(trans))


def dot(a, b, ca=1, cb=0):
    return lax.dot_general(a, b, (((ca,), (cb,)), ((), ())), preferred_element_type=F32)


def norm(values):
    center = values - jnp.mean(values, axis=1, keepdims=True)
    inverse = lax.rsqrt(jnp.mean(center * center, axis=1, keepdims=True) + EPS)
    return center * inverse, inverse


def norm_back(grad_hat, scaled, inverse):
    return inverse * (
        grad_hat
        - jnp.mean(grad_hat, axis=1, keepdims=True)
        - scaled * jnp.mean(grad_hat * scaled, axis=1, keepdims=True)
    )


def gelu_parts(v):
    cdf = 0.5 * (1.0 + lax.erf(v * ROOT_HALF))
    return v * cdf, cdf + v * jnp.exp(-0.5 * v * v) * INV_ROOT_TAU


def three(v):
    hi = v.astype(BF).astype(F32)
    mid = (v - hi).astype(BF).astype(F32)
    return hi, mid, v - hi - mid


def iota(shape, dim):
    return lax.broadcasted_iota(jnp.int32, shape, dim)


def pack_rows(scr, rows):
    for j in range(CAP):
        for c in range(CHUNKS):
            scr[pl.ds(c * CAP + j, E, stride=SLAB), :] = rows[
                j * E : (j + 1) * E, c * LANES : (c + 1) * LANES
            ]


def unpack_rows(scr, rows):
    for j in range(CAP):
        for c in range(CHUNKS):
            rows[j * E : (j + 1) * E, c * LANES : (c + 1) * LANES] = scr[
                pl.ds(c * CAP + j, E, stride=SLAB), :
            ]


def meta_chance(meta, j):
    return meta[:, j : j + 1] + meta[:, 16 + j : 17 + j] + meta[:, 32 + j : 33 + j]


def meta_kind(meta, k, j):
    lane = 48 + 16 * k + j
    return meta[:, lane : lane + 1]


def dispatch_kernel(x, route_row, route_col, kind, chance, out, slot, scr, rows):
    onehot_t = (iota((E, TOK), 0) == route_row[...]).astype(F32)
    upper = (iota((TOK, TOK), 0) <= iota((TOK, TOK), 1)).astype(BF)
    run_t = dot(onehot_t.astype(BF), upper)
    pos_row = jnp.sum(onehot_t * run_t, axis=0, keepdims=True).astype(jnp.int32) - 1
    target = pos_row * E + route_row[...]
    placing = (iota((ROWS, TOK), 0) == target).astype(F32).astype(BF)
    rows[...] = dot(placing, x[...])

    onehot = (iota((TOK, E), 1) == route_col[...]).astype(F32)
    lower = (iota((TOK, TOK), 0) >= iota((TOK, TOK), 1)).astype(BF)
    run = dot(lower, onehot.astype(BF))
    pos = jnp.sum(onehot * run, axis=1, keepdims=True).astype(jnp.int32) - 1
    slot[...] = pos * E + route_col[...]
    lane = iota((TOK, LANES), 1)
    field = lane // 16
    hi, mid, low = three(chance[...])
    held = jnp.where(
        field == 0,
        hi,
        jnp.where(
            field == 1,
            mid,
            jnp.where(field == 2, low, (kind[...] == field - 3).astype(F32)),
        ),
    )
    held = jnp.where(lane % 16 == pos, held, 0.0).astype(BF)
    scr[...] = jnp.zeros_like(scr)
    scr[pl.ds(META, E, stride=SLAB), :] = dot(onehot_t.astype(BF), held)
    pack_rows(scr, rows)
    out[...] = scr[...].astype(BF)


def dispatch(x, route, kind, chance):
    return pl.pallas_call(
        dispatch_kernel,
        out_shape=(
            jax.ShapeDtypeStruct((PACKED, LANES), BF),
            jax.ShapeDtypeStruct((TOK, 1), jnp.int32),
        ),
        scratch_shapes=[pltpu.VMEM((PACKED, LANES), F32), pltpu.VMEM((ROWS, D), F32)],
        compiler_params=params(16),
        cost_estimate=cost(2 * ROWS * TOK * D, 700000),
    )(x, route.reshape(1, TOK), route.reshape(TOK, 1), kind.reshape(TOK, 1), chance.reshape(TOK, 1))


def forward_kernel(
    arr, gain_in, gain_out, w1, w2, part, bundle, slope, inv_out, scr, x, normed, acc, sums, ordered
):
    step = pl.program_id(0)

    @pl.when(step == 0)
    def _():
        scr[...] = arr[...].astype(F32)
        unpack_rows(scr, x)
        scaled, _ = norm(x[...])
        normed[...] = (scaled * gain_in[...]).astype(BF)
        acc[...] = jnp.zeros_like(acc)

    hidden, grad = gelu_parts(dot(normed[...], w1[...]))
    slope[...] = grad.astype(BF)
    acc[...] += dot(hidden.astype(BF), w2[...])

    @pl.when(step == pl.num_programs(0) - 1)
    def _():
        meta = scr[pl.ds(META, E, stride=SLAB), :]
        sums[...] = jnp.zeros_like(sums)
        lane = iota((E, LANES), 1)
        routing = jnp.where(lane >= 48, meta, 0.0)
        for j in range(CAP):
            at = slice(j * E, (j + 1) * E)
            chance = meta_chance(meta, j)
            mixed = x[at, :] + chance * acc[at, :].astype(BF).astype(F32)
            scaled, inverse = norm(mixed)
            bundle[at, :] = scaled.astype(BF)
            inv_out[at, :] = inverse
            final = scaled * gain_out[...]
            for k in range(4):
                sums[k * E : (k + 1) * E, :] += meta_kind(meta, k, j) * final
            for f, v in enumerate(three(chance * inverse)):
                routing = jnp.where(lane == 16 * f + j, v, routing)
        bundle[ROWS:, :] = jnp.zeros((E, D), BF)
        bundle[ROWS:, :LANES] = routing.astype(BF)
        for c in range(CHUNKS):
            for k in range(4):
                for xs in range(NX):
                    first = k * E + xs * NZ
                    ordered[c, pl.ds(k * NX + xs, NZ, stride=16), :] = sums[
                        first : first + NZ, c * LANES : (c + 1) * LANES
                    ]
            part[:, c * LANES : (c + 1) * LANES] = ordered[c].astype(BF)


def whole(shape):
    return pl.BlockSpec(shape, lambda *_: (0,) * len(shape))


def forward(arr, gain_in, gain_out, w1, w2):
    return pl.pallas_call(
        forward_kernel,
        grid=(H // HB,),
        in_specs=[
            whole((PACKED, LANES)),
            whole((1, D)),
            whole((1, D)),
            pl.BlockSpec((D, HB), lambda i: (0, i)),
            pl.BlockSpec((HB, D), lambda i: (i, 0)),
        ],
        out_specs=(
            whole((GROUP, D)),
            whole((ROWS + E, D)),
            pl.BlockSpec((ROWS, HB), lambda i: (0, i)),
            whole((ROWS, 1)),
        ),
        out_shape=(
            jax.ShapeDtypeStruct((GROUP, D), BF),
            jax.ShapeDtypeStruct((ROWS + E, D), BF),
            jax.ShapeDtypeStruct((ROWS, H), BF),
            jax.ShapeDtypeStruct((ROWS, 1), F32),
        ),
        scratch_shapes=[
            pltpu.VMEM((PACKED, LANES), F32),
            pltpu.VMEM((ROWS, D), F32),
            pltpu.VMEM((ROWS, D), BF),
            pltpu.VMEM((ROWS, D), F32),
            pltpu.VMEM((GROUP, D), F32),
            pltpu.VMEM((CHUNKS, GROUP, LANES), F32),
        ],
        compiler_params=params(28),
        cost_estimate=cost(4 * ROWS * D * H, 4 * D * H, 2 * ROWS * H),
    )(arr, gain_in, gain_out, w1, w2)


def loss_kernel(scalars, near, far, own, every, unit, inverse, img, txt, ordered):
    sharpness, shift, factor = scalars[0], scalars[1], scalars[2]
    half = PAIRS // DP
    for i in range(DP):
        src = near if i < DP // 2 else far
        first = (i % (DP // 2)) * GROUP
        pooled = src[first : first + GROUP, :].astype(F32)
        inv = lax.rsqrt(jnp.sum(pooled * pooled, axis=1, keepdims=True) + EPS)
        u = pooled * inv
        unit[i * GROUP : (i + 1) * GROUP, :] = u
        inverse[i * GROUP : (i + 1) * GROUP, :] = inv
        u = u.reshape(NZ, 2 * NZ, D)
        img[i * half : (i + 1) * half, :] = u[:, :NZ].reshape(half, D).astype(BF)
        txt[i * half : (i + 1) * half, :] = u[:, NZ:].reshape(half, D).astype(BF)
    logits = sharpness * dot(img[...], txt[...], 1, 1) + shift
    diagonal = iota((PAIRS, PAIRS), 0) == iota((PAIRS, PAIRS), 1)
    sign = jnp.where(diagonal, 1.0, -1.0)
    slope = (-(factor / PAIRS) * sharpness) * sign * jax.nn.sigmoid(-sign * logits)
    hi = slope.astype(BF)
    low = (slope - hi.astype(F32)).astype(BF)
    g_img = dot(hi, txt[...]) + dot(low, txt[...])
    g_txt = dot(hi, img[...], 0, 0) + dot(low, img[...], 0, 0)
    for i in range(DP):
        a = g_img[i * half : (i + 1) * half].reshape(NZ, NZ, D)
        b = g_txt[i * half : (i + 1) * half].reshape(NZ, NZ, D)
        inner = iota((NZ, 2 * NZ, 1), 1)
        grad = jnp.concatenate([a, b], axis=1).reshape(GROUP, D)
        count = jnp.where(inner < NZ, 1.0 / IMG, 1.0 / TXT).reshape(GROUP, 1)
        u = unit[i * GROUP : (i + 1) * GROUP, :]
        inv = inverse[i * GROUP : (i + 1) * GROUP, :] * count
        grad = inv * (grad - u * jnp.sum(u * grad, axis=1, keepdims=True))
        for c in range(CHUNKS):
            ordered[c] = grad[:, c * LANES : (c + 1) * LANES]
        for c in range(CHUNKS):
            cols = slice(c * LANES, (c + 1) * LANES)
            for k in range(4):
                rows = jnp.concatenate(
                    [ordered[c, pl.ds(k * NX + xs, NZ, stride=16), :] for xs in range(NX)], axis=0
                )
                every[i, k * E : (k + 1) * E, cols] = rows.astype(BF)
                if i == 0:
                    own[k * E : (k + 1) * E, cols] = rows


def loss(scalars, near, far):
    vm = pl.BlockSpec(memory_space=pltpu.VMEM)
    return pl.pallas_call(
        loss_kernel,
        in_specs=[pl.BlockSpec(memory_space=pltpu.SMEM), vm, vm],
        out_specs=(vm, vm),
        out_shape=(
            jax.ShapeDtypeStruct((GROUP, D), F32),
            jax.ShapeDtypeStruct((DP, GROUP, D), BF),
        ),
        scratch_shapes=[
            pltpu.VMEM((DP * GROUP, D), F32),
            pltpu.VMEM((DP * GROUP, 1), F32),
            pltpu.VMEM((PAIRS, D), BF),
            pltpu.VMEM((PAIRS, D), BF),
            pltpu.VMEM((CHUNKS, GROUP, LANES), F32),
        ],
        compiler_params=params(40),
        cost_estimate=cost(10 * PAIRS * PAIRS * D, 5000000, PAIRS * PAIRS),
    )(scalars, near, far)


def spread(grads, meta, j):
    rows = meta_kind(meta, 0, j) * grads[0:E, :]
    for k in range(1, 4):
        rows += meta_kind(meta, k, j) * grads[k * E : (k + 1) * E, :]
    return rows


def backward_kernel(
    arr, bundle, inv_out, grads, gain_in, gain_out, slope, w1, w2, out, scr, x, mixed, rows, acc
):
    step = pl.program_id(0)

    @pl.when(step == 0)
    def _():
        scr[...] = arr[...].astype(F32)
        unpack_rows(scr, x)
        meta = scr[pl.ds(META, E, stride=SLAB), :]
        for j in range(CAP):
            at = slice(j * E, (j + 1) * E)
            q = spread(grads, meta, j) * gain_out[...]
            grad = norm_back(q, bundle[at, :].astype(F32), inv_out[at, :])
            mixed[at, :] = grad
            rows[at, :] = (meta_chance(meta, j) * grad).astype(BF)
        acc[...] = jnp.zeros_like(acc)

    hidden = (dot(rows[...], w2[...], 1, 1) * slope[...].astype(F32)).astype(BF)
    acc[...] += dot(hidden, w1[...], 1, 1)

    @pl.when(step == pl.num_programs(0) - 1)
    def _():
        scaled, inverse = norm(x[...])
        back = acc[...].astype(BF).astype(F32) * gain_in[...]
        mixed[...] += norm_back(back, scaled, inverse)
        pack_rows(scr, mixed)
        out[...] = scr[...].astype(BF)


def backward(arr, bundle, inv_out, grads, gain_in, gain_out, slope, w1, w2):
    return pl.pallas_call(
        backward_kernel,
        grid=(H // HB,),
        in_specs=[
            whole((PACKED, LANES)),
            whole((ROWS + E, D)),
            whole((ROWS, 1)),
            whole((GROUP, D)),
            whole((1, D)),
            whole((1, D)),
            pl.BlockSpec((ROWS, HB), lambda i: (0, i)),
            pl.BlockSpec((D, HB), lambda i: (0, i)),
            pl.BlockSpec((HB, D), lambda i: (i, 0)),
        ],
        out_specs=whole((PACKED, LANES)),
        out_shape=jax.ShapeDtypeStruct((PACKED, LANES), BF),
        scratch_shapes=[
            pltpu.VMEM((PACKED, LANES), F32),
            pltpu.VMEM((ROWS, D), F32),
            pltpu.VMEM((ROWS, D), F32),
            pltpu.VMEM((ROWS, D), BF),
            pltpu.VMEM((ROWS, D), F32),
        ],
        compiler_params=params(28),
        cost_estimate=cost(4 * ROWS * D * H, 4 * D * H + 2 * ROWS * H),
    )(arr, bundle, inv_out, grads, gain_in, gain_out, slope, w1, w2)


def slice_kernel(dp, arr, gain_in, w1, normed, hidden, slope, scr, x):
    scr[...] = arr[0].astype(F32)
    unpack_rows(scr, x)
    scaled, _ = norm(x[...])
    rows = (scaled * gain_in[...]).astype(BF)
    normed[0] = rows
    value, grad = gelu_parts(dot(rows, w1[...]))
    hidden[0] = value.astype(BF)
    slope[0] = grad.astype(BF)


def hidden_slice(dp, arrs, gain_in, w1):
    group = lambda rows, cols: pl.BlockSpec((1, rows, cols), lambda h, dp: (h, 0, 0))
    return pl.pallas_call(
        slice_kernel,
        grid_spec=pltpu.PrefetchScalarGridSpec(
            num_scalar_prefetch=1,
            grid=(DP,),
            in_specs=[
                group(PACKED, LANES),
                whole((1, D)),
                pl.BlockSpec((D, HS), lambda h, dp: (0, dp[0])),
            ],
            out_specs=(group(ROWS, D), group(ROWS, HS), group(ROWS, HS)),
            scratch_shapes=[pltpu.VMEM((PACKED, LANES), F32), pltpu.VMEM((ROWS, D), F32)],
        ),
        out_shape=(
            jax.ShapeDtypeStruct((DP, ROWS, D), BF),
            jax.ShapeDtypeStruct((DP, ROWS, HS), BF),
            jax.ShapeDtypeStruct((DP, ROWS, HS), BF),
        ),
        compiler_params=params(24),
        cost_estimate=cost(2 * DP * ROWS * D * HS, 12000000, 2 * DP * ROWS * HS),
    )(dp, arrs, gain_in, w1)


def weights_kernel(
    dp, bundle, grads, normed, hidden, slope, gain_out, w2, g_in, g_out, rows, acc_in, acc_out
):
    step = pl.program_id(0)

    @pl.when(step == 0)
    def _():
        acc_in[...] = jnp.zeros_like(acc_in)
        acc_out[...] = jnp.zeros_like(acc_out)

    meta = bundle[0, ROWS:, :LANES].astype(F32)
    every = grads[0].astype(F32)
    for j in range(CAP):
        at = slice(j * E, (j + 1) * E)
        q = spread(every, meta, j) * gain_out[...]
        grad = norm_back(q, bundle[0, at, :].astype(F32), meta_chance(meta, j))
        rows[at, :] = grad.astype(BF)
    g_rows = rows[...]
    g_hidden = (dot(g_rows, w2[...], 1, 1) * slope[0].astype(F32)).astype(BF)
    acc_in[...] += dot(normed[0], g_hidden, 0, 0)
    acc_out[...] += dot(hidden[0], g_rows, 0, 0)

    @pl.when(step == pl.num_programs(0) - 1)
    def _():
        g_in[...] = acc_in[...].astype(BF)
        g_out[...] = acc_out[...].astype(BF)


def weight_grads(dp, bundles, grads, normed, hidden, slope, gain_out, w2):
    def place(h, dp):
        m = lax.bitwise_xor(h, dp[0])
        return (lax.div(m, 2) + 4 * lax.rem(m, 2), 0, 0)

    group = lambda rows, cols: pl.BlockSpec((1, rows, cols), lambda h, dp: (h, 0, 0))
    return pl.pallas_call(
        weights_kernel,
        grid_spec=pltpu.PrefetchScalarGridSpec(
            num_scalar_prefetch=1,
            grid=(DP,),
            in_specs=[
                group(ROWS + E, D),
                pl.BlockSpec((1, GROUP, D), place),
                group(ROWS, D),
                group(ROWS, HS),
                group(ROWS, HS),
                whole((1, D)),
                pl.BlockSpec((HS, D), lambda h, dp: (dp[0], 0)),
            ],
            out_specs=(whole((D, HS)), whole((HS, D))),
            scratch_shapes=[
                pltpu.VMEM((ROWS, D), BF),
                pltpu.VMEM((D, HS), F32),
                pltpu.VMEM((HS, D), F32),
            ],
        ),
        out_shape=(
            jax.ShapeDtypeStruct((D, HS), BF),
            jax.ShapeDtypeStruct((HS, D), BF),
        ),
        compiler_params=params(24),
        cost_estimate=cost(6 * DP * ROWS * D * HS, 15000000),
    )(dp, bundles, grads, normed, hidden, slope, gain_out, w2)


def collect_kernel(arr, slot, out, scr, rows):
    scr[...] = arr[...].astype(F32)
    unpack_rows(scr, rows)
    taking = (iota((TOK, ROWS), 1) == slot[...]).astype(F32).astype(BF)
    out[...] = dot(taking, rows[...].astype(BF)).astype(BF)


def collect(arr, slot):
    return pl.pallas_call(
        collect_kernel,
        out_shape=jax.ShapeDtypeStruct((TOK, D), BF),
        scratch_shapes=[pltpu.VMEM((PACKED, LANES), F32), pltpu.VMEM((ROWS, D), F32)],
        compiler_params=params(16),
        cost_estimate=cost(2 * ROWS * TOK * D, 700000),
    )(arr, slot)


Z_GROUPS = [[x * NZ + z for z in range(NZ)] for x in range(NX)]


def to_experts(packed):
    slabs = packed.reshape(E, SLAB, LANES)
    slabs = lax.all_to_all(slabs, "expert", split_axis=0, concat_axis=0, tiled=True)
    return slabs.reshape(PACKED, LANES)


def along_z(values):
    return lax.all_to_all(
        values, "expert", split_axis=0, concat_axis=0, tiled=True, axis_index_groups=Z_GROUPS
    )


def swap(values, axis, size, by):
    return lax.ppermute(values, axis, [(i, i ^ by) for i in range(size)])


def on_device(
    incoming_elements,
    assigned_specialist,
    element_couple_kind,
    chosen_specialist_chance,
    specialist_layernorm_multiplier,
    final_layernorm_multiplier_vec,
    specialist_first_matrix,
    specialist_second_matrix,
    sharpness_factor,
    similarity_shift_term,
    objective_adjoint_factor,
):
    gain_in = specialist_layernorm_multiplier.reshape(1, D)
    gain_out = final_layernorm_multiplier_vec.reshape(1, D)
    w1 = specialist_first_matrix[0]
    w2 = specialist_second_matrix[0]
    dp = lax.axis_index("dp").astype(jnp.int32).reshape(1)

    packed, slot = dispatch(
        incoming_elements, assigned_specialist, element_couple_kind, chosen_specialist_chance
    )
    arr = to_experts(packed)
    arrs = lax.all_gather(arr, "dp", axis=0)
    part, bundle, slope, inv_out = forward(arr, gain_in, gain_out, w1, w2)
    bundles = lax.all_gather(bundle, "dp", axis=0)

    part = along_z(part.reshape(NZ, 2 * NZ, D))
    part = jnp.sum(part.astype(F32), axis=0)
    others = [swap(part, "expert", E, NZ * m) for m in range(1, NX)]
    share = jnp.where(jnp.arange(2 * NZ) < NZ, 1.0 / IMG, 1.0 / TXT).astype(F32)
    pooled = (((part + others[0]) + (others[1] + others[2])) * share[:, None]).astype(BF)
    pooled = along_z(jnp.broadcast_to(pooled[None], (NZ, 2 * NZ, D))).reshape(GROUP, D)
    near = jnp.concatenate([pooled] + [swap(pooled, "dp", DP, m) for m in (2, 4, 6)], axis=0)
    far = swap(near, "dp", DP, 1)

    scalars = jnp.concatenate([sharpness_factor, similarity_shift_term, objective_adjoint_factor])
    own, every = loss(scalars, near, far)
    packed = backward(arr, bundle, inv_out, own, gain_in, gain_out, slope, w1, w2)
    returned = to_experts(packed)

    normed, hidden, grads = hidden_slice(dp, arrs, gain_in, w1)
    grad_in, grad_out = weight_grads(dp, bundles, every, normed, hidden, grads, gain_out, w2)
    token_grads = collect(returned, slot)
    return (token_grads, grad_in[None], grad_out[None])


def solution(mesh):
    return jax.shard_map(
        on_device,
        mesh=mesh,
        in_specs=(
            P(("expert", "dp"), None),
            P(("expert", "dp"), None),
            P(("expert", "dp")),
            P(("expert", "dp")),
            P(),
            P(),
            P("expert", None, None),
            P("expert", None, None),
            P(),
            P(),
            P(),
        ),
        out_specs=(P(("expert", "dp"), None), P("expert", None, "dp"), P("expert", "dp", None)),
        check_vma=False,
    )
```

```python
import jax
import jax.numpy as jnp
from jax import lax
from jax.experimental import pallas as pl
from jax.experimental.pallas import tpu as pltpu
from jax.sharding import PartitionSpec as P

D = 768
H = 3072
IMG = 50
TXT = 16
E = 32
DP = 8
NX = 4
NZ = 8
TOK = 132
CAP = 9
PAIRS = 512
ROWS = E * CAP
LANES = 128
CHUNKS = D // LANES
SLAB = 56
META = CAP * CHUNKS
PACKED = E * SLAB
HB = 1024
HS = H // DP
GROUP = 4 * E

EPS = 1e-06
ROOT_HALF = 0.7071067811865476
INV_ROOT_TAU = 0.3989422804014327
BF = jnp.bfloat16
F32 = jnp.float32


def params(mib):
    return pltpu.CompilerParams(vmem_limit_bytes=mib * 1024 * 1024)


def cost(flops, moved, trans=0):
    return pl.CostEstimate(flops=int(flops), bytes_accessed=int(moved), transcendentals=int(trans))


def dot(a, b, ca=1, cb=0):
    return lax.dot_general(a, b, (((ca,), (cb,)), ((), ())), preferred_element_type=F32)


def norm(values):
    center = values - jnp.mean(values, axis=1, keepdims=True)
    inverse = lax.rsqrt(jnp.mean(center * center, axis=1, keepdims=True) + EPS)
    return center * inverse, inverse


def norm_back(grad_hat, scaled, inverse):
    return inverse * (
        grad_hat
        - jnp.mean(grad_hat, axis=1, keepdims=True)
        - scaled * jnp.mean(grad_hat * scaled, axis=1, keepdims=True)
    )


def gelu_parts(v):
    e = jnp.exp(-0.5 * v * v)
    t = pl.reciprocal(1.0 + (0.3275911 * ROOT_HALF) * jnp.abs(v))
    tail = t * (0.5 * 1.061405429) + (0.5 * -1.453152027)
    tail = t * tail + (0.5 * 1.421413741)
    tail = t * tail + (0.5 * -0.284496736)
    tail = t * tail + (0.5 * 0.254829592)
    tail = t * tail * e
    cdf = jnp.where(v < 0.0, tail, 1.0 - tail)
    return v * cdf, cdf + v * e * INV_ROOT_TAU


def three(v):
    hi = v.astype(BF).astype(F32)
    mid = (v - hi).astype(BF).astype(F32)
    return hi, mid, v - hi - mid


def iota(shape, dim):
    return lax.broadcasted_iota(jnp.int32, shape, dim)


def pack_rows(scr, rows):
    for j in range(CAP):
        for c in range(CHUNKS):
            scr[pl.ds(c * CAP + j, E, stride=SLAB), :] = rows[
                j * E : (j + 1) * E, c * LANES : (c + 1) * LANES
            ]


def unpack_rows(scr, rows):
    for j in range(CAP):
        for c in range(CHUNKS):
            rows[j * E : (j + 1) * E, c * LANES : (c + 1) * LANES] = scr[
                pl.ds(c * CAP + j, E, stride=SLAB), :
            ]


def meta_chance(meta, j):
    return meta[:, j : j + 1] + meta[:, 16 + j : 17 + j] + meta[:, 32 + j : 33 + j]


def fill_hot(hot, meta):
    s, lane = iota((E, GROUP), 0), iota((E, GROUP), 1)
    first = (s % NZ) * (4 * NX) + s // NZ
    marks = [(lane == first + NX * k).astype(F32) for k in range(4)]
    for j in range(CAP):
        rows = jnp.zeros((E, GROUP), F32)
        for k in range(4):
            at = 48 + 16 * k + j
            rows += marks[k] * meta[:, at : at + 1]
        hot[j * E : (j + 1) * E, :GROUP] = rows.astype(BF)


def two(v):
    hi = v.astype(BF)
    return hi, (v - hi.astype(F32)).astype(BF)


VM = pl.BlockSpec(memory_space=pltpu.VMEM)
IN_HBM = pl.BlockSpec(memory_space=pltpu.HBM)
MARK = jax.ShapeDtypeStruct((8, LANES), F32)


def dispatch_kernel(x, route, kind, chance, gain_in, gain_out, out, slot, gains, scr, rows):
    gains[0:1, :] = gain_in[...].reshape(1, D)
    gains[1:2, :] = gain_out[...].reshape(1, D)
    eye = iota((TOK, TOK), 0) == iota((TOK, TOK), 1)

    def column(row):
        return jnp.sum(jnp.where(eye, row, 0.0), axis=1, keepdims=True)

    onehot = (iota((E, TOK), 0) == route[...]).astype(F32)
    upper = (iota((TOK, TOK), 0) <= iota((TOK, TOK), 1)).astype(BF)
    run = dot(onehot.astype(BF), upper)
    pos = jnp.sum(onehot * run, axis=0, keepdims=True) - 1.0
    target = pos * E + route[...].astype(F32)
    placing = (iota((ROWS, TOK), 0) == target.astype(jnp.int32)).astype(F32).astype(BF)
    rows[...] = dot(placing, x[...])

    slot[...] = column(target)
    lane = iota((TOK, LANES), 1)
    field = lane // 16
    hi, mid, low = three(column(chance[...]))
    same = (column(kind[...].astype(F32)).astype(jnp.int32) == field - 3).astype(F32)
    held = jnp.where(
        field == 0, hi, jnp.where(field == 1, mid, jnp.where(field == 2, low, same))
    )
    held = jnp.where(lane % 16 == column(pos).astype(jnp.int32), held, 0.0).astype(BF)
    scr[pl.ds(META, E, stride=SLAB), :] = dot(onehot.astype(BF), held)
    scr[pl.ds(META + 1, E, stride=SLAB), :] = jnp.zeros((E, LANES), F32)
    pack_rows(scr, rows)
    out[...] = scr[...].astype(BF)


def dispatch(x, route, kind, chance, gain_in, gain_out):
    return pl.pallas_call(
        dispatch_kernel,
        out_shape=(
            jax.ShapeDtypeStruct((PACKED, LANES), BF),
            jax.ShapeDtypeStruct((TOK, 1), F32),
            jax.ShapeDtypeStruct((2, D), F32),
        ),
        scratch_shapes=[pltpu.VMEM((PACKED, LANES), F32), pltpu.VMEM((ROWS, D), F32)],
        compiler_params=params(60),
        cost_estimate=cost(2 * ROWS * TOK * D, 700000),
    )(
        x,
        route.reshape(1, TOK),
        kind.reshape(1, TOK),
        chance.reshape(1, TOK),
        gain_in,
        gain_out,
    )


def forward_kernel(
    arr, gains, w1, w2, part, bundle, slope, hot, scaled_in,
    scr, x, normed, acc,
):
    scr[...] = arr[...].astype(F32)
    unpack_rows(scr, x)
    scaled, inverse = norm(x[...])
    normed[...] = (scaled * gains[0:1, :]).astype(BF)
    scaled_in[...] = scaled.astype(BF)
    for f, v in enumerate(three(inverse)):
        hot[:, GROUP + 3 + f : GROUP + 4 + f] = v.astype(BF)
    for i in range(H // HB):
        at = slice(i * HB, (i + 1) * HB)
        hidden, grad = gelu_parts(dot(normed[...], w1[:, at]))
        slope[:, at] = grad.astype(BF)
        term = dot(hidden.astype(BF), w2[at, :])
        acc[...] = term if i == 0 else acc[...] + term
    meta = scr[pl.ds(META, E, stride=SLAB), :]
    fill_hot(hot, meta)
    lane = iota((E, LANES), 1)
    routing = jnp.where(lane >= 48, meta, 0.0)
    for j in range(CAP):
        at = slice(j * E, (j + 1) * E)
        chance = meta_chance(meta, j)
        mixed = x[at, :] + chance * acc[at, :].astype(BF).astype(F32)
        scaled, inverse = norm(mixed)
        bundle[at, :] = scaled.astype(BF)
        for f, v in enumerate(three(inverse) + three(chance)):
            lane_at = GROUP + f + (3 if f > 2 else 0)
            hot[at, lane_at : lane_at + 1] = v.astype(BF)
        acc[at, :] = scaled * gains[1:2, :]
        for f, v in enumerate(three(chance * inverse)):
            routing = jnp.where(lane == 16 * f + j, v, routing)
    bundle[ROWS:, :] = jnp.zeros((E, D), BF)
    bundle[ROWS:, :LANES] = routing.astype(BF)
    hi, low = two(acc[...])
    part[...] = (dot(hot[:, :GROUP], hi, 0, 0) + dot(hot[:, :GROUP], low, 0, 0)).astype(BF)


def whole(shape):
    return pl.BlockSpec(shape, lambda *_: (0,) * len(shape))


def forward(arr, gains, w1, w2):
    return pl.pallas_call(
        forward_kernel,
        in_specs=[VM] * 4,
        out_specs=(VM,) * 5,
        out_shape=(
            jax.ShapeDtypeStruct((GROUP, D), BF),
            jax.ShapeDtypeStruct((ROWS + E, D), BF),
            jax.ShapeDtypeStruct((ROWS, H), BF),
            jax.ShapeDtypeStruct((ROWS, 2 * GROUP), BF),
            jax.ShapeDtypeStruct((ROWS, D), BF),
        ),
        scratch_shapes=[
            pltpu.VMEM((PACKED, LANES), F32),
            pltpu.VMEM((ROWS, D), F32),
            pltpu.VMEM((ROWS, D), BF),
            pltpu.VMEM((ROWS, D), F32),
        ],
        compiler_params=params(24),
        cost_estimate=cost(4 * ROWS * D * H, 4 * D * H, 2 * ROWS * H),
    )(arr, gains, w1, w2)


HALF = PAIRS // DP


def load_units(near, far, unit, inverse, img, txt, keep):
    for i in range(DP):
        src = near if i < DP // 2 else far
        first = (i % (DP // 2)) * GROUP
        pooled = src[first : first + GROUP, :].astype(F32)
        inv = lax.rsqrt(jnp.sum(pooled * pooled, axis=1, keepdims=True) + EPS)
        u = pooled * inv
        if i < keep:
            unit[i * GROUP : (i + 1) * GROUP, :] = u
            inverse[i * GROUP : (i + 1) * GROUP, :] = inv
        u = u.reshape(NZ, 2 * NZ, D)
        img[i * HALF : (i + 1) * HALF, :] = u[:, :NZ].reshape(HALF, D).astype(BF)
        txt[i * HALF : (i + 1) * HALF, :] = u[:, NZ:].reshape(HALF, D).astype(BF)


def slopes(scalars, products):
    sharpness, shift, factor = scalars[0], scalars[1], scalars[2]
    logits = sharpness * products + shift
    diagonal = iota(products.shape, 0) == iota(products.shape, 1)
    sign = jnp.where(diagonal, 1.0, -1.0)
    return (-(factor / PAIRS) * sharpness) * sign * jax.nn.sigmoid(-sign * logits)


def pool_grads(g_img, g_txt, u, inv, gain):
    a, b = g_img.reshape(NZ, NZ, D), g_txt.reshape(NZ, NZ, D)
    grad = jnp.concatenate([a, b], axis=1).reshape(GROUP, D)
    share = jnp.where(iota((NZ, 2 * NZ, 1), 1) < NZ, 1.0 / IMG, 1.0 / TXT).reshape(GROUP, 1)
    return (inv * share) * (grad - u * jnp.sum(u * grad, axis=1, keepdims=True)) * gain


def own_loss_kernel(scalars, near, far, gains, own, unit, inverse, img, txt):
    load_units(near, far, unit, inverse, img, txt, 1)

    def side(mine, others):
        hi, low = two(slopes(scalars, dot(mine[:HALF, :], others[...], 1, 1)))
        both = dot(jnp.concatenate([hi, low], axis=0), others[...])
        return both[:HALF] + both[HALF:]

    own[...] = pool_grads(side(img, txt), side(txt, img), unit[...], inverse[...], gains[1:2, :])


def all_loss(scalars, near, far, gains, every, unit, inverse, img, txt):
    load_units(near, far, unit, inverse, img, txt, DP)
    hi, low = two(slopes(scalars, dot(img[...], txt[...], 1, 1)))
    g_img = dot(hi, txt[...]) + dot(low, txt[...])
    g_txt = dot(hi, img[...], 0, 0) + dot(low, img[...], 0, 0)
    for i in range(DP):
        at, half = slice(i * GROUP, (i + 1) * GROUP), slice(i * HALF, (i + 1) * HALF)
        every[i] = pool_grads(
            g_img[half], g_txt[half], unit[at, :], inverse[at, :], gains[1:2, :]
        ).astype(BF)


def merge_kernel(a, b, c, d, out):
    for i, piece in enumerate((a, b, c, d)):
        out[i * GROUP : (i + 1) * GROUP, :] = piece[...]


def merge(pieces):
    return pl.pallas_call(
        merge_kernel,
        out_shape=jax.ShapeDtypeStruct((DP // 2 * GROUP, D), BF),
        compiler_params=params(8),
    )(*pieces)


def own_loss(scalars, near, far, gains):
    return pl.pallas_call(
        own_loss_kernel,
        in_specs=[pl.BlockSpec(memory_space=pltpu.SMEM)] + [VM] * 3,
        out_specs=VM,
        out_shape=jax.ShapeDtypeStruct((GROUP, D), F32),
        scratch_shapes=[
            pltpu.VMEM((GROUP, D), F32),
            pltpu.VMEM((GROUP, 1), F32),
            pltpu.VMEM((PAIRS, D), BF),
            pltpu.VMEM((PAIRS, D), BF),
        ],
        compiler_params=params(24),
        cost_estimate=cost(6 * GROUP * PAIRS * D, 3000000, GROUP * PAIRS),
    )(scalars, near, far, gains)


def backward_kernel(
    bundle, hot, scaled_in, grads, gains, slope, w1, w2, out, mark,
    scr, mixed, rows, acc,
):
    hi, low = two(grads[...])
    mixed[...] = dot(hot[:, :GROUP], hi) + dot(hot[:, :GROUP], low)

    def column(at, n):
        return jnp.sum(hot[at, GROUP + 3 * n : GROUP + 3 * n + 3].astype(F32), axis=1, keepdims=True)

    for j in range(CAP):
        at = slice(j * E, (j + 1) * E)
        grad = norm_back(mixed[at, :], bundle[at, :].astype(F32), column(at, 0))
        mixed[at, :] = grad
        rows[at, :] = (column(at, 2) * grad).astype(BF)
    for i in range(H // HB):
        at = slice(i * HB, (i + 1) * HB)
        hidden = (dot(rows[...], w2[at, :], 1, 1) * slope[:, at].astype(F32)).astype(BF)
        term = dot(hidden, w1[:, at], 1, 1)
        acc[...] = term if i == 0 else acc[...] + term
    for j in range(CAP):
        at = slice(j * E, (j + 1) * E)
        back = acc[at, :].astype(BF).astype(F32) * gains[0:1, :]
        mixed[at, :] += norm_back(back, scaled_in[at, :].astype(F32), column(at, 1))
    for row in (META, META + 1):
        scr[pl.ds(row, E, stride=SLAB), :] = jnp.zeros((E, LANES), F32)
    pack_rows(scr, mixed)
    out[...] = scr[...].astype(BF)
    mark[...] = jnp.zeros_like(mark)


def backward(bundle, hot, scaled_in, grads, gains, slope, w1, w2):
    return pl.pallas_call(
        backward_kernel,
        in_specs=[VM] * 8,
        out_specs=(VM, VM),
        out_shape=(jax.ShapeDtypeStruct((PACKED, LANES), BF), MARK),
        scratch_shapes=[
            pltpu.VMEM((PACKED, LANES), F32),
            pltpu.VMEM((ROWS, D), F32),
            pltpu.VMEM((ROWS, D), BF),
            pltpu.VMEM((ROWS, D), F32),
        ],
        compiler_params=params(24),
        cost_estimate=cost(4 * ROWS * D * H, 4 * D * H + 2 * ROWS * H),
    )(bundle, hot, scaled_in, grads, gains, slope, w1, w2)


def slice_kernel(
    dp, arr, gains, w1, pooled, normed_t, hidden_t, slope, passed, scr, x, normed, hidden, w1s, sem
):
    step = pl.program_id(0)
    at = pl.ds(pl.multiple_of(dp[0] * HS, HS), HS)
    copy = pltpu.make_async_copy(w1.at[:, at], w1s, sem)

    @pl.when(step == 0)
    def _():
        copy.start()
        passed[...] = pooled[...]

    scr[...] = arr[0].astype(F32)
    unpack_rows(scr, x)
    scaled, _inverse = norm(x[...])
    rows = (scaled * gains[0:1, :]).astype(BF)
    at = pl.ds(pl.multiple_of(step * ROWS, ROWS), ROWS)
    normed[at, :] = rows

    @pl.when(step == 0)
    def _():
        copy.wait()

    value, grad = gelu_parts(dot(rows, w1s[...]))
    hidden[at, :] = value.astype(BF)
    slope[...] = grad.astype(BF)

    @pl.when(step == pl.num_programs(0) - 1)
    def _():
        normed_t[...] = normed[...].T
        hidden_t[...] = hidden[...].T


ALL = DP * ROWS


def hidden_slice(dp, arrs, gains, w1, pooled):
    return pl.pallas_call(
        slice_kernel,
        grid_spec=pltpu.PrefetchScalarGridSpec(
            num_scalar_prefetch=1,
            grid=(DP,),
            in_specs=[
                pl.BlockSpec((1, PACKED, LANES), lambda h, dp: (h, 0, 0)),
                whole((2, D)),
                IN_HBM,
                whole((GROUP, D)),
            ],
            out_specs=(
                whole((D, ALL)),
                whole((HS, ALL)),
                pl.BlockSpec((ROWS, HS), lambda h, dp: (h, 0)),
                whole((GROUP, D)),
            ),
            scratch_shapes=[
                pltpu.VMEM((PACKED, LANES), F32),
                pltpu.VMEM((ROWS, D), F32),
                pltpu.VMEM((ALL, D), BF),
                pltpu.VMEM((ALL, HS), BF),
                pltpu.VMEM((D, HS), BF),
                pltpu.SemaphoreType.DMA,
            ],
        ),
        out_shape=(
            jax.ShapeDtypeStruct((D, ALL), BF),
            jax.ShapeDtypeStruct((HS, ALL), BF),
            jax.ShapeDtypeStruct((ALL, HS), BF),
            jax.ShapeDtypeStruct((GROUP, D), BF),
        ),
        compiler_params=params(46),
        cost_estimate=cost(2 * ALL * D * HS, 12000000, 2 * ALL * HS),
    )(dp, arrs, gains, w1, pooled)


def weights_kernel(
    dp, scalars, near, far, gains, bundle, slope, _, normed_t, hidden_t, w2, g_in, g_out, mark,
    hot, rows, hidden, normed, value, w2s, every, unit, inverse, img, txt, sem,
):
    step = pl.program_id(0)
    at = pl.ds(pl.multiple_of(dp[0] * HS, HS), HS)
    weights = pltpu.make_async_copy(w2.at[at, :], w2s, sem.at[0])
    late = [
        pltpu.make_async_copy(normed_t, normed, sem.at[1]),
        pltpu.make_async_copy(hidden_t, value, sem.at[2]),
    ]

    @pl.when(step == 0)
    def _():
        weights.start()
        for copy in late:
            copy.start()
        all_loss(scalars, near, far, gains, every, unit, inverse, img, txt)
        weights.wait()

    for b in range(2):
        meta = bundle[b, ROWS:, :LANES].astype(F32)
        fill_hot(hot, meta)
        place = (step ^ lax.div(dp[0], 2)) + 4 * (b ^ lax.rem(dp[0], 2))
        q = dot(hot[...], every[place])
        for j in range(CAP):
            at = slice(j * E, (j + 1) * E)
            grad = norm_back(q[at, :], bundle[b, at, :].astype(F32), meta_chance(meta, j))
            first = pl.multiple_of((2 * step + b) * ROWS + j * E, E)
            rows[pl.ds(first, E), :] = grad.astype(BF)
    at = pl.ds(pl.multiple_of(step * (2 * ROWS), 2 * ROWS), 2 * ROWS)
    hidden[at, :] = (dot(rows[at, :], w2s[...], 1, 1) * slope[...].astype(F32)).astype(BF)

    @pl.when(step == pl.num_programs(0) - 1)
    def _():
        for copy in late:
            copy.wait()
        g_in[...] = dot(normed[...], hidden[...]).astype(BF)
        g_out[...] = dot(value[...], rows[...]).astype(BF)
        mark[...] = jnp.zeros_like(mark)


def weight_grads(dp, scalars, near, far, gains, bundles, slope, after, normed_t, hidden_t, w2):
    return pl.pallas_call(
        weights_kernel,
        grid_spec=pltpu.PrefetchScalarGridSpec(
            num_scalar_prefetch=2,
            grid=(DP // 2,),
            in_specs=[
                whole((DP // 2 * GROUP, D)),
                whole((DP // 2 * GROUP, D)),
                whole((2, D)),
                pl.BlockSpec((2, ROWS + E, D), lambda h, *_: (h, 0, 0)),
                pl.BlockSpec((2 * ROWS, HS), lambda h, *_: (h, 0)),
                whole(MARK.shape),
                IN_HBM,
                IN_HBM,
                IN_HBM,
            ],
            out_specs=(whole((D, HS)), whole((HS, D)), whole(MARK.shape)),
            scratch_shapes=[
                pltpu.VMEM((ROWS, GROUP), BF),
                pltpu.VMEM((ALL, D), BF),
                pltpu.VMEM((ALL, HS), BF),
                pltpu.VMEM((D, ALL), BF),
                pltpu.VMEM((HS, ALL), BF),
                pltpu.VMEM((HS, D), BF),
                pltpu.VMEM((DP, GROUP, D), BF),
                pltpu.VMEM((DP * GROUP, D), F32),
                pltpu.VMEM((DP * GROUP, 1), F32),
                pltpu.VMEM((PAIRS, D), BF),
                pltpu.VMEM((PAIRS, D), BF),
                pltpu.SemaphoreType.DMA((3,)),
            ],
        ),
        out_shape=(
            jax.ShapeDtypeStruct((D, HS), BF),
            jax.ShapeDtypeStruct((HS, D), BF),
            MARK,
        ),
        compiler_params=params(57),
        cost_estimate=cost(6 * ALL * D * HS + 10 * PAIRS * PAIRS * D, 15000000),
    )(dp, scalars, near, far, gains, bundles, slope, after, normed_t, hidden_t, w2)


def collect_kernel(arr, slot, _, out, scr, rows):
    scr[...] = arr[...].astype(F32)
    unpack_rows(scr, rows)
    taking = (iota((TOK, ROWS), 1) == slot[...].astype(jnp.int32)).astype(F32).astype(BF)
    out[...] = dot(taking, rows[...].astype(BF)).astype(BF)


def collect(arr, slot, after):
    return pl.pallas_call(
        collect_kernel,
        out_shape=jax.ShapeDtypeStruct((TOK, D), BF),
        scratch_shapes=[pltpu.VMEM((PACKED, LANES), F32), pltpu.VMEM((ROWS, D), F32)],
        compiler_params=params(16),
        cost_estimate=cost(2 * ROWS * TOK * D, 700000),
    )(arr, slot, after)


Z_GROUPS = [[x * NZ + z for z in range(NZ)] for x in range(NX)]


def to_experts(packed):
    slabs = packed.reshape(E, SLAB, LANES)
    slabs = lax.all_to_all(slabs, "expert", split_axis=0, concat_axis=0, tiled=True)
    return slabs.reshape(PACKED, LANES)


def along_z(values):
    return lax.all_to_all(
        values, "expert", split_axis=0, concat_axis=0, tiled=True, axis_index_groups=Z_GROUPS
    )


def swap(values, axis, size, by):
    return lax.ppermute(values, axis, [(i, i ^ by) for i in range(size)])


def on_device(
    incoming_elements,
    assigned_specialist,
    element_couple_kind,
    chosen_specialist_chance,
    specialist_layernorm_multiplier,
    final_layernorm_multiplier_vec,
    specialist_first_matrix,
    specialist_second_matrix,
    sharpness_factor,
    similarity_shift_term,
    objective_adjoint_factor,
):
    w1 = specialist_first_matrix[0]
    w2 = specialist_second_matrix[0]
    dp = lax.axis_index("dp").astype(jnp.int32).reshape(1)

    packed, slot, gains = dispatch(
        incoming_elements,
        assigned_specialist,
        element_couple_kind,
        chosen_specialist_chance,
        specialist_layernorm_multiplier,
        final_layernorm_multiplier_vec,
    )
    arr = to_experts(packed)
    arrs = lax.all_gather(arr, "dp", axis=0)
    part, bundle, slope, hot, scaled_in = forward(arr, gains, w1, w2)
    bundles = lax.all_gather(bundle, "dp", axis=0)

    part = along_z(part.reshape(NZ, 2 * NZ, D))
    part = jnp.sum(part.astype(F32), axis=0)
    others = [swap(part, "expert", E, NZ * m) for m in range(1, NX)]
    share = jnp.where(jnp.arange(2 * NZ) < NZ, 1.0 / IMG, 1.0 / TXT).astype(F32)
    pooled = (((part + others[0]) + (others[1] + others[2])) * share[:, None]).astype(BF)
    pooled = along_z(jnp.broadcast_to(pooled[None], (NZ, 2 * NZ, D))).reshape(GROUP, D)
    normed_t, hidden_t, grads, passed = hidden_slice(dp, arrs, gains, w1, pooled)
    near = merge([passed] + [swap(pooled, "dp", DP, m) for m in (2, 4, 6)])
    far = swap(near, "dp", DP, 1)

    scalars = jnp.concatenate([sharpness_factor, similarity_shift_term, objective_adjoint_factor])
    own = own_loss(scalars, near, far, gains)
    packed, mark = backward(bundle, hot, scaled_in, own, gains, slope, w1, w2)
    returned = to_experts(packed)
    grad_in, grad_out, mark = weight_grads(
        dp, scalars, near, far, gains, bundles, grads, mark, normed_t, hidden_t, w2
    )
    token_grads = collect(returned, slot, mark)
    return (token_grads, grad_in[None], grad_out[None])


def solution(mesh):
    return jax.shard_map(
        on_device,
        mesh=mesh,
        in_specs=(
            P(("expert", "dp"), None),
            P(("expert", "dp"), None),
            P(("expert", "dp")),
            P(("expert", "dp")),
            P(),
            P(),
            P("expert", None, None),
            P("expert", None, None),
            P(),
            P(),
            P(),
        ),
        out_specs=(P(("expert", "dp"), None), P("expert", None, "dp"), P("expert", "dp", None)),
        check_vma=False,
    )
```

```python
import jax
import jax.numpy as jnp
from jax import lax
from jax.experimental import pallas as pl
from jax.experimental.pallas import tpu as pltpu
from jax.sharding import PartitionSpec as P

D = 768
H = 3072
IMG = 50
TXT = 16
E = 32
DP = 8
NX = 4
NZ = 8
TOK = 132
CAP = 9
PAIRS = 512
ROWS = E * CAP
LANES = 128
CHUNKS = D // LANES
SLAB = 56
META = CAP * CHUNKS
PACKED = E * SLAB
HB = 1024
HS = H // DP
GROUP = 4 * E

EPS = 1e-06
ROOT_HALF = 0.7071067811865476
INV_ROOT_TAU = 0.3989422804014327
BF = jnp.bfloat16
F32 = jnp.float32


def params(mib):
    return pltpu.CompilerParams(vmem_limit_bytes=mib * 1024 * 1024)


def cost(flops, moved, trans=0):
    return pl.CostEstimate(flops=int(flops), bytes_accessed=int(moved), transcendentals=int(trans))


def dot(a, b, ca=1, cb=0):
    return lax.dot_general(a, b, (((ca,), (cb,)), ((), ())), preferred_element_type=F32)


def norm(values):
    center = values - jnp.mean(values, axis=1, keepdims=True)
    inverse = lax.rsqrt(jnp.mean(center * center, axis=1, keepdims=True) + EPS)
    return center * inverse, inverse


def norm_back(grad_hat, scaled, inverse):
    return inverse * (
        grad_hat
        - jnp.mean(grad_hat, axis=1, keepdims=True)
        - scaled * jnp.mean(grad_hat * scaled, axis=1, keepdims=True)
    )


def gelu_parts(v):
    e = jnp.exp(-0.5 * v * v)
    t = pl.reciprocal(1.0 + (0.3275911 * ROOT_HALF) * jnp.abs(v))
    tail = t * (0.5 * 1.061405429) + (0.5 * -1.453152027)
    tail = t * tail + (0.5 * 1.421413741)
    tail = t * tail + (0.5 * -0.284496736)
    tail = t * tail + (0.5 * 0.254829592)
    tail = t * tail * e
    cdf = jnp.where(v < 0.0, tail, 1.0 - tail)
    return v * cdf, cdf + v * e * INV_ROOT_TAU


def three(v):
    hi = v.astype(BF).astype(F32)
    mid = (v - hi).astype(BF).astype(F32)
    return hi, mid, v - hi - mid


def iota(shape, dim):
    return lax.broadcasted_iota(jnp.int32, shape, dim)


def pack_rows(scr, rows):
    for j in range(CAP):
        for c in range(CHUNKS):
            scr[pl.ds(c * CAP + j, E, stride=SLAB), :] = rows[
                j * E : (j + 1) * E, c * LANES : (c + 1) * LANES
            ]


def unpack_rows(scr, rows):
    for j in range(CAP):
        for c in range(CHUNKS):
            rows[j * E : (j + 1) * E, c * LANES : (c + 1) * LANES] = scr[
                pl.ds(c * CAP + j, E, stride=SLAB), :
            ]


def meta_chance(meta, j):
    return meta[:, j : j + 1] + meta[:, 16 + j : 17 + j] + meta[:, 32 + j : 33 + j]


def fill_hot(hot, meta):
    s, lane = iota((E, GROUP), 0), iota((E, GROUP), 1)
    first = (s % NZ) * (4 * NX) + s // NZ
    marks = [(lane == first + NX * k).astype(F32) for k in range(4)]
    for j in range(CAP):
        rows = jnp.zeros((E, GROUP), F32)
        for k in range(4):
            at = 48 + 16 * k + j
            rows += marks[k] * meta[:, at : at + 1]
        hot[j * E : (j + 1) * E, :GROUP] = rows.astype(BF)


def two(v):
    hi = v.astype(BF)
    return hi, (v - hi.astype(F32)).astype(BF)


VM = pl.BlockSpec(memory_space=pltpu.VMEM)
IN_HBM = pl.BlockSpec(memory_space=pltpu.HBM)
MARK = jax.ShapeDtypeStruct((8, LANES), F32)


def dispatch_kernel(x, route, kind, chance, gain_in, gain_out, out, slot, gains, scr, rows):
    gains[0:1, :] = gain_in[...].reshape(1, D)
    gains[1:2, :] = gain_out[...].reshape(1, D)
    eye = iota((TOK, TOK), 0) == iota((TOK, TOK), 1)

    def column(row):
        return jnp.sum(jnp.where(eye, row, 0.0), axis=1, keepdims=True)

    onehot = (iota((E, TOK), 0) == route[...]).astype(F32)
    upper = (iota((TOK, TOK), 0) <= iota((TOK, TOK), 1)).astype(BF)
    run = dot(onehot.astype(BF), upper)
    pos = jnp.sum(onehot * run, axis=0, keepdims=True) - 1.0
    target = pos * E + route[...].astype(F32)
    placing = (iota((ROWS, TOK), 0) == target.astype(jnp.int32)).astype(F32).astype(BF)
    rows[...] = dot(placing, x[...])

    slot[...] = column(target)
    lane = iota((TOK, LANES), 1)
    field = lane // 16
    hi, mid, low = three(column(chance[...]))
    same = (column(kind[...].astype(F32)).astype(jnp.int32) == field - 3).astype(F32)
    held = jnp.where(
        field == 0, hi, jnp.where(field == 1, mid, jnp.where(field == 2, low, same))
    )
    held = jnp.where(lane % 16 == column(pos).astype(jnp.int32), held, 0.0).astype(BF)
    scr[pl.ds(META, E, stride=SLAB), :] = dot(onehot.astype(BF), held)
    scr[pl.ds(META + 1, E, stride=SLAB), :] = jnp.zeros((E, LANES), F32)
    pack_rows(scr, rows)
    out[...] = scr[...].astype(BF)


def dispatch(x, route, kind, chance, gain_in, gain_out):
    return pl.pallas_call(
        dispatch_kernel,
        out_shape=(
            jax.ShapeDtypeStruct((PACKED, LANES), BF),
            jax.ShapeDtypeStruct((TOK, 1), F32),
            jax.ShapeDtypeStruct((2, D), F32),
        ),
        scratch_shapes=[pltpu.VMEM((PACKED, LANES), F32), pltpu.VMEM((ROWS, D), F32)],
        compiler_params=params(60),
        cost_estimate=cost(2 * ROWS * TOK * D, 700000),
    )(
        x,
        route.reshape(1, TOK),
        kind.reshape(1, TOK),
        chance.reshape(1, TOK),
        gain_in,
        gain_out,
    )


def forward_kernel(
    arr, gains, w1, w2, part, bundle, slope, hot, scaled_in,
    scr, x, normed, acc, w1v, w2v, sem,
):
    cols = [slice(i * HB, (i + 1) * HB) for i in range(H // HB)]
    fetches = [
        (
            pltpu.make_async_copy(w1.at[:, at], w1v.at[:, at], sem.at[0, i]),
            pltpu.make_async_copy(w2.at[at, :], w2v.at[at, :], sem.at[1, i]),
        )
        for i, at in enumerate(cols)
    ]
    for first, second in fetches:
        first.start()
        second.start()
    scr[...] = arr[...].astype(F32)
    unpack_rows(scr, x)
    scaled, inverse = norm(x[...])
    normed[...] = (scaled * gains[0:1, :]).astype(BF)
    scaled_in[...] = scaled.astype(BF)
    for f, v in enumerate(three(inverse)):
        hot[:, GROUP + 3 + f : GROUP + 4 + f] = v.astype(BF)
    for i, at in enumerate(cols):
        fetches[i][0].wait()
        hidden, grad = gelu_parts(dot(normed[...], w1v[:, at]))
        slope[:, at] = grad.astype(BF)
        fetches[i][1].wait()
        term = dot(hidden.astype(BF), w2v[at, :])
        acc[...] = term if i == 0 else acc[...] + term
    meta = scr[pl.ds(META, E, stride=SLAB), :]
    fill_hot(hot, meta)
    lane = iota((E, LANES), 1)
    routing = jnp.where(lane >= 48, meta, 0.0)
    for j in range(CAP):
        at = slice(j * E, (j + 1) * E)
        chance = meta_chance(meta, j)
        mixed = x[at, :] + chance * acc[at, :].astype(BF).astype(F32)
        scaled, inverse = norm(mixed)
        bundle[at, :] = scaled.astype(BF)
        for f, v in enumerate(three(inverse) + three(chance)):
            lane_at = GROUP + f + (3 if f > 2 else 0)
            hot[at, lane_at : lane_at + 1] = v.astype(BF)
        acc[at, :] = scaled * gains[1:2, :]
        for f, v in enumerate(three(chance * inverse)):
            routing = jnp.where(lane == 16 * f + j, v, routing)
    bundle[ROWS:, :] = jnp.zeros((E, D), BF)
    bundle[ROWS:, :LANES] = routing.astype(BF)
    hi, low = two(acc[...])
    part[...] = (dot(hot[:, :GROUP], hi, 0, 0) + dot(hot[:, :GROUP], low, 0, 0)).astype(BF)


def whole(shape):
    return pl.BlockSpec(shape, lambda *_: (0,) * len(shape))


def forward(arr, gains, w1, w2):
    return pl.pallas_call(
        forward_kernel,
        in_specs=[VM, VM, IN_HBM, IN_HBM],
        out_specs=(VM,) * 5,
        out_shape=(
            jax.ShapeDtypeStruct((GROUP, D), BF),
            jax.ShapeDtypeStruct((ROWS + E, D), BF),
            jax.ShapeDtypeStruct((ROWS, H), BF),
            jax.ShapeDtypeStruct((ROWS, 2 * GROUP), BF),
            jax.ShapeDtypeStruct((ROWS, D), BF),
        ),
        scratch_shapes=[
            pltpu.VMEM((PACKED, LANES), F32),
            pltpu.VMEM((ROWS, D), F32),
            pltpu.VMEM((ROWS, D), BF),
            pltpu.VMEM((ROWS, D), F32),
            pltpu.VMEM((D, H), BF),
            pltpu.VMEM((H, D), BF),
            pltpu.SemaphoreType.DMA((2, H // HB)),
        ],
        compiler_params=params(48),
        cost_estimate=cost(4 * ROWS * D * H, 4 * D * H, 2 * ROWS * H),
    )(arr, gains, w1, w2)


HALF = PAIRS // DP


def load_units(near, far, unit, inverse, img, txt, keep):
    for i in range(DP):
        src = near if i < DP // 2 else far
        first = (i % (DP // 2)) * GROUP
        pooled = src[first : first + GROUP, :].astype(F32)
        inv = lax.rsqrt(jnp.sum(pooled * pooled, axis=1, keepdims=True) + EPS)
        u = pooled * inv
        if i < keep:
            unit[i * GROUP : (i + 1) * GROUP, :] = u
            inverse[i * GROUP : (i + 1) * GROUP, :] = inv
        u = u.reshape(NZ, 2 * NZ, D)
        img[i * HALF : (i + 1) * HALF, :] = u[:, :NZ].reshape(HALF, D).astype(BF)
        txt[i * HALF : (i + 1) * HALF, :] = u[:, NZ:].reshape(HALF, D).astype(BF)


def slopes(scalars, products):
    sharpness, shift, factor = scalars[0], scalars[1], scalars[2]
    logits = sharpness * products + shift
    diagonal = iota(products.shape, 0) == iota(products.shape, 1)
    sign = jnp.where(diagonal, 1.0, -1.0)
    return (-(factor / PAIRS) * sharpness) * sign * jax.nn.sigmoid(-sign * logits)


def pool_grads(g_img, g_txt, u, inv, gain):
    a, b = g_img.reshape(NZ, NZ, D), g_txt.reshape(NZ, NZ, D)
    grad = jnp.concatenate([a, b], axis=1).reshape(GROUP, D)
    share = jnp.where(iota((NZ, 2 * NZ, 1), 1) < NZ, 1.0 / IMG, 1.0 / TXT).reshape(GROUP, 1)
    return (inv * share) * (grad - u * jnp.sum(u * grad, axis=1, keepdims=True)) * gain


def own_loss_kernel(scalars, near, far, gains, own, unit, inverse, img, txt):
    load_units(near, far, unit, inverse, img, txt, 1)

    def side(mine, others):
        hi, low = two(slopes(scalars, dot(mine[:HALF, :], others[...], 1, 1)))
        both = dot(jnp.concatenate([hi, low], axis=0), others[...])
        return both[:HALF] + both[HALF:]

    own[...] = pool_grads(side(img, txt), side(txt, img), unit[...], inverse[...], gains[1:2, :])


def all_loss(scalars, near, far, gains, every, unit, inverse, img, txt):
    load_units(near, far, unit, inverse, img, txt, DP)
    hi, low = two(slopes(scalars, dot(img[...], txt[...], 1, 1)))
    g_img = dot(hi, txt[...]) + dot(low, txt[...])
    g_txt = dot(hi, img[...], 0, 0) + dot(low, img[...], 0, 0)
    for i in range(DP):
        at, half = slice(i * GROUP, (i + 1) * GROUP), slice(i * HALF, (i + 1) * HALF)
        every[i] = pool_grads(
            g_img[half], g_txt[half], unit[at, :], inverse[at, :], gains[1:2, :]
        ).astype(BF)


def merge_kernel(a, b, c, d, out):
    for i, piece in enumerate((a, b, c, d)):
        out[i * GROUP : (i + 1) * GROUP, :] = piece[...]


def merge(pieces):
    return pl.pallas_call(
        merge_kernel,
        out_shape=jax.ShapeDtypeStruct((DP // 2 * GROUP, D), BF),
        compiler_params=params(8),
    )(*pieces)


def own_loss(scalars, near, far, gains):
    return pl.pallas_call(
        own_loss_kernel,
        in_specs=[pl.BlockSpec(memory_space=pltpu.SMEM)] + [VM] * 3,
        out_specs=VM,
        out_shape=jax.ShapeDtypeStruct((GROUP, D), F32),
        scratch_shapes=[
            pltpu.VMEM((GROUP, D), F32),
            pltpu.VMEM((GROUP, 1), F32),
            pltpu.VMEM((PAIRS, D), BF),
            pltpu.VMEM((PAIRS, D), BF),
        ],
        compiler_params=params(24),
        cost_estimate=cost(6 * GROUP * PAIRS * D, 3000000, GROUP * PAIRS),
    )(scalars, near, far, gains)


def backward_kernel(
    bundle, hot, scaled_in, grads, gains, slope, w1, w2, out, mark,
    scr, mixed, rows, acc,
):
    hi, low = two(grads[...])
    mixed[...] = dot(hot[:, :GROUP], hi) + dot(hot[:, :GROUP], low)

    def column(at, n):
        return jnp.sum(hot[at, GROUP + 3 * n : GROUP + 3 * n + 3].astype(F32), axis=1, keepdims=True)

    for j in range(CAP):
        at = slice(j * E, (j + 1) * E)
        grad = norm_back(mixed[at, :], bundle[at, :].astype(F32), column(at, 0))
        mixed[at, :] = grad
        rows[at, :] = (column(at, 2) * grad).astype(BF)
    for i in range(H // HB):
        at = slice(i * HB, (i + 1) * HB)
        hidden = (dot(rows[...], w2[at, :], 1, 1) * slope[:, at].astype(F32)).astype(BF)
        term = dot(hidden, w1[:, at], 1, 1)
        acc[...] = term if i == 0 else acc[...] + term
    for j in range(CAP):
        at = slice(j * E, (j + 1) * E)
        back = acc[at, :].astype(BF).astype(F32) * gains[0:1, :]
        mixed[at, :] += norm_back(back, scaled_in[at, :].astype(F32), column(at, 1))
    for row in (META, META + 1):
        scr[pl.ds(row, E, stride=SLAB), :] = jnp.zeros((E, LANES), F32)
    pack_rows(scr, mixed)
    out[...] = scr[...].astype(BF)
    mark[...] = jnp.zeros_like(mark)


def backward(bundle, hot, scaled_in, grads, gains, slope, w1, w2):
    return pl.pallas_call(
        backward_kernel,
        in_specs=[VM] * 8,
        out_specs=(VM, VM),
        out_shape=(jax.ShapeDtypeStruct((PACKED, LANES), BF), MARK),
        scratch_shapes=[
            pltpu.VMEM((PACKED, LANES), F32),
            pltpu.VMEM((ROWS, D), F32),
            pltpu.VMEM((ROWS, D), BF),
            pltpu.VMEM((ROWS, D), F32),
        ],
        compiler_params=params(24),
        cost_estimate=cost(4 * ROWS * D * H, 4 * D * H + 2 * ROWS * H),
    )(bundle, hot, scaled_in, grads, gains, slope, w1, w2)


def slice_kernel(
    dp, arr, gains, w1, pooled, normed_t, hidden_t, slope, passed, scr, x, normed, hidden, w1s, sem
):
    step = pl.program_id(0)
    at = pl.ds(pl.multiple_of(dp[0] * HS, HS), HS)
    copy = pltpu.make_async_copy(w1.at[:, at], w1s, sem)

    @pl.when(step == 0)
    def _():
        copy.start()
        passed[...] = pooled[...]

    scr[...] = arr[0].astype(F32)
    unpack_rows(scr, x)
    scaled, _inverse = norm(x[...])
    rows = (scaled * gains[0:1, :]).astype(BF)
    at = pl.ds(pl.multiple_of(step * ROWS, ROWS), ROWS)
    normed[at, :] = rows

    @pl.when(step == 0)
    def _():
        copy.wait()

    value, grad = gelu_parts(dot(rows, w1s[...]))
    hidden[at, :] = value.astype(BF)
    slope[...] = grad.astype(BF)

    @pl.when(step == pl.num_programs(0) - 1)
    def _():
        normed_t[...] = normed[...].T
        hidden_t[...] = hidden[...].T


ALL = DP * ROWS


def hidden_slice(dp, arrs, gains, w1, pooled):
    return pl.pallas_call(
        slice_kernel,
        grid_spec=pltpu.PrefetchScalarGridSpec(
            num_scalar_prefetch=1,
            grid=(DP,),
            in_specs=[
                pl.BlockSpec((1, PACKED, LANES), lambda h, dp: (h, 0, 0)),
                whole((2, D)),
                IN_HBM,
                whole((GROUP, D)),
            ],
            out_specs=(
                whole((D, ALL)),
                whole((HS, ALL)),
                pl.BlockSpec((ROWS, HS), lambda h, dp: (h, 0)),
                whole((GROUP, D)),
            ),
            scratch_shapes=[
                pltpu.VMEM((PACKED, LANES), F32),
                pltpu.VMEM((ROWS, D), F32),
                pltpu.VMEM((ALL, D), BF),
                pltpu.VMEM((ALL, HS), BF),
                pltpu.VMEM((D, HS), BF),
                pltpu.SemaphoreType.DMA,
            ],
        ),
        out_shape=(
            jax.ShapeDtypeStruct((D, ALL), BF),
            jax.ShapeDtypeStruct((HS, ALL), BF),
            jax.ShapeDtypeStruct((ALL, HS), BF),
            jax.ShapeDtypeStruct((GROUP, D), BF),
        ),
        compiler_params=params(40),
        cost_estimate=cost(2 * ALL * D * HS, 12000000, 2 * ALL * HS),
    )(dp, arrs, gains, w1, pooled)


def weights_kernel(
    dp, scalars, near, far, gains, bundle, slope, _, normed_t, hidden_t, w2, g_in, g_out, mark,
    hot, rows, hidden, normed, value, w2s, every, unit, inverse, img, txt, sem,
):
    step = pl.program_id(0)
    at = pl.ds(pl.multiple_of(dp[0] * HS, HS), HS)
    weights = pltpu.make_async_copy(w2.at[at, :], w2s, sem.at[0])
    late = [
        pltpu.make_async_copy(normed_t, normed, sem.at[1]),
        pltpu.make_async_copy(hidden_t, value, sem.at[2]),
    ]

    @pl.when(step == 0)
    def _():
        weights.start()
        for copy in late:
            copy.start()
        all_loss(scalars, near, far, gains, every, unit, inverse, img, txt)
        weights.wait()

    for b in range(2):
        meta = bundle[b, ROWS:, :LANES].astype(F32)
        fill_hot(hot, meta)
        place = (step ^ lax.div(dp[0], 2)) + 4 * (b ^ lax.rem(dp[0], 2))
        q = dot(hot[...], every[place])
        for j in range(CAP):
            at = slice(j * E, (j + 1) * E)
            grad = norm_back(q[at, :], bundle[b, at, :].astype(F32), meta_chance(meta, j))
            first = pl.multiple_of((2 * step + b) * ROWS + j * E, E)
            rows[pl.ds(first, E), :] = grad.astype(BF)
    at = pl.ds(pl.multiple_of(step * (2 * ROWS), 2 * ROWS), 2 * ROWS)
    hidden[at, :] = (dot(rows[at, :], w2s[...], 1, 1) * slope[...].astype(F32)).astype(BF)

    @pl.when(step == pl.num_programs(0) - 1)
    def _():
        for copy in late:
            copy.wait()
        g_in[...] = dot(normed[...], hidden[...]).astype(BF)
        g_out[...] = dot(value[...], rows[...]).astype(BF)
        mark[...] = jnp.zeros_like(mark)


def weight_grads(dp, scalars, near, far, gains, bundles, slope, after, normed_t, hidden_t, w2):
    return pl.pallas_call(
        weights_kernel,
        grid_spec=pltpu.PrefetchScalarGridSpec(
            num_scalar_prefetch=2,
            grid=(DP // 2,),
            in_specs=[
                whole((DP // 2 * GROUP, D)),
                whole((DP // 2 * GROUP, D)),
                whole((2, D)),
                pl.BlockSpec((2, ROWS + E, D), lambda h, *_: (h, 0, 0)),
                pl.BlockSpec((2 * ROWS, HS), lambda h, *_: (h, 0)),
                whole(MARK.shape),
                IN_HBM,
                IN_HBM,
                IN_HBM,
            ],
            out_specs=(whole((D, HS)), whole((HS, D)), whole(MARK.shape)),
            scratch_shapes=[
                pltpu.VMEM((ROWS, GROUP), BF),
                pltpu.VMEM((ALL, D), BF),
                pltpu.VMEM((ALL, HS), BF),
                pltpu.VMEM((D, ALL), BF),
                pltpu.VMEM((HS, ALL), BF),
                pltpu.VMEM((HS, D), BF),
                pltpu.VMEM((DP, GROUP, D), BF),
                pltpu.VMEM((DP * GROUP, D), F32),
                pltpu.VMEM((DP * GROUP, 1), F32),
                pltpu.VMEM((PAIRS, D), BF),
                pltpu.VMEM((PAIRS, D), BF),
                pltpu.SemaphoreType.DMA((3,)),
            ],
        ),
        out_shape=(
            jax.ShapeDtypeStruct((D, HS), BF),
            jax.ShapeDtypeStruct((HS, D), BF),
            MARK,
        ),
        compiler_params=params(57),
        cost_estimate=cost(6 * ALL * D * HS + 10 * PAIRS * PAIRS * D, 15000000),
    )(dp, scalars, near, far, gains, bundles, slope, after, normed_t, hidden_t, w2)


def collect_kernel(arr, slot, _, out, scr, rows):
    scr[...] = arr[...].astype(F32)
    unpack_rows(scr, rows)
    taking = (iota((TOK, ROWS), 1) == slot[...].astype(jnp.int32)).astype(F32).astype(BF)
    out[...] = dot(taking, rows[...].astype(BF)).astype(BF)


def collect(arr, slot, after):
    return pl.pallas_call(
        collect_kernel,
        out_shape=jax.ShapeDtypeStruct((TOK, D), BF),
        scratch_shapes=[pltpu.VMEM((PACKED, LANES), F32), pltpu.VMEM((ROWS, D), F32)],
        compiler_params=params(16),
        cost_estimate=cost(2 * ROWS * TOK * D, 700000),
    )(arr, slot, after)


Z_GROUPS = [[x * NZ + z for z in range(NZ)] for x in range(NX)]


def to_experts(packed):
    slabs = packed.reshape(E, SLAB, LANES)
    slabs = lax.all_to_all(slabs, "expert", split_axis=0, concat_axis=0, tiled=True)
    return slabs.reshape(PACKED, LANES)


def along_z(values):
    return lax.all_to_all(
        values, "expert", split_axis=0, concat_axis=0, tiled=True, axis_index_groups=Z_GROUPS
    )


def swap(values, axis, size, by):
    return lax.ppermute(values, axis, [(i, i ^ by) for i in range(size)])


def on_device(
    incoming_elements,
    assigned_specialist,
    element_couple_kind,
    chosen_specialist_chance,
    specialist_layernorm_multiplier,
    final_layernorm_multiplier_vec,
    specialist_first_matrix,
    specialist_second_matrix,
    sharpness_factor,
    similarity_shift_term,
    objective_adjoint_factor,
):
    w1 = specialist_first_matrix[0]
    w2 = specialist_second_matrix[0]
    dp = lax.axis_index("dp").astype(jnp.int32).reshape(1)

    packed, slot, gains = dispatch(
        incoming_elements,
        assigned_specialist,
        element_couple_kind,
        chosen_specialist_chance,
        specialist_layernorm_multiplier,
        final_layernorm_multiplier_vec,
    )
    arr = to_experts(packed)
    arrs = lax.all_gather(arr, "dp", axis=0)
    part, bundle, slope, hot, scaled_in = forward(arr, gains, w1, w2)
    bundles = lax.all_gather(bundle, "dp", axis=0)

    part = along_z(part.reshape(NZ, 2 * NZ, D))
    part = jnp.sum(part.astype(F32), axis=0)
    others = [swap(part, "expert", E, NZ * m) for m in range(1, NX)]
    share = jnp.where(jnp.arange(2 * NZ) < NZ, 1.0 / IMG, 1.0 / TXT).astype(F32)
    pooled = (((part + others[0]) + (others[1] + others[2])) * share[:, None]).astype(BF)
    pooled = along_z(jnp.broadcast_to(pooled[None], (NZ, 2 * NZ, D))).reshape(GROUP, D)
    normed_t, hidden_t, grads, passed = hidden_slice(dp, arrs, gains, w1, pooled)
    near = merge([passed] + [swap(pooled, "dp", DP, m) for m in (2, 4, 6)])
    far = swap(near, "dp", DP, 1)

    scalars = jnp.concatenate([sharpness_factor, similarity_shift_term, objective_adjoint_factor])
    own = own_loss(scalars, near, far, gains)
    packed, mark = backward(bundle, hot, scaled_in, own, gains, slope, w1, w2)
    returned = to_experts(packed)
    grad_in, grad_out, mark = weight_grads(
        dp, scalars, near, far, gains, bundles, grads, mark, normed_t, hidden_t, w2
    )
    token_grads = collect(returned, slot, mark)
    return (token_grads, grad_in[None], grad_out[None])


def solution(mesh):
    return jax.shard_map(
        on_device,
        mesh=mesh,
        in_specs=(
            P(("expert", "dp"), None),
            P(("expert", "dp"), None),
            P(("expert", "dp")),
            P(("expert", "dp")),
            P(),
            P(),
            P("expert", None, None),
            P("expert", None, None),
            P(),
            P(),
            P(),
        ),
        out_specs=(P(("expert", "dp"), None), P("expert", None, "dp"), P("expert", "dp", None)),
        check_vma=False,
    )
```

```python
import jax
import jax.numpy as jnp
from jax import lax
from jax.experimental import pallas as pl
from jax.experimental.pallas import tpu as pltpu
from jax.sharding import PartitionSpec as P

D = 768
H = 3072
IMG = 50
TXT = 16
E = 32
DP = 8
NX = 4
NZ = 8
TOK = 132
CAP = 9
PAIRS = 512
ROWS = E * CAP
LANES = 128
CHUNKS = D // LANES
SLAB = 56
META = CAP * CHUNKS
TAIL = 16
PACKED = E * SLAB
HB = 1024
HS = H // DP
GROUP = 4 * E

EPS = 1e-06
ROOT_HALF = 0.7071067811865476
INV_ROOT_TAU = 0.3989422804014327
BF = jnp.bfloat16
F32 = jnp.float32


def params(mib):
    return pltpu.CompilerParams(vmem_limit_bytes=mib * 1024 * 1024)


def cost(flops, moved, trans=0):
    return pl.CostEstimate(flops=int(flops), bytes_accessed=int(moved), transcendentals=int(trans))


def dot(a, b, ca=1, cb=0):
    return lax.dot_general(a, b, (((ca,), (cb,)), ((), ())), preferred_element_type=F32)


def norm(values):
    center = values - jnp.mean(values, axis=1, keepdims=True)
    inverse = lax.rsqrt(jnp.mean(center * center, axis=1, keepdims=True) + EPS)
    return center * inverse, inverse


def norm_back(grad_hat, scaled, inverse):
    return inverse * (
        grad_hat
        - jnp.mean(grad_hat, axis=1, keepdims=True)
        - scaled * jnp.mean(grad_hat * scaled, axis=1, keepdims=True)
    )


def gelu_parts(v):
    e = jnp.exp(-0.5 * v * v)
    t = pl.reciprocal(1.0 + (0.3275911 * ROOT_HALF) * jnp.abs(v))
    tail = t * (0.5 * 1.061405429) + (0.5 * -1.453152027)
    tail = t * tail + (0.5 * 1.421413741)
    tail = t * tail + (0.5 * -0.284496736)
    tail = t * tail + (0.5 * 0.254829592)
    tail = t * tail * e
    cdf = jnp.where(v < 0.0, tail, 1.0 - tail)
    return v * cdf, cdf + v * e * INV_ROOT_TAU


def three(v):
    hi = v.astype(BF).astype(F32)
    mid = (v - hi).astype(BF).astype(F32)
    return hi, mid, v - hi - mid


def iota(shape, dim):
    return lax.broadcasted_iota(jnp.int32, shape, dim)


def pack_rows(scr, rows):
    for j in range(CAP):
        for c in range(CHUNKS):
            scr[pl.ds(c * CAP + j, E, stride=SLAB), :] = rows[
                j * E : (j + 1) * E, c * LANES : (c + 1) * LANES
            ]


def unpack_rows(scr, rows):
    for j in range(CAP):
        for c in range(CHUNKS):
            rows[j * E : (j + 1) * E, c * LANES : (c + 1) * LANES] = scr[
                pl.ds(c * CAP + j, E, stride=SLAB), :
            ]


def meta_chance(meta, j):
    return meta[:, j : j + 1] + meta[:, 16 + j : 17 + j] + meta[:, 32 + j : 33 + j]


def fill_hot(hot, meta):
    s, lane = iota((E, GROUP), 0), iota((E, GROUP), 1)
    first = (s % NZ) * (4 * NX) + s // NZ
    marks = [(lane == first + NX * k).astype(F32) for k in range(4)]
    for j in range(CAP):
        rows = jnp.zeros((E, GROUP), F32)
        for k in range(4):
            at = 48 + 16 * k + j
            rows += marks[k] * meta[:, at : at + 1]
        hot[j * E : (j + 1) * E, :GROUP] = rows.astype(BF)


def two(v):
    hi = v.astype(BF)
    return hi, (v - hi.astype(F32)).astype(BF)


VM = pl.BlockSpec(memory_space=pltpu.VMEM)
IN_HBM = pl.BlockSpec(memory_space=pltpu.HBM)
MARK = jax.ShapeDtypeStruct((8, LANES), F32)


def dispatch_kernel(x, route, kind, chance, gain_in, gain_out, out, slot, gains, scr, rows):
    gains[0:1, :] = gain_in[...].reshape(1, D)
    gains[1:2, :] = gain_out[...].reshape(1, D)
    eye = iota((TOK, TOK), 0) == iota((TOK, TOK), 1)

    def column(row):
        return jnp.sum(jnp.where(eye, row, 0.0), axis=1, keepdims=True)

    onehot = (iota((E, TOK), 0) == route[...]).astype(F32)
    upper = (iota((TOK, TOK), 0) <= iota((TOK, TOK), 1)).astype(BF)
    run = dot(onehot.astype(BF), upper)
    pos = jnp.sum(onehot * run, axis=0, keepdims=True) - 1.0
    target = pos * E + route[...].astype(F32)
    placing = (iota((ROWS, TOK), 0) == target.astype(jnp.int32)).astype(F32).astype(BF)
    rows[...] = dot(placing, x[...])

    slot[...] = column(target)
    lane = iota((TOK, LANES), 1)
    field = lane // 16
    hi, mid, low = three(column(chance[...]))
    same = (column(kind[...].astype(F32)).astype(jnp.int32) == field - 3).astype(F32)
    held = jnp.where(
        field == 0, hi, jnp.where(field == 1, mid, jnp.where(field == 2, low, same))
    )
    held = jnp.where(lane % 16 == column(pos).astype(jnp.int32), held, 0.0).astype(BF)
    scr[pl.ds(META, E, stride=SLAB), :] = dot(onehot.astype(BF), held)
    scr[pl.ds(META + 1, E, stride=SLAB), :] = jnp.zeros((E, LANES), F32)
    pack_rows(scr, rows)
    out[...] = scr[...].astype(BF)


def dispatch(x, route, kind, chance, gain_in, gain_out):
    return pl.pallas_call(
        dispatch_kernel,
        out_shape=(
            jax.ShapeDtypeStruct((PACKED, LANES), BF),
            jax.ShapeDtypeStruct((TOK, 1), F32),
            jax.ShapeDtypeStruct((2, D), F32),
        ),
        scratch_shapes=[pltpu.VMEM((PACKED, LANES), F32), pltpu.VMEM((ROWS, D), F32)],
        compiler_params=params(60),
        cost_estimate=cost(2 * ROWS * TOK * D, 700000),
    )(
        x,
        route.reshape(1, TOK),
        kind.reshape(1, TOK),
        chance.reshape(1, TOK),
        gain_in,
        gain_out,
    )


def forward_kernel(
    arr, gains, w1, w2, part, bundle, slope, hot, scaled_in,
    scr, x, normed, acc, w1v, w2v, sem,
):
    cols = [slice(i * HB, (i + 1) * HB) for i in range(H // HB)]
    fetches = [
        (
            pltpu.make_async_copy(w1.at[:, at], w1v.at[:, at], sem.at[0, i]),
            pltpu.make_async_copy(w2.at[at, :], w2v.at[at, :], sem.at[1, i]),
        )
        for i, at in enumerate(cols)
    ]
    for first, second in fetches:
        first.start()
        second.start()
    scr[...] = arr[...].astype(F32)
    unpack_rows(scr, x)
    scaled, inverse = norm(x[...])
    normed[...] = (scaled * gains[0:1, :]).astype(BF)
    scaled_in[...] = scaled.astype(BF)
    for f, v in enumerate(three(inverse)):
        hot[:, GROUP + 3 + f : GROUP + 4 + f] = v.astype(BF)
    for i, at in enumerate(cols):
        fetches[i][0].wait()
        hidden, grad = gelu_parts(dot(normed[...], w1v[:, at]))
        slope[:, at] = grad.astype(BF)
        fetches[i][1].wait()
        term = dot(hidden.astype(BF), w2v[at, :])
        acc[...] = term if i == 0 else acc[...] + term
    meta = scr[pl.ds(META, E, stride=SLAB), :]
    fill_hot(hot, meta)
    lane = iota((E, LANES), 1)
    routing = jnp.where(lane >= 48, meta, 0.0)
    for j in range(CAP):
        at = slice(j * E, (j + 1) * E)
        chance = meta_chance(meta, j)
        mixed = x[at, :] + chance * acc[at, :].astype(BF).astype(F32)
        scaled, inverse = norm(mixed)
        bundle[at, :] = scaled.astype(BF)
        for f, v in enumerate(three(inverse) + three(chance)):
            lane_at = GROUP + f + (3 if f > 2 else 0)
            hot[at, lane_at : lane_at + 1] = v.astype(BF)
        acc[at, :] = scaled * gains[1:2, :]
        for f, v in enumerate(three(chance * inverse)):
            routing = jnp.where(lane == 16 * f + j, v, routing)
    bundle[ROWS:, 2 * LANES :] = jnp.zeros((TAIL, D - 2 * LANES), BF)
    for c in range(E // TAIL):
        bundle[ROWS:, c * LANES : (c + 1) * LANES] = routing[c * TAIL : (c + 1) * TAIL].astype(BF)
    hi, low = two(acc[...])
    part[...] = (dot(hot[:, :GROUP], hi, 0, 0) + dot(hot[:, :GROUP], low, 0, 0)).astype(BF)


def whole(shape):
    return pl.BlockSpec(shape, lambda *_: (0,) * len(shape))


def forward(arr, gains, w1, w2):
    return pl.pallas_call(
        forward_kernel,
        in_specs=[VM, VM, IN_HBM, IN_HBM],
        out_specs=(VM,) * 5,
        out_shape=(
            jax.ShapeDtypeStruct((GROUP, D), BF),
            jax.ShapeDtypeStruct((ROWS + TAIL, D), BF),
            jax.ShapeDtypeStruct((ROWS, H), BF),
            jax.ShapeDtypeStruct((ROWS, 2 * GROUP), BF),
            jax.ShapeDtypeStruct((ROWS, D), BF),
        ),
        scratch_shapes=[
            pltpu.VMEM((PACKED, LANES), F32),
            pltpu.VMEM((ROWS, D), F32),
            pltpu.VMEM((ROWS, D), BF),
            pltpu.VMEM((ROWS, D), F32),
            pltpu.VMEM((D, H), BF),
            pltpu.VMEM((H, D), BF),
            pltpu.SemaphoreType.DMA((2, H // HB)),
        ],
        compiler_params=params(48),
        cost_estimate=cost(4 * ROWS * D * H, 4 * D * H, 2 * ROWS * H),
    )(arr, gains, w1, w2)


HALF = PAIRS // DP


def load_units(near, far, unit, inverse, img, txt, keep):
    for i in range(DP):
        src = near if i < DP // 2 else far
        first = (i % (DP // 2)) * GROUP
        pooled = src[first : first + GROUP, :].astype(F32)
        inv = lax.rsqrt(jnp.sum(pooled * pooled, axis=1, keepdims=True) + EPS)
        u = pooled * inv
        if i < keep:
            unit[i * GROUP : (i + 1) * GROUP, :] = u
            inverse[i * GROUP : (i + 1) * GROUP, :] = inv
        u = u.reshape(NZ, 2 * NZ, D)
        img[i * HALF : (i + 1) * HALF, :] = u[:, :NZ].reshape(HALF, D).astype(BF)
        txt[i * HALF : (i + 1) * HALF, :] = u[:, NZ:].reshape(HALF, D).astype(BF)


def slopes(scalars, products):
    sharpness, shift, factor = scalars[0], scalars[1], scalars[2]
    logits = sharpness * products + shift
    diagonal = iota(products.shape, 0) == iota(products.shape, 1)
    sign = jnp.where(diagonal, 1.0, -1.0)
    return (-(factor / PAIRS) * sharpness) * sign * jax.nn.sigmoid(-sign * logits)


def pool_grads(g_img, g_txt, u, inv, gain):
    a, b = g_img.reshape(NZ, NZ, D), g_txt.reshape(NZ, NZ, D)
    grad = jnp.concatenate([a, b], axis=1).reshape(GROUP, D)
    share = jnp.where(iota((NZ, 2 * NZ, 1), 1) < NZ, 1.0 / IMG, 1.0 / TXT).reshape(GROUP, 1)
    return (inv * share) * (grad - u * jnp.sum(u * grad, axis=1, keepdims=True)) * gain


def own_loss_kernel(scalars, near, far, gains, own, unit, inverse, img, txt):
    load_units(near, far, unit, inverse, img, txt, 1)

    def side(mine, others):
        hi, low = two(slopes(scalars, dot(mine[:HALF, :], others[...], 1, 1)))
        both = dot(jnp.concatenate([hi, low], axis=0), others[...])
        return both[:HALF] + both[HALF:]

    own[...] = pool_grads(side(img, txt), side(txt, img), unit[...], inverse[...], gains[1:2, :])


def all_loss(scalars, near, far, gains, every, unit, inverse, img, txt):
    load_units(near, far, unit, inverse, img, txt, DP)
    slope = slopes(scalars, dot(img[...], txt[...], 1, 1)).astype(BF)
    g_img = dot(slope, txt[...])
    g_txt = dot(slope, img[...], 0, 0)
    for i in range(DP):
        at, half = slice(i * GROUP, (i + 1) * GROUP), slice(i * HALF, (i + 1) * HALF)
        every[i] = pool_grads(
            g_img[half], g_txt[half], unit[at, :], inverse[at, :], gains[1:2, :]
        ).astype(BF)


def merge_kernel(a, b, c, d, out):
    for i, piece in enumerate((a, b, c, d)):
        out[i * GROUP : (i + 1) * GROUP, :] = piece[...]


def merge(pieces):
    return pl.pallas_call(
        merge_kernel,
        out_shape=jax.ShapeDtypeStruct((DP // 2 * GROUP, D), BF),
        compiler_params=params(8),
    )(*pieces)


def own_loss(scalars, near, far, gains):
    return pl.pallas_call(
        own_loss_kernel,
        in_specs=[pl.BlockSpec(memory_space=pltpu.SMEM)] + [VM] * 3,
        out_specs=VM,
        out_shape=jax.ShapeDtypeStruct((GROUP, D), F32),
        scratch_shapes=[
            pltpu.VMEM((GROUP, D), F32),
            pltpu.VMEM((GROUP, 1), F32),
            pltpu.VMEM((PAIRS, D), BF),
            pltpu.VMEM((PAIRS, D), BF),
        ],
        compiler_params=params(24),
        cost_estimate=cost(6 * GROUP * PAIRS * D, 3000000, GROUP * PAIRS),
    )(scalars, near, far, gains)


def backward_kernel(
    bundle, hot, scaled_in, grads, gains, slope, w1, w2, out, mark,
    scr, mixed, rows, acc,
):
    hi, low = two(grads[...])
    mixed[...] = dot(hot[:, :GROUP], hi) + dot(hot[:, :GROUP], low)

    def column(at, n):
        return jnp.sum(hot[at, GROUP + 3 * n : GROUP + 3 * n + 3].astype(F32), axis=1, keepdims=True)

    for j in range(CAP):
        at = slice(j * E, (j + 1) * E)
        grad = norm_back(mixed[at, :], bundle[at, :].astype(F32), column(at, 0))
        mixed[at, :] = grad
        rows[at, :] = (column(at, 2) * grad).astype(BF)
    for i in range(H // HB):
        at = slice(i * HB, (i + 1) * HB)
        hidden = (dot(rows[...], w2[at, :], 1, 1) * slope[:, at].astype(F32)).astype(BF)
        term = dot(hidden, w1[:, at], 1, 1)
        acc[...] = term if i == 0 else acc[...] + term
    for j in range(CAP):
        at = slice(j * E, (j + 1) * E)
        back = acc[at, :].astype(BF).astype(F32) * gains[0:1, :]
        mixed[at, :] += norm_back(back, scaled_in[at, :].astype(F32), column(at, 1))
    for row in (META, META + 1):
        scr[pl.ds(row, E, stride=SLAB), :] = jnp.zeros((E, LANES), F32)
    pack_rows(scr, mixed)
    out[...] = scr[...].astype(BF)
    mark[...] = jnp.zeros_like(mark)


def backward(bundle, hot, scaled_in, grads, gains, slope, w1, w2):
    return pl.pallas_call(
        backward_kernel,
        in_specs=[VM] * 8,
        out_specs=(VM, VM),
        out_shape=(jax.ShapeDtypeStruct((PACKED, LANES), BF), MARK),
        scratch_shapes=[
            pltpu.VMEM((PACKED, LANES), F32),
            pltpu.VMEM((ROWS, D), F32),
            pltpu.VMEM((ROWS, D), BF),
            pltpu.VMEM((ROWS, D), F32),
        ],
        compiler_params=params(24),
        cost_estimate=cost(4 * ROWS * D * H, 4 * D * H + 2 * ROWS * H),
    )(bundle, hot, scaled_in, grads, gains, slope, w1, w2)


def slice_kernel(
    dp, arr, gains, w1, pooled, normed_t, hidden_t, slope, passed, scr, x, normed, hidden, w1s, sem
):
    step = pl.program_id(0)
    at = pl.ds(pl.multiple_of(dp[0] * HS, HS), HS)
    copy = pltpu.make_async_copy(w1.at[:, at], w1s, sem)

    @pl.when(step == 0)
    def _():
        copy.start()
        passed[...] = pooled[...]

    scr[...] = arr[0].astype(F32)
    unpack_rows(scr, x)
    scaled, _inverse = norm(x[...])
    rows = (scaled * gains[0:1, :]).astype(BF)
    at = pl.ds(pl.multiple_of(step * ROWS, ROWS), ROWS)
    normed[at, :] = rows

    @pl.when(step == 0)
    def _():
        copy.wait()

    value, grad = gelu_parts(dot(rows, w1s[...]))
    hidden[at, :] = value.astype(BF)
    slope[...] = grad.astype(BF)

    @pl.when(step == pl.num_programs(0) - 1)
    def _():
        normed_t[...] = normed[...].T
        hidden_t[...] = hidden[...].T


ALL = DP * ROWS


def hidden_slice(dp, arrs, gains, w1, pooled):
    return pl.pallas_call(
        slice_kernel,
        grid_spec=pltpu.PrefetchScalarGridSpec(
            num_scalar_prefetch=1,
            grid=(DP,),
            in_specs=[
                pl.BlockSpec((1, PACKED, LANES), lambda h, dp: (h, 0, 0)),
                whole((2, D)),
                IN_HBM,
                whole((GROUP, D)),
            ],
            out_specs=(
                whole((D, ALL)),
                whole((HS, ALL)),
                pl.BlockSpec((ROWS, HS), lambda h, dp: (h, 0)),
                whole((GROUP, D)),
            ),
            scratch_shapes=[
                pltpu.VMEM((PACKED, LANES), F32),
                pltpu.VMEM((ROWS, D), F32),
                pltpu.VMEM((ALL, D), BF),
                pltpu.VMEM((ALL, HS), BF),
                pltpu.VMEM((D, HS), BF),
                pltpu.SemaphoreType.DMA,
            ],
        ),
        out_shape=(
            jax.ShapeDtypeStruct((D, ALL), BF),
            jax.ShapeDtypeStruct((HS, ALL), BF),
            jax.ShapeDtypeStruct((ALL, HS), BF),
            jax.ShapeDtypeStruct((GROUP, D), BF),
        ),
        compiler_params=params(40),
        cost_estimate=cost(2 * ALL * D * HS, 12000000, 2 * ALL * HS),
    )(dp, arrs, gains, w1, pooled)


def weights_kernel(
    dp, scalars, near, far, gains, bundle, slope, _, normed_t, hidden_t, w2, g_in, g_out, mark,
    hot, rows, hidden, normed, value, w2s, every, unit, inverse, img, txt, sem,
):
    step = pl.program_id(0)
    at = pl.ds(pl.multiple_of(dp[0] * HS, HS), HS)
    weights = pltpu.make_async_copy(w2.at[at, :], w2s, sem.at[0])
    late = [
        pltpu.make_async_copy(normed_t, normed, sem.at[1]),
        pltpu.make_async_copy(hidden_t, value, sem.at[2]),
    ]

    @pl.when(step == 0)
    def _():
        weights.start()
        for copy in late:
            copy.start()
        all_loss(scalars, near, far, gains, every, unit, inverse, img, txt)
        weights.wait()

    for b in range(2):
        meta = bundle[b, ROWS:, : 2 * LANES].astype(F32)
        meta = jnp.concatenate([meta[:, :LANES], meta[:, LANES:]], axis=0)
        fill_hot(hot, meta)
        place = (step ^ lax.div(dp[0], 2)) + 4 * (b ^ lax.rem(dp[0], 2))
        q = dot(hot[...], every[place])
        for j in range(CAP):
            at = slice(j * E, (j + 1) * E)
            grad = norm_back(q[at, :], bundle[b, at, :].astype(F32), meta_chance(meta, j))
            first = pl.multiple_of((2 * step + b) * ROWS + j * E, E)
            rows[pl.ds(first, E), :] = grad.astype(BF)
    at = pl.ds(pl.multiple_of(step * (2 * ROWS), 2 * ROWS), 2 * ROWS)
    hidden[at, :] = (dot(rows[at, :], w2s[...], 1, 1) * slope[...].astype(F32)).astype(BF)

    @pl.when(step == pl.num_programs(0) - 1)
    def _():
        for copy in late:
            copy.wait()
        g_in[...] = dot(normed[...], hidden[...]).astype(BF)
        g_out[...] = dot(value[...], rows[...]).astype(BF)
        mark[...] = jnp.zeros_like(mark)


def weight_grads(dp, scalars, near, far, gains, bundles, slope, after, normed_t, hidden_t, w2):
    return pl.pallas_call(
        weights_kernel,
        grid_spec=pltpu.PrefetchScalarGridSpec(
            num_scalar_prefetch=2,
            grid=(DP // 2,),
            in_specs=[
                whole((DP // 2 * GROUP, D)),
                whole((DP // 2 * GROUP, D)),
                whole((2, D)),
                pl.BlockSpec((2, ROWS + TAIL, D), lambda h, *_: (h, 0, 0)),
                pl.BlockSpec((2 * ROWS, HS), lambda h, *_: (h, 0)),
                whole(MARK.shape),
                IN_HBM,
                IN_HBM,
                IN_HBM,
            ],
            out_specs=(whole((D, HS)), whole((HS, D)), whole(MARK.shape)),
            scratch_shapes=[
                pltpu.VMEM((ROWS, GROUP), BF),
                pltpu.VMEM((ALL, D), BF),
                pltpu.VMEM((ALL, HS), BF),
                pltpu.VMEM((D, ALL), BF),
                pltpu.VMEM((HS, ALL), BF),
                pltpu.VMEM((HS, D), BF),
                pltpu.VMEM((DP, GROUP, D), BF),
                pltpu.VMEM((DP * GROUP, D), F32),
                pltpu.VMEM((DP * GROUP, 1), F32),
                pltpu.VMEM((PAIRS, D), BF),
                pltpu.VMEM((PAIRS, D), BF),
                pltpu.SemaphoreType.DMA((3,)),
            ],
        ),
        out_shape=(
            jax.ShapeDtypeStruct((D, HS), BF),
            jax.ShapeDtypeStruct((HS, D), BF),
            MARK,
        ),
        compiler_params=params(57),
        cost_estimate=cost(6 * ALL * D * HS + 10 * PAIRS * PAIRS * D, 15000000),
    )(dp, scalars, near, far, gains, bundles, slope, after, normed_t, hidden_t, w2)


def collect_kernel(arr, slot, _, out, scr, rows):
    scr[...] = arr[...].astype(F32)
    unpack_rows(scr, rows)
    taking = (iota((TOK, ROWS), 1) == slot[...].astype(jnp.int32)).astype(F32).astype(BF)
    out[...] = dot(taking, rows[...].astype(BF)).astype(BF)


def collect(arr, slot, after):
    return pl.pallas_call(
        collect_kernel,
        out_shape=jax.ShapeDtypeStruct((TOK, D), BF),
        scratch_shapes=[pltpu.VMEM((PACKED, LANES), F32), pltpu.VMEM((ROWS, D), F32)],
        compiler_params=params(16),
        cost_estimate=cost(2 * ROWS * TOK * D, 700000),
    )(arr, slot, after)


Z_GROUPS = [[x * NZ + z for z in range(NZ)] for x in range(NX)]


def to_experts(packed):
    slabs = packed.reshape(E, SLAB, LANES)
    slabs = lax.all_to_all(slabs, "expert", split_axis=0, concat_axis=0, tiled=True)
    return slabs.reshape(PACKED, LANES)


def along_z(values):
    return lax.all_to_all(
        values, "expert", split_axis=0, concat_axis=0, tiled=True, axis_index_groups=Z_GROUPS
    )


def swap(values, axis, size, by):
    return lax.ppermute(values, axis, [(i, i ^ by) for i in range(size)])


def on_device(
    incoming_elements,
    assigned_specialist,
    element_couple_kind,
    chosen_specialist_chance,
    specialist_layernorm_multiplier,
    final_layernorm_multiplier_vec,
    specialist_first_matrix,
    specialist_second_matrix,
    sharpness_factor,
    similarity_shift_term,
    objective_adjoint_factor,
):
    w1 = specialist_first_matrix[0]
    w2 = specialist_second_matrix[0]
    dp = lax.axis_index("dp").astype(jnp.int32).reshape(1)

    packed, slot, gains = dispatch(
        incoming_elements,
        assigned_specialist,
        element_couple_kind,
        chosen_specialist_chance,
        specialist_layernorm_multiplier,
        final_layernorm_multiplier_vec,
    )
    arr = to_experts(packed)
    arrs = lax.all_gather(arr, "dp", axis=0)
    part, bundle, slope, hot, scaled_in = forward(arr, gains, w1, w2)
    bundles = lax.all_gather(bundle, "dp", axis=0)

    part = along_z(part.reshape(NZ, 2 * NZ, D))
    part = jnp.sum(part.astype(F32), axis=0)
    others = [swap(part, "expert", E, NZ * m) for m in range(1, NX)]
    share = jnp.where(jnp.arange(2 * NZ) < NZ, 1.0 / IMG, 1.0 / TXT).astype(F32)
    pooled = (((part + others[0]) + (others[1] + others[2])) * share[:, None]).astype(BF)
    pooled = along_z(jnp.broadcast_to(pooled[None], (NZ, 2 * NZ, D))).reshape(GROUP, D)
    normed_t, hidden_t, grads, passed = hidden_slice(dp, arrs, gains, w1, pooled)
    near = merge([passed] + [swap(pooled, "dp", DP, m) for m in (2, 4, 6)])
    far = swap(near, "dp", DP, 1)

    scalars = jnp.concatenate([sharpness_factor, similarity_shift_term, objective_adjoint_factor])
    own = own_loss(scalars, near, far, gains)
    packed, mark = backward(bundle, hot, scaled_in, own, gains, slope, w1, w2)
    returned = to_experts(packed)
    grad_in, grad_out, mark = weight_grads(
        dp, scalars, near, far, gains, bundles, grads, mark, normed_t, hidden_t, w2
    )
    token_grads = collect(returned, slot, mark)
    return (token_grads, grad_in[None], grad_out[None])


def solution(mesh):
    return jax.shard_map(
        on_device,
        mesh=mesh,
        in_specs=(
            P(("expert", "dp"), None),
            P(("expert", "dp"), None),
            P(("expert", "dp")),
            P(("expert", "dp")),
            P(),
            P(),
            P("expert", None, None),
            P("expert", None, None),
            P(),
            P(),
            P(),
        ),
        out_specs=(P(("expert", "dp"), None), P("expert", None, "dp"), P("expert", "dp", None)),
        check_vma=False,
    )
```

```python
import jax
import jax.numpy as jnp
from jax import lax
from jax.experimental import pallas as pl
from jax.experimental.pallas import tpu as pltpu
from jax.sharding import PartitionSpec as P

D = 768
H = 3072
IMG = 50
TXT = 16
E = 32
DP = 8
NX = 4
NZ = 8
TOK = 132
CAP = 9
PAIRS = 512
ROWS = E * CAP
LANES = 128
CHUNKS = D // LANES
SLAB = 56
META = CAP * CHUNKS
TAIL = 16
PACKED = E * SLAB
HB = 1024
HS = H // DP
GROUP = 4 * E

EPS = 1e-06
ROOT_HALF = 0.7071067811865476
INV_ROOT_TAU = 0.3989422804014327
BF = jnp.bfloat16
F32 = jnp.float32


def params(mib):
    return pltpu.CompilerParams(vmem_limit_bytes=mib * 1024 * 1024)


def cost(flops, moved, trans=0):
    return pl.CostEstimate(flops=int(flops), bytes_accessed=int(moved), transcendentals=int(trans))


def dot(a, b, ca=1, cb=0):
    return lax.dot_general(a, b, (((ca,), (cb,)), ((), ())), preferred_element_type=F32)


def norm(values):
    center = values - jnp.mean(values, axis=1, keepdims=True)
    inverse = lax.rsqrt(jnp.mean(center * center, axis=1, keepdims=True) + EPS)
    return center * inverse, inverse


def norm_back(grad_hat, scaled, inverse):
    return inverse * (
        grad_hat
        - jnp.mean(grad_hat, axis=1, keepdims=True)
        - scaled * jnp.mean(grad_hat * scaled, axis=1, keepdims=True)
    )


def gelu_parts(v):
    e = jnp.exp(-0.5 * v * v)
    t = pl.reciprocal(1.0 + (0.3275911 * ROOT_HALF) * jnp.abs(v))
    tail = t * (0.5 * 1.061405429) + (0.5 * -1.453152027)
    tail = t * tail + (0.5 * 1.421413741)
    tail = t * tail + (0.5 * -0.284496736)
    tail = t * tail + (0.5 * 0.254829592)
    tail = t * tail * e
    cdf = jnp.where(v < 0.0, tail, 1.0 - tail)
    return v * cdf, cdf + v * e * INV_ROOT_TAU


def three(v):
    hi = v.astype(BF).astype(F32)
    mid = (v - hi).astype(BF).astype(F32)
    return hi, mid, v - hi - mid


def iota(shape, dim):
    return lax.broadcasted_iota(jnp.int32, shape, dim)


def pack_rows(scr, rows):
    for j in range(CAP):
        for c in range(CHUNKS):
            scr[pl.ds(c * CAP + j, E, stride=SLAB), :] = rows[
                j * E : (j + 1) * E, c * LANES : (c + 1) * LANES
            ]


def unpack_rows(scr, rows):
    for j in range(CAP):
        for c in range(CHUNKS):
            rows[j * E : (j + 1) * E, c * LANES : (c + 1) * LANES] = scr[
                pl.ds(c * CAP + j, E, stride=SLAB), :
            ]


def meta_chance(meta, j):
    return meta[:, j : j + 1] + meta[:, 16 + j : 17 + j] + meta[:, 32 + j : 33 + j]


def fill_hot(hot, meta):
    s, lane = iota((E, GROUP), 0), iota((E, GROUP), 1)
    first = (s % NZ) * (4 * NX) + s // NZ
    marks = [(lane == first + NX * k).astype(F32) for k in range(4)]
    for j in range(CAP):
        rows = jnp.zeros((E, GROUP), F32)
        for k in range(4):
            at = 48 + 16 * k + j
            rows += marks[k] * meta[:, at : at + 1]
        hot[j * E : (j + 1) * E, :GROUP] = rows.astype(BF)


def two(v):
    hi = v.astype(BF)
    return hi, (v - hi.astype(F32)).astype(BF)


VM = pl.BlockSpec(memory_space=pltpu.VMEM)
IN_HBM = pl.BlockSpec(memory_space=pltpu.HBM)
MARK = jax.ShapeDtypeStruct((8, LANES), F32)


def dispatch_kernel(x, route, kind, chance, gain_in, gain_out, out, slot, gains, scr, rows):
    gains[0:1, :] = gain_in[...].reshape(1, D)
    gains[1:2, :] = gain_out[...].reshape(1, D)
    eye = iota((TOK, TOK), 0) == iota((TOK, TOK), 1)

    def column(row):
        return jnp.sum(jnp.where(eye, row, 0.0), axis=1, keepdims=True)

    onehot = (iota((E, TOK), 0) == route[...]).astype(F32)
    upper = (iota((TOK, TOK), 0) <= iota((TOK, TOK), 1)).astype(BF)
    run = dot(onehot.astype(BF), upper)
    pos = jnp.sum(onehot * run, axis=0, keepdims=True) - 1.0
    target = pos * E + route[...].astype(F32)
    placing = (iota((ROWS, TOK), 0) == target.astype(jnp.int32)).astype(F32).astype(BF)
    rows[...] = dot(placing, x[...])

    slot[...] = column(target)
    lane = iota((TOK, LANES), 1)
    field = lane // 16
    hi, mid, low = three(column(chance[...]))
    same = (column(kind[...].astype(F32)).astype(jnp.int32) == field - 3).astype(F32)
    held = jnp.where(
        field == 0, hi, jnp.where(field == 1, mid, jnp.where(field == 2, low, same))
    )
    held = jnp.where(lane % 16 == column(pos).astype(jnp.int32), held, 0.0).astype(BF)
    scr[pl.ds(META, E, stride=SLAB), :] = dot(onehot.astype(BF), held)
    scr[pl.ds(META + 1, E, stride=SLAB), :] = jnp.zeros((E, LANES), F32)
    pack_rows(scr, rows)
    out[...] = scr[...].astype(BF)


def dispatch(x, route, kind, chance, gain_in, gain_out):
    return pl.pallas_call(
        dispatch_kernel,
        out_shape=(
            jax.ShapeDtypeStruct((PACKED, LANES), BF),
            jax.ShapeDtypeStruct((TOK, 1), F32),
            jax.ShapeDtypeStruct((2, D), F32),
        ),
        scratch_shapes=[pltpu.VMEM((PACKED, LANES), F32), pltpu.VMEM((ROWS, D), F32)],
        compiler_params=params(60),
        cost_estimate=cost(2 * ROWS * TOK * D, 700000),
    )(
        x,
        route.reshape(1, TOK),
        kind.reshape(1, TOK),
        chance.reshape(1, TOK),
        gain_in,
        gain_out,
    )


def forward_kernel(
    arr, gains, w1, w2, part, bundle, slope, hot, scaled_in,
    scr, x, normed, acc, w1v, w2v, sem,
):
    cols = [slice(i * HB, (i + 1) * HB) for i in range(H // HB)]
    fetches = [
        (
            pltpu.make_async_copy(w1.at[:, at], w1v.at[:, at], sem.at[0, i]),
            pltpu.make_async_copy(w2.at[at, :], w2v.at[at, :], sem.at[1, i]),
        )
        for i, at in enumerate(cols)
    ]
    for first, second in fetches:
        first.start()
        second.start()
    scr[...] = arr[...].astype(F32)
    unpack_rows(scr, x)
    scaled, inverse = norm(x[...])
    normed[...] = (scaled * gains[0:1, :]).astype(BF)
    scaled_in[...] = scaled.astype(BF)
    for f, v in enumerate(three(inverse)):
        hot[:, GROUP + 3 + f : GROUP + 4 + f] = v.astype(BF)
    for i, at in enumerate(cols):
        fetches[i][0].wait()
        hidden, grad = gelu_parts(dot(normed[...], w1v[:, at]))
        slope[:, at] = grad.astype(BF)
        fetches[i][1].wait()
        term = dot(hidden.astype(BF), w2v[at, :])
        acc[...] = term if i == 0 else acc[...] + term
    meta = scr[pl.ds(META, E, stride=SLAB), :]
    fill_hot(hot, meta)
    lane = iota((E, LANES), 1)
    routing = jnp.where(lane >= 48, meta, 0.0)
    for j in range(CAP):
        at = slice(j * E, (j + 1) * E)
        chance = meta_chance(meta, j)
        mixed = x[at, :] + chance * acc[at, :].astype(BF).astype(F32)
        scaled, inverse = norm(mixed)
        bundle[at, :] = scaled.astype(BF)
        for f, v in enumerate(three(inverse) + three(chance)):
            lane_at = GROUP + f + (3 if f > 2 else 0)
            hot[at, lane_at : lane_at + 1] = v.astype(BF)
        acc[at, :] = scaled * gains[1:2, :]
        for f, v in enumerate(three(chance * inverse)):
            routing = jnp.where(lane == 16 * f + j, v, routing)
    bundle[ROWS:, 2 * LANES :] = jnp.zeros((TAIL, D - 2 * LANES), BF)
    for c in range(E // TAIL):
        bundle[ROWS:, c * LANES : (c + 1) * LANES] = routing[c * TAIL : (c + 1) * TAIL].astype(BF)
    hi, low = two(acc[...])
    part[...] = (dot(hot[:, :GROUP], hi, 0, 0) + dot(hot[:, :GROUP], low, 0, 0)).astype(BF)


def whole(shape):
    return pl.BlockSpec(shape, lambda *_: (0,) * len(shape))


def forward(arr, gains, w1, w2):
    return pl.pallas_call(
        forward_kernel,
        in_specs=[VM, VM, IN_HBM, IN_HBM],
        out_specs=(VM,) * 5,
        out_shape=(
            jax.ShapeDtypeStruct((GROUP, D), BF),
            jax.ShapeDtypeStruct((ROWS + TAIL, D), BF),
            jax.ShapeDtypeStruct((ROWS, H), BF),
            jax.ShapeDtypeStruct((ROWS, 2 * GROUP), BF),
            jax.ShapeDtypeStruct((ROWS, D), BF),
        ),
        scratch_shapes=[
            pltpu.VMEM((PACKED, LANES), F32),
            pltpu.VMEM((ROWS, D), F32),
            pltpu.VMEM((ROWS, D), BF),
            pltpu.VMEM((ROWS, D), F32),
            pltpu.VMEM((D, H), BF),
            pltpu.VMEM((H, D), BF),
            pltpu.SemaphoreType.DMA((2, H // HB)),
        ],
        compiler_params=params(48),
        cost_estimate=cost(4 * ROWS * D * H, 4 * D * H, 2 * ROWS * H),
    )(arr, gains, w1, w2)


HALF = PAIRS // DP


def load_units(near, far, unit, inverse, img, txt, keep):
    for i in range(DP):
        src = near if i < DP // 2 else far
        first = (i % (DP // 2)) * GROUP
        pooled = src[first : first + GROUP, :].astype(F32)
        inv = lax.rsqrt(jnp.sum(pooled * pooled, axis=1, keepdims=True) + EPS)
        u = pooled * inv
        if i < keep:
            unit[i * GROUP : (i + 1) * GROUP, :] = u
            inverse[i * GROUP : (i + 1) * GROUP, :] = inv
        u = u.reshape(NZ, 2 * NZ, D)
        img[i * HALF : (i + 1) * HALF, :] = u[:, :NZ].reshape(HALF, D).astype(BF)
        txt[i * HALF : (i + 1) * HALF, :] = u[:, NZ:].reshape(HALF, D).astype(BF)


def slopes(scalars, products):
    sharpness, shift, factor = scalars[0], scalars[1], scalars[2]
    logits = sharpness * products + shift
    diagonal = iota(products.shape, 0) == iota(products.shape, 1)
    sign = jnp.where(diagonal, 1.0, -1.0)
    return (-(factor / PAIRS) * sharpness) * sign * jax.nn.sigmoid(-sign * logits)


def pool_grads(g_img, g_txt, u, inv, gain):
    a, b = g_img.reshape(NZ, NZ, D), g_txt.reshape(NZ, NZ, D)
    grad = jnp.concatenate([a, b], axis=1).reshape(GROUP, D)
    share = jnp.where(iota((NZ, 2 * NZ, 1), 1) < NZ, 1.0 / IMG, 1.0 / TXT).reshape(GROUP, 1)
    return (inv * share) * (grad - u * jnp.sum(u * grad, axis=1, keepdims=True)) * gain


def own_loss(scalars, near, far, gains, unit, inverse, img, txt):
    load_units(near, far, unit, inverse, img, txt, 1)

    def side(mine, others):
        hi, low = two(slopes(scalars, dot(mine[:HALF, :], others[...], 1, 1)))
        both = dot(jnp.concatenate([hi, low], axis=0), others[...])
        return both[:HALF] + both[HALF:]

    return pool_grads(side(img, txt), side(txt, img), unit[...], inverse[...], gains[1:2, :])


def all_loss(scalars, near, far, gains, every, unit, inverse, img, txt):
    load_units(near, far, unit, inverse, img, txt, DP)
    slope = slopes(scalars, dot(img[...], txt[...], 1, 1)).astype(BF)
    g_img = dot(slope, txt[...])
    g_txt = dot(slope, img[...], 0, 0)
    for i in range(DP):
        at, half = slice(i * GROUP, (i + 1) * GROUP), slice(i * HALF, (i + 1) * HALF)
        every[i] = pool_grads(
            g_img[half], g_txt[half], unit[at, :], inverse[at, :], gains[1:2, :]
        ).astype(BF)


def merge_kernel(a, b, c, d, out):
    for i, piece in enumerate((a, b, c, d)):
        out[i * GROUP : (i + 1) * GROUP, :] = piece[...]


def merge(pieces):
    return pl.pallas_call(
        merge_kernel,
        out_shape=jax.ShapeDtypeStruct((DP // 2 * GROUP, D), BF),
        compiler_params=params(8),
    )(*pieces)


def backward_kernel(
    scalars, near, far, gains, bundle, hot, scaled_in, slope, w1, w2, out, mark,
    scr, mixed, rows, acc, unit, inverse, img, txt, w2v, sem,
):
    fetch = pltpu.make_async_copy(w2, w2v, sem)
    fetch.start()
    hi, low = two(own_loss(scalars, near, far, gains, unit, inverse, img, txt))
    mixed[...] = dot(hot[:, :GROUP], hi) + dot(hot[:, :GROUP], low)

    def column(at, n):
        return jnp.sum(hot[at, GROUP + 3 * n : GROUP + 3 * n + 3].astype(F32), axis=1, keepdims=True)

    for j in range(CAP):
        at = slice(j * E, (j + 1) * E)
        grad = norm_back(mixed[at, :], bundle[at, :].astype(F32), column(at, 0))
        mixed[at, :] = grad
        rows[at, :] = (column(at, 2) * grad).astype(BF)
    fetch.wait()
    for i in range(H // HB):
        at = slice(i * HB, (i + 1) * HB)
        hidden = (dot(rows[...], w2v[at, :], 1, 1) * slope[:, at].astype(F32)).astype(BF)
        term = dot(hidden, w1[:, at], 1, 1)
        acc[...] = term if i == 0 else acc[...] + term
    for j in range(CAP):
        at = slice(j * E, (j + 1) * E)
        back = acc[at, :].astype(BF).astype(F32) * gains[0:1, :]
        mixed[at, :] += norm_back(back, scaled_in[at, :].astype(F32), column(at, 1))
    for row in (META, META + 1):
        scr[pl.ds(row, E, stride=SLAB), :] = jnp.zeros((E, LANES), F32)
    pack_rows(scr, mixed)
    out[...] = scr[...].astype(BF)
    mark[...] = jnp.zeros_like(mark)


def backward(scalars, near, far, gains, bundle, hot, scaled_in, slope, w1, w2):
    return pl.pallas_call(
        backward_kernel,
        in_specs=[pl.BlockSpec(memory_space=pltpu.SMEM)] + [VM] * 8 + [IN_HBM],
        out_specs=(VM, VM),
        out_shape=(jax.ShapeDtypeStruct((PACKED, LANES), BF), MARK),
        scratch_shapes=[
            pltpu.VMEM((PACKED, LANES), F32),
            pltpu.VMEM((ROWS, D), F32),
            pltpu.VMEM((ROWS, D), BF),
            pltpu.VMEM((ROWS, D), F32),
            pltpu.VMEM((GROUP, D), F32),
            pltpu.VMEM((GROUP, 1), F32),
            pltpu.VMEM((PAIRS, D), BF),
            pltpu.VMEM((PAIRS, D), BF),
            pltpu.VMEM((H, D), BF),
            pltpu.SemaphoreType.DMA,
        ],
        compiler_params=params(44),
        cost_estimate=cost(4 * ROWS * D * H + 6 * GROUP * PAIRS * D, 4 * D * H + 2 * ROWS * H),
    )(scalars, near, far, gains, bundle, hot, scaled_in, slope, w1, w2)


def slice_kernel(
    dp, arr, gains, w1, pooled, normed_t, hidden_t, slope, passed, scr, x, normed, hidden, w1s, sem
):
    step = pl.program_id(0)
    at = pl.ds(pl.multiple_of(dp[0] * HS, HS), HS)
    copy = pltpu.make_async_copy(w1.at[:, at], w1s, sem)

    @pl.when(step == 0)
    def _():
        copy.start()
        passed[...] = pooled[...]

    scr[...] = arr[0].astype(F32)
    unpack_rows(scr, x)
    scaled, _inverse = norm(x[...])
    rows = (scaled * gains[0:1, :]).astype(BF)
    at = pl.ds(pl.multiple_of(step * ROWS, ROWS), ROWS)
    normed[at, :] = rows

    @pl.when(step == 0)
    def _():
        copy.wait()

    value, grad = gelu_parts(dot(rows, w1s[...]))
    hidden[at, :] = value.astype(BF)
    slope[...] = grad.astype(BF)

    @pl.when(step == pl.num_programs(0) - 1)
    def _():
        normed_t[...] = normed[...].T
        hidden_t[...] = hidden[...].T


ALL = DP * ROWS


def hidden_slice(dp, arrs, gains, w1, pooled):
    return pl.pallas_call(
        slice_kernel,
        grid_spec=pltpu.PrefetchScalarGridSpec(
            num_scalar_prefetch=1,
            grid=(DP,),
            in_specs=[
                pl.BlockSpec((1, PACKED, LANES), lambda h, dp: (h, 0, 0)),
                whole((2, D)),
                IN_HBM,
                whole((GROUP, D)),
            ],
            out_specs=(
                whole((D, ALL)),
                whole((HS, ALL)),
                pl.BlockSpec((ROWS, HS), lambda h, dp: (h, 0)),
                whole((GROUP, D)),
            ),
            scratch_shapes=[
                pltpu.VMEM((PACKED, LANES), F32),
                pltpu.VMEM((ROWS, D), F32),
                pltpu.VMEM((ALL, D), BF),
                pltpu.VMEM((ALL, HS), BF),
                pltpu.VMEM((D, HS), BF),
                pltpu.SemaphoreType.DMA,
            ],
        ),
        out_shape=(
            jax.ShapeDtypeStruct((D, ALL), BF),
            jax.ShapeDtypeStruct((HS, ALL), BF),
            jax.ShapeDtypeStruct((ALL, HS), BF),
            jax.ShapeDtypeStruct((GROUP, D), BF),
        ),
        compiler_params=params(50),
        cost_estimate=cost(2 * ALL * D * HS, 12000000, 2 * ALL * HS),
    )(dp, arrs, gains, w1, pooled)


def weights_kernel(
    dp, scalars, near, far, gains, bundle, slope, _, normed_t, hidden_t, w2, g_in, g_out, mark,
    hot, rows, hidden, normed, value, w2s, every, unit, inverse, img, txt, sem,
):
    step = pl.program_id(0)
    at = pl.ds(pl.multiple_of(dp[0] * HS, HS), HS)
    weights = pltpu.make_async_copy(w2.at[at, :], w2s, sem.at[0])
    late = [
        pltpu.make_async_copy(normed_t, normed, sem.at[1]),
        pltpu.make_async_copy(hidden_t, value, sem.at[2]),
    ]

    @pl.when(step == 0)
    def _():
        weights.start()
        for copy in late:
            copy.start()
        all_loss(scalars, near, far, gains, every, unit, inverse, img, txt)
        weights.wait()

    for b in range(2):
        meta = bundle[b, ROWS:, : 2 * LANES].astype(F32)
        meta = jnp.concatenate([meta[:, :LANES], meta[:, LANES:]], axis=0)
        fill_hot(hot, meta)
        place = (step ^ lax.div(dp[0], 2)) + 4 * (b ^ lax.rem(dp[0], 2))
        q = dot(hot[...], every[place])
        for j in range(CAP):
            at = slice(j * E, (j + 1) * E)
            grad = norm_back(q[at, :], bundle[b, at, :].astype(F32), meta_chance(meta, j))
            first = pl.multiple_of((2 * step + b) * ROWS + j * E, E)
            rows[pl.ds(first, E), :] = grad.astype(BF)
    at = pl.ds(pl.multiple_of(step * (2 * ROWS), 2 * ROWS), 2 * ROWS)
    hidden[at, :] = (dot(rows[at, :], w2s[...], 1, 1) * slope[...].astype(F32)).astype(BF)

    @pl.when(step == pl.num_programs(0) - 1)
    def _():
        for copy in late:
            copy.wait()
        g_in[...] = dot(normed[...], hidden[...]).astype(BF)
        g_out[...] = dot(value[...], rows[...]).astype(BF)
        mark[...] = jnp.zeros_like(mark)


def weight_grads(dp, scalars, near, far, gains, bundles, slope, after, normed_t, hidden_t, w2):
    return pl.pallas_call(
        weights_kernel,
        grid_spec=pltpu.PrefetchScalarGridSpec(
            num_scalar_prefetch=2,
            grid=(DP // 2,),
            in_specs=[
                whole((DP // 2 * GROUP, D)),
                whole((DP // 2 * GROUP, D)),
                whole((2, D)),
                pl.BlockSpec((2, ROWS + TAIL, D), lambda h, *_: (h, 0, 0)),
                pl.BlockSpec((2 * ROWS, HS), lambda h, *_: (h, 0)),
                whole(MARK.shape),
                IN_HBM,
                IN_HBM,
                IN_HBM,
            ],
            out_specs=(whole((D, HS)), whole((HS, D)), whole(MARK.shape)),
            scratch_shapes=[
                pltpu.VMEM((ROWS, GROUP), BF),
                pltpu.VMEM((ALL, D), BF),
                pltpu.VMEM((ALL, HS), BF),
                pltpu.VMEM((D, ALL), BF),
                pltpu.VMEM((HS, ALL), BF),
                pltpu.VMEM((HS, D), BF),
                pltpu.VMEM((DP, GROUP, D), BF),
                pltpu.VMEM((DP * GROUP, D), F32),
                pltpu.VMEM((DP * GROUP, 1), F32),
                pltpu.VMEM((PAIRS, D), BF),
                pltpu.VMEM((PAIRS, D), BF),
                pltpu.SemaphoreType.DMA((3,)),
            ],
        ),
        out_shape=(
            jax.ShapeDtypeStruct((D, HS), BF),
            jax.ShapeDtypeStruct((HS, D), BF),
            MARK,
        ),
        compiler_params=params(57),
        cost_estimate=cost(6 * ALL * D * HS + 10 * PAIRS * PAIRS * D, 15000000),
    )(dp, scalars, near, far, gains, bundles, slope, after, normed_t, hidden_t, w2)


def collect_kernel(arr, slot, _, out, scr, rows):
    scr[...] = arr[...].astype(F32)
    unpack_rows(scr, rows)
    taking = (iota((TOK, ROWS), 1) == slot[...].astype(jnp.int32)).astype(F32).astype(BF)
    out[...] = dot(taking, rows[...].astype(BF)).astype(BF)


def collect(arr, slot, after):
    return pl.pallas_call(
        collect_kernel,
        out_shape=jax.ShapeDtypeStruct((TOK, D), BF),
        scratch_shapes=[pltpu.VMEM((PACKED, LANES), F32), pltpu.VMEM((ROWS, D), F32)],
        compiler_params=params(16),
        cost_estimate=cost(2 * ROWS * TOK * D, 700000),
    )(arr, slot, after)


Z_GROUPS = [[x * NZ + z for z in range(NZ)] for x in range(NX)]


def to_experts(packed):
    slabs = packed.reshape(E, SLAB, LANES)
    slabs = lax.all_to_all(slabs, "expert", split_axis=0, concat_axis=0, tiled=True)
    return slabs.reshape(PACKED, LANES)


def along_z(values):
    return lax.all_to_all(
        values, "expert", split_axis=0, concat_axis=0, tiled=True, axis_index_groups=Z_GROUPS
    )


def swap(values, axis, size, by):
    return lax.ppermute(values, axis, [(i, i ^ by) for i in range(size)])


def on_device(
    incoming_elements,
    assigned_specialist,
    element_couple_kind,
    chosen_specialist_chance,
    specialist_layernorm_multiplier,
    final_layernorm_multiplier_vec,
    specialist_first_matrix,
    specialist_second_matrix,
    sharpness_factor,
    similarity_shift_term,
    objective_adjoint_factor,
):
    w1 = specialist_first_matrix[0]
    w2 = specialist_second_matrix[0]
    dp = lax.axis_index("dp").astype(jnp.int32).reshape(1)

    packed, slot, gains = dispatch(
        incoming_elements,
        assigned_specialist,
        element_couple_kind,
        chosen_specialist_chance,
        specialist_layernorm_multiplier,
        final_layernorm_multiplier_vec,
    )
    arr = to_experts(packed)
    arrs = lax.all_gather(arr, "dp", axis=0)
    part, bundle, slope, hot, scaled_in = forward(arr, gains, w1, w2)
    bundles = lax.all_gather(bundle, "dp", axis=0)

    part = along_z(part.reshape(NZ, 2 * NZ, D))
    part = jnp.sum(part.astype(F32), axis=0)
    others = [swap(part, "expert", E, NZ * m) for m in range(1, NX)]
    share = jnp.where(jnp.arange(2 * NZ) < NZ, 1.0 / IMG, 1.0 / TXT).astype(F32)
    pooled = (((part + others[0]) + (others[1] + others[2])) * share[:, None]).astype(BF)
    pooled = along_z(jnp.broadcast_to(pooled[None], (NZ, 2 * NZ, D))).reshape(GROUP, D)
    normed_t, hidden_t, grads, passed = hidden_slice(dp, arrs, gains, w1, pooled)
    near = merge([passed] + [swap(pooled, "dp", DP, m) for m in (2, 4, 6)])
    far = swap(near, "dp", DP, 1)

    scalars = jnp.concatenate([sharpness_factor, similarity_shift_term, objective_adjoint_factor])
    packed, mark = backward(scalars, near, far, gains, bundle, hot, scaled_in, slope, w1, w2)
    returned = to_experts(packed)
    grad_in, grad_out, mark = weight_grads(
        dp, scalars, near, far, gains, bundles, grads, mark, normed_t, hidden_t, w2
    )
    token_grads = collect(returned, slot, mark)
    return (token_grads, grad_in[None], grad_out[None])


def solution(mesh):
    return jax.shard_map(
        on_device,
        mesh=mesh,
        in_specs=(
            P(("expert", "dp"), None),
            P(("expert", "dp"), None),
            P(("expert", "dp")),
            P(("expert", "dp")),
            P(),
            P(),
            P("expert", None, None),
            P("expert", None, None),
            P(),
            P(),
            P(),
        ),
        out_specs=(P(("expert", "dp"), None), P("expert", None, "dp"), P("expert", "dp", None)),
        check_vma=False,
    )
```

```python
import jax
import jax.numpy as jnp
from jax import lax
from jax.experimental import pallas as pl
from jax.experimental.pallas import tpu as pltpu
from jax.sharding import PartitionSpec as P

D = 768
H = 3072
IMG = 50
TXT = 16
E = 32
DP = 8
NX = 4
NZ = 8
TOK = 132
CAP = 9
PAIRS = 512
ROWS = E * CAP
LANES = 128
CHUNKS = D // LANES
SLAB = 56
META = CAP * CHUNKS
TAIL = 16
PACKED = E * SLAB
HB = 1024
HS = H // DP
GROUP = 4 * E

EPS = 1e-06
ROOT_HALF = 0.7071067811865476
INV_ROOT_TAU = 0.3989422804014327
BF = jnp.bfloat16
F32 = jnp.float32


def params(mib):
    return pltpu.CompilerParams(vmem_limit_bytes=mib * 1024 * 1024)


def cost(flops, moved, trans=0):
    return pl.CostEstimate(flops=int(flops), bytes_accessed=int(moved), transcendentals=int(trans))


def dot(a, b, ca=1, cb=0):
    return lax.dot_general(a, b, (((ca,), (cb,)), ((), ())), preferred_element_type=F32)


def norm(values):
    center = values - jnp.mean(values, axis=1, keepdims=True)
    inverse = lax.rsqrt(jnp.mean(center * center, axis=1, keepdims=True) + EPS)
    return center * inverse, inverse


def norm_back(grad_hat, scaled, inverse):
    return inverse * (
        grad_hat
        - jnp.mean(grad_hat, axis=1, keepdims=True)
        - scaled * jnp.mean(grad_hat * scaled, axis=1, keepdims=True)
    )


def gelu_parts(v):
    e = jnp.exp(-0.5 * v * v)
    t = pl.reciprocal(1.0 + (0.3275911 * ROOT_HALF) * jnp.abs(v))
    tail = t * (0.5 * 1.061405429) + (0.5 * -1.453152027)
    tail = t * tail + (0.5 * 1.421413741)
    tail = t * tail + (0.5 * -0.284496736)
    tail = t * tail + (0.5 * 0.254829592)
    tail = t * tail * e
    cdf = jnp.where(v < 0.0, tail, 1.0 - tail)
    return v * cdf, cdf + v * e * INV_ROOT_TAU


def three(v):
    hi = v.astype(BF).astype(F32)
    mid = (v - hi).astype(BF).astype(F32)
    return hi, mid, v - hi - mid


def iota(shape, dim):
    return lax.broadcasted_iota(jnp.int32, shape, dim)


def pack_rows(scr, rows):
    for j in range(CAP):
        for c in range(CHUNKS):
            scr[pl.ds(c * CAP + j, E, stride=SLAB), :] = rows[
                j * E : (j + 1) * E, c * LANES : (c + 1) * LANES
            ]


def unpack_rows(scr, rows):
    for j in range(CAP):
        for c in range(CHUNKS):
            rows[j * E : (j + 1) * E, c * LANES : (c + 1) * LANES] = scr[
                pl.ds(c * CAP + j, E, stride=SLAB), :
            ]


def meta_chance(meta, j):
    return meta[:, j : j + 1] + meta[:, 16 + j : 17 + j] + meta[:, 32 + j : 33 + j]


def fill_hot(hot, meta):
    s, lane = iota((E, GROUP), 0), iota((E, GROUP), 1)
    first = (s % NZ) * (4 * NX) + s // NZ
    marks = [(lane == first + NX * k).astype(F32) for k in range(4)]
    for j in range(CAP):
        rows = jnp.zeros((E, GROUP), F32)
        for k in range(4):
            at = 48 + 16 * k + j
            rows += marks[k] * meta[:, at : at + 1]
        hot[j * E : (j + 1) * E, :GROUP] = rows.astype(BF)


def two(v):
    hi = v.astype(BF)
    return hi, (v - hi.astype(F32)).astype(BF)


VM = pl.BlockSpec(memory_space=pltpu.VMEM)
IN_HBM = pl.BlockSpec(memory_space=pltpu.HBM)
MARK = jax.ShapeDtypeStruct((8, LANES), F32)


def dispatch_kernel(x, route, kind, chance, gain_in, gain_out, out, slot, gains, scr, rows):
    gains[0:1, :] = gain_in[...].reshape(1, D)
    gains[1:2, :] = gain_out[...].reshape(1, D)
    eye = iota((TOK, TOK), 0) == iota((TOK, TOK), 1)

    def column(row):
        return jnp.sum(jnp.where(eye, row, 0.0), axis=1, keepdims=True)

    onehot = (iota((E, TOK), 0) == route[...]).astype(F32)
    upper = (iota((TOK, TOK), 0) <= iota((TOK, TOK), 1)).astype(BF)
    run = dot(onehot.astype(BF), upper)
    pos = jnp.sum(onehot * run, axis=0, keepdims=True) - 1.0
    target = pos * E + route[...].astype(F32)
    placing = (iota((ROWS, TOK), 0) == target.astype(jnp.int32)).astype(F32).astype(BF)
    rows[...] = dot(placing, x[...])

    slot[...] = column(target)
    lane = iota((TOK, LANES), 1)
    field = lane // 16
    hi, mid, low = three(column(chance[...]))
    same = (column(kind[...].astype(F32)).astype(jnp.int32) == field - 3).astype(F32)
    held = jnp.where(
        field == 0, hi, jnp.where(field == 1, mid, jnp.where(field == 2, low, same))
    )
    held = jnp.where(lane % 16 == column(pos).astype(jnp.int32), held, 0.0).astype(BF)
    scr[pl.ds(META, E, stride=SLAB), :] = dot(onehot.astype(BF), held)
    scr[pl.ds(META + 1, E, stride=SLAB), :] = jnp.zeros((E, LANES), F32)
    pack_rows(scr, rows)
    out[...] = scr[...].astype(BF)


def dispatch(x, route, kind, chance, gain_in, gain_out):
    return pl.pallas_call(
        dispatch_kernel,
        out_shape=(
            jax.ShapeDtypeStruct((PACKED, LANES), BF),
            jax.ShapeDtypeStruct((TOK, 1), F32),
            jax.ShapeDtypeStruct((2, D), F32),
        ),
        scratch_shapes=[pltpu.VMEM((PACKED, LANES), F32), pltpu.VMEM((ROWS, D), F32)],
        compiler_params=params(60),
        cost_estimate=cost(2 * ROWS * TOK * D, 700000),
    )(
        x,
        route.reshape(1, TOK),
        kind.reshape(1, TOK),
        chance.reshape(1, TOK),
        gain_in,
        gain_out,
    )


def forward_kernel(
    arr, gains, w1, w2, part, bundle, slope, hot, scaled_in,
    scr, x, normed, acc, w1v, w2v, sem,
):
    cols = [slice(i * HB, (i + 1) * HB) for i in range(H // HB)]
    fetches = [
        (
            pltpu.make_async_copy(w1.at[:, at], w1v.at[:, at], sem.at[0, i]),
            pltpu.make_async_copy(w2.at[at, :], w2v.at[at, :], sem.at[1, i]),
        )
        for i, at in enumerate(cols)
    ]
    for first, second in fetches:
        first.start()
        second.start()
    scr[...] = arr[...].astype(F32)
    unpack_rows(scr, x)
    scaled, inverse = norm(x[...])
    normed[...] = (scaled * gains[0:1, :]).astype(BF)
    scaled_in[...] = scaled.astype(BF)
    for f, v in enumerate(three(inverse)):
        hot[:, GROUP + 3 + f : GROUP + 4 + f] = v.astype(BF)
    for i, at in enumerate(cols):
        fetches[i][0].wait()
        hidden, grad = gelu_parts(dot(normed[...], w1v[:, at]))
        slope[:, at] = grad.astype(BF)
        fetches[i][1].wait()
        term = dot(hidden.astype(BF), w2v[at, :])
        acc[...] = term if i == 0 else acc[...] + term
    meta = scr[pl.ds(META, E, stride=SLAB), :]
    fill_hot(hot, meta)
    lane = iota((E, LANES), 1)
    routing = jnp.where(lane >= 48, meta, 0.0)
    for j in range(CAP):
        at = slice(j * E, (j + 1) * E)
        chance = meta_chance(meta, j)
        mixed = x[at, :] + chance * acc[at, :].astype(BF).astype(F32)
        scaled, inverse = norm(mixed)
        bundle[at, :] = scaled.astype(BF)
        for f, v in enumerate(three(inverse) + three(chance)):
            lane_at = GROUP + f + (3 if f > 2 else 0)
            hot[at, lane_at : lane_at + 1] = v.astype(BF)
        acc[at, :] = scaled * gains[1:2, :]
        for f, v in enumerate(three(chance * inverse)):
            routing = jnp.where(lane == 16 * f + j, v, routing)
    bundle[ROWS:, 2 * LANES :] = jnp.zeros((TAIL, D - 2 * LANES), BF)
    for c in range(E // TAIL):
        bundle[ROWS:, c * LANES : (c + 1) * LANES] = routing[c * TAIL : (c + 1) * TAIL].astype(BF)
    hi, low = two(acc[...])
    part[...] = (dot(hot[:, :GROUP], hi, 0, 0) + dot(hot[:, :GROUP], low, 0, 0)).astype(BF)


def whole(shape):
    return pl.BlockSpec(shape, lambda *_: (0,) * len(shape))


def forward(arr, gains, w1, w2):
    return pl.pallas_call(
        forward_kernel,
        in_specs=[VM, VM, IN_HBM, IN_HBM],
        out_specs=(VM,) * 5,
        out_shape=(
            jax.ShapeDtypeStruct((GROUP, D), BF),
            jax.ShapeDtypeStruct((ROWS + TAIL, D), BF),
            jax.ShapeDtypeStruct((ROWS, H), BF),
            jax.ShapeDtypeStruct((ROWS, 2 * GROUP), BF),
            jax.ShapeDtypeStruct((ROWS, D), BF),
        ),
        scratch_shapes=[
            pltpu.VMEM((PACKED, LANES), F32),
            pltpu.VMEM((ROWS, D), F32),
            pltpu.VMEM((ROWS, D), BF),
            pltpu.VMEM((ROWS, D), F32),
            pltpu.VMEM((D, H), BF),
            pltpu.VMEM((H, D), BF),
            pltpu.SemaphoreType.DMA((2, H // HB)),
        ],
        compiler_params=params(48),
        cost_estimate=cost(4 * ROWS * D * H, 4 * D * H, 2 * ROWS * H),
    )(arr, gains, w1, w2)


HALF = PAIRS // DP


def load_units(near, far, unit, inverse, img, txt, keep):
    for i in range(DP):
        src = near if i < DP // 2 else far
        first = (i % (DP // 2)) * GROUP
        pooled = src[first : first + GROUP, :].astype(F32)
        inv = lax.rsqrt(jnp.sum(pooled * pooled, axis=1, keepdims=True) + EPS)
        u = pooled * inv
        if i < keep:
            unit[i * GROUP : (i + 1) * GROUP, :] = u
            inverse[i * GROUP : (i + 1) * GROUP, :] = inv
        u = u.reshape(NZ, 2 * NZ, D)
        img[i * HALF : (i + 1) * HALF, :] = u[:, :NZ].reshape(HALF, D).astype(BF)
        txt[i * HALF : (i + 1) * HALF, :] = u[:, NZ:].reshape(HALF, D).astype(BF)


def slopes(scalars, products):
    sharpness, shift, factor = scalars[0], scalars[1], scalars[2]
    logits = sharpness * products + shift
    diagonal = iota(products.shape, 0) == iota(products.shape, 1)
    sign = jnp.where(diagonal, 1.0, -1.0)
    return (-(factor / PAIRS) * sharpness) * sign * jax.nn.sigmoid(-sign * logits)


def pool_grads(g_img, g_txt, u, inv, gain):
    a, b = g_img.reshape(NZ, NZ, D), g_txt.reshape(NZ, NZ, D)
    grad = jnp.concatenate([a, b], axis=1).reshape(GROUP, D)
    share = jnp.where(iota((NZ, 2 * NZ, 1), 1) < NZ, 1.0 / IMG, 1.0 / TXT).reshape(GROUP, 1)
    return (inv * share) * (grad - u * jnp.sum(u * grad, axis=1, keepdims=True)) * gain


def own_loss(scalars, near, far, gains, unit, inverse, img, txt):
    load_units(near, far, unit, inverse, img, txt, 1)

    def side(mine, others):
        hi, low = two(slopes(scalars, dot(mine[:HALF, :], others[...], 1, 1)))
        both = dot(jnp.concatenate([hi, low], axis=0), others[...])
        return both[:HALF] + both[HALF:]

    return pool_grads(side(img, txt), side(txt, img), unit[...], inverse[...], gains[1:2, :])


def all_loss(scalars, near, far, gains, every, unit, inverse, img, txt):
    load_units(near, far, unit, inverse, img, txt, DP)
    slope = slopes(scalars, dot(img[...], txt[...], 1, 1)).astype(BF)
    g_img = dot(slope, txt[...])
    g_txt = dot(slope, img[...], 0, 0)
    for i in range(DP):
        at, half = slice(i * GROUP, (i + 1) * GROUP), slice(i * HALF, (i + 1) * HALF)
        every[i] = pool_grads(
            g_img[half], g_txt[half], unit[at, :], inverse[at, :], gains[1:2, :]
        ).astype(BF)


def merge_kernel(a, b, c, d, out):
    for i, piece in enumerate((a, b, c, d)):
        out[i * GROUP : (i + 1) * GROUP, :] = piece[...]


def merge(pieces):
    return pl.pallas_call(
        merge_kernel,
        out_shape=jax.ShapeDtypeStruct((DP // 2 * GROUP, D), BF),
        compiler_params=params(8),
    )(*pieces)


def backward_kernel(
    scalars, near, far, gains, bundle, hot, scaled_in, slope, w1, w2, out, mark,
    scr, mixed, rows, acc, unit, inverse, img, txt,
):
    hi, low = two(own_loss(scalars, near, far, gains, unit, inverse, img, txt))
    mixed[...] = dot(hot[:, :GROUP], hi) + dot(hot[:, :GROUP], low)

    def column(at, n):
        return jnp.sum(hot[at, GROUP + 3 * n : GROUP + 3 * n + 3].astype(F32), axis=1, keepdims=True)

    for j in range(CAP):
        at = slice(j * E, (j + 1) * E)
        grad = norm_back(mixed[at, :], bundle[at, :].astype(F32), column(at, 0))
        mixed[at, :] = grad
        rows[at, :] = (column(at, 2) * grad).astype(BF)
    for i in range(H // HB):
        at = slice(i * HB, (i + 1) * HB)
        hidden = (dot(rows[...], w2[at, :], 1, 1) * slope[:, at].astype(F32)).astype(BF)
        term = dot(hidden, w1[:, at], 1, 1)
        acc[...] = term if i == 0 else acc[...] + term
    for j in range(CAP):
        at = slice(j * E, (j + 1) * E)
        back = acc[at, :].astype(BF).astype(F32) * gains[0:1, :]
        mixed[at, :] += norm_back(back, scaled_in[at, :].astype(F32), column(at, 1))
    for row in (META, META + 1):
        scr[pl.ds(row, E, stride=SLAB), :] = jnp.zeros((E, LANES), F32)
    pack_rows(scr, mixed)
    out[...] = scr[...].astype(BF)
    mark[...] = jnp.zeros_like(mark)


def backward(scalars, near, far, gains, bundle, hot, scaled_in, slope, w1, w2):
    return pl.pallas_call(
        backward_kernel,
        in_specs=[pl.BlockSpec(memory_space=pltpu.SMEM)] + [VM] * 9,
        out_specs=(VM, VM),
        out_shape=(jax.ShapeDtypeStruct((PACKED, LANES), BF), MARK),
        scratch_shapes=[
            pltpu.VMEM((PACKED, LANES), F32),
            pltpu.VMEM((ROWS, D), F32),
            pltpu.VMEM((ROWS, D), BF),
            pltpu.VMEM((ROWS, D), F32),
            pltpu.VMEM((GROUP, D), F32),
            pltpu.VMEM((GROUP, 1), F32),
            pltpu.VMEM((PAIRS, D), BF),
            pltpu.VMEM((PAIRS, D), BF),
        ],
        compiler_params=params(24),
        cost_estimate=cost(4 * ROWS * D * H + 6 * GROUP * PAIRS * D, 4 * D * H + 2 * ROWS * H),
    )(scalars, near, far, gains, bundle, hot, scaled_in, slope, w1, w2)


def slice_kernel(
    dp, arr, gains, w1, pooled, normed_t, hidden_t, slope, passed, scr, x, normed, hidden, w1s, sem
):
    step = pl.program_id(0)
    at = pl.ds(pl.multiple_of(dp[0] * HS, HS), HS)
    copy = pltpu.make_async_copy(w1.at[:, at], w1s, sem)

    @pl.when(step == 0)
    def _():
        copy.start()
        passed[...] = pooled[...]

    scr[...] = arr[0].astype(F32)
    unpack_rows(scr, x)
    scaled, _inverse = norm(x[...])
    rows = (scaled * gains[0:1, :]).astype(BF)
    at = pl.ds(pl.multiple_of(step * ROWS, ROWS), ROWS)
    normed[at, :] = rows

    @pl.when(step == 0)
    def _():
        copy.wait()

    value, grad = gelu_parts(dot(rows, w1s[...]))
    hidden[at, :] = value.astype(BF)
    slope[...] = grad.astype(BF)

    @pl.when(step == pl.num_programs(0) - 1)
    def _():
        normed_t[...] = normed[...].T
        hidden_t[...] = hidden[...].T


ALL = DP * ROWS


def hidden_slice(dp, arrs, gains, w1, pooled):
    return pl.pallas_call(
        slice_kernel,
        grid_spec=pltpu.PrefetchScalarGridSpec(
            num_scalar_prefetch=1,
            grid=(DP,),
            in_specs=[
                pl.BlockSpec((1, PACKED, LANES), lambda h, dp: (h, 0, 0)),
                whole((2, D)),
                IN_HBM,
                whole((GROUP, D)),
            ],
            out_specs=(
                whole((D, ALL)),
                whole((HS, ALL)),
                pl.BlockSpec((ROWS, HS), lambda h, dp: (h, 0)),
                whole((GROUP, D)),
            ),
            scratch_shapes=[
                pltpu.VMEM((PACKED, LANES), F32),
                pltpu.VMEM((ROWS, D), F32),
                pltpu.VMEM((ALL, D), BF),
                pltpu.VMEM((ALL, HS), BF),
                pltpu.VMEM((D, HS), BF),
                pltpu.SemaphoreType.DMA,
            ],
        ),
        out_shape=(
            jax.ShapeDtypeStruct((D, ALL), BF),
            jax.ShapeDtypeStruct((HS, ALL), BF),
            jax.ShapeDtypeStruct((ALL, HS), BF),
            jax.ShapeDtypeStruct((GROUP, D), BF),
        ),
        compiler_params=params(40),
        cost_estimate=cost(2 * ALL * D * HS, 12000000, 2 * ALL * HS),
    )(dp, arrs, gains, w1, pooled)


def weights_kernel(
    dp, scalars, near, far, gains, bundle, slope, _, normed_t, hidden_t, w2, g_in, g_out, mark,
    hot, rows, hidden, normed, value, w2s, every, unit, inverse, img, txt, sem,
):
    step = pl.program_id(0)
    at = pl.ds(pl.multiple_of(dp[0] * HS, HS), HS)
    weights = pltpu.make_async_copy(w2.at[at, :], w2s, sem.at[0])
    late = [
        pltpu.make_async_copy(normed_t, normed, sem.at[1]),
        pltpu.make_async_copy(hidden_t, value, sem.at[2]),
    ]

    @pl.when(step == 0)
    def _():
        weights.start()
        for copy in late:
            copy.start()
        all_loss(scalars, near, far, gains, every, unit, inverse, img, txt)
        weights.wait()

    for b in range(2):
        meta = bundle[b, ROWS:, : 2 * LANES].astype(F32)
        meta = jnp.concatenate([meta[:, :LANES], meta[:, LANES:]], axis=0)
        fill_hot(hot, meta)
        place = (step ^ lax.div(dp[0], 2)) + 4 * (b ^ lax.rem(dp[0], 2))
        q = dot(hot[...], every[place])
        for j in range(CAP):
            at = slice(j * E, (j + 1) * E)
            grad = norm_back(q[at, :], bundle[b, at, :].astype(F32), meta_chance(meta, j))
            first = pl.multiple_of((2 * step + b) * ROWS + j * E, E)
            rows[pl.ds(first, E), :] = grad.astype(BF)
    at = pl.ds(pl.multiple_of(step * (2 * ROWS), 2 * ROWS), 2 * ROWS)
    hidden[at, :] = (dot(rows[at, :], w2s[...], 1, 1) * slope[...].astype(F32)).astype(BF)

    @pl.when(step == pl.num_programs(0) - 1)
    def _():
        for copy in late:
            copy.wait()
        g_in[...] = dot(normed[...], hidden[...]).astype(BF)
        g_out[...] = dot(value[...], rows[...]).astype(BF)
        mark[...] = jnp.zeros_like(mark)


def weight_grads(dp, scalars, near, far, gains, bundles, slope, after, normed_t, hidden_t, w2):
    return pl.pallas_call(
        weights_kernel,
        grid_spec=pltpu.PrefetchScalarGridSpec(
            num_scalar_prefetch=2,
            grid=(DP // 2,),
            in_specs=[
                whole((DP // 2 * GROUP, D)),
                whole((DP // 2 * GROUP, D)),
                whole((2, D)),
                pl.BlockSpec((2, ROWS + TAIL, D), lambda h, *_: (h, 0, 0)),
                pl.BlockSpec((2 * ROWS, HS), lambda h, *_: (h, 0)),
                whole(MARK.shape),
                IN_HBM,
                IN_HBM,
                IN_HBM,
            ],
            out_specs=(whole((D, HS)), whole((HS, D)), whole(MARK.shape)),
            scratch_shapes=[
                pltpu.VMEM((ROWS, GROUP), BF),
                pltpu.VMEM((ALL, D), BF),
                pltpu.VMEM((ALL, HS), BF),
                pltpu.VMEM((D, ALL), BF),
                pltpu.VMEM((HS, ALL), BF),
                pltpu.VMEM((HS, D), BF),
                pltpu.VMEM((DP, GROUP, D), BF),
                pltpu.VMEM((DP * GROUP, D), F32),
                pltpu.VMEM((DP * GROUP, 1), F32),
                pltpu.VMEM((PAIRS, D), BF),
                pltpu.VMEM((PAIRS, D), BF),
                pltpu.SemaphoreType.DMA((3,)),
            ],
        ),
        out_shape=(
            jax.ShapeDtypeStruct((D, HS), BF),
            jax.ShapeDtypeStruct((HS, D), BF),
            MARK,
        ),
        compiler_params=params(57),
        cost_estimate=cost(6 * ALL * D * HS + 10 * PAIRS * PAIRS * D, 15000000),
    )(dp, scalars, near, far, gains, bundles, slope, after, normed_t, hidden_t, w2)


def collect_kernel(arr, slot, _, out, scr, rows):
    scr[...] = arr[...].astype(F32)
    unpack_rows(scr, rows)
    taking = (iota((TOK, ROWS), 1) == slot[...].astype(jnp.int32)).astype(F32).astype(BF)
    out[...] = dot(taking, rows[...].astype(BF)).astype(BF)


def collect(arr, slot, after):
    return pl.pallas_call(
        collect_kernel,
        out_shape=jax.ShapeDtypeStruct((TOK, D), BF),
        scratch_shapes=[pltpu.VMEM((PACKED, LANES), F32), pltpu.VMEM((ROWS, D), F32)],
        compiler_params=params(16),
        cost_estimate=cost(2 * ROWS * TOK * D, 700000),
    )(arr, slot, after)


Z_GROUPS = [[x * NZ + z for z in range(NZ)] for x in range(NX)]


def to_experts(packed):
    slabs = packed.reshape(E, SLAB, LANES)
    slabs = lax.all_to_all(slabs, "expert", split_axis=0, concat_axis=0, tiled=True)
    return slabs.reshape(PACKED, LANES)


def along_z(values):
    return lax.all_to_all(
        values, "expert", split_axis=0, concat_axis=0, tiled=True, axis_index_groups=Z_GROUPS
    )


def swap(values, axis, size, by):
    return lax.ppermute(values, axis, [(i, i ^ by) for i in range(size)])


def on_device(
    incoming_elements,
    assigned_specialist,
    element_couple_kind,
    chosen_specialist_chance,
    specialist_layernorm_multiplier,
    final_layernorm_multiplier_vec,
    specialist_first_matrix,
    specialist_second_matrix,
    sharpness_factor,
    similarity_shift_term,
    objective_adjoint_factor,
):
    w1 = specialist_first_matrix[0]
    w2 = specialist_second_matrix[0]
    dp = lax.axis_index("dp").astype(jnp.int32).reshape(1)

    packed, slot, gains = dispatch(
        incoming_elements,
        assigned_specialist,
        element_couple_kind,
        chosen_specialist_chance,
        specialist_layernorm_multiplier,
        final_layernorm_multiplier_vec,
    )
    arr = to_experts(packed)
    arrs = lax.all_gather(arr, "dp", axis=0)
    part, bundle, slope, hot, scaled_in = forward(arr, gains, w1, w2)
    bundles = lax.all_gather(bundle, "dp", axis=0)

    part = along_z(part.reshape(NZ, 2 * NZ, D))
    part = jnp.sum(part.astype(F32), axis=0)
    others = [swap(part, "expert", E, NZ * m) for m in range(1, NX)]
    share = jnp.where(jnp.arange(2 * NZ) < NZ, 1.0 / IMG, 1.0 / TXT).astype(F32)
    pooled = (((part + others[0]) + (others[1] + others[2])) * share[:, None]).astype(BF)
    pooled = along_z(jnp.broadcast_to(pooled[None], (NZ, 2 * NZ, D))).reshape(GROUP, D)
    normed_t, hidden_t, grads, passed = hidden_slice(dp, arrs, gains, w1, pooled)
    near = merge([passed] + [swap(pooled, "dp", DP, m) for m in (2, 4, 6)])
    far = swap(near, "dp", DP, 1)

    scalars = jnp.concatenate([sharpness_factor, similarity_shift_term, objective_adjoint_factor])
    packed, mark = backward(scalars, near, far, gains, bundle, hot, scaled_in, slope, w1, w2)
    returned = to_experts(packed)
    grad_in, grad_out, mark = weight_grads(
        dp, scalars, near, far, gains, bundles, grads, mark, normed_t, hidden_t, w2
    )
    token_grads = collect(returned, slot, mark)
    return (token_grads, grad_in[None], grad_out[None])


def solution(mesh):
    return jax.shard_map(
        on_device,
        mesh=mesh,
        in_specs=(
            P(("expert", "dp"), None),
            P(("expert", "dp"), None),
            P(("expert", "dp")),
            P(("expert", "dp")),
            P(),
            P(),
            P("expert", None, None),
            P("expert", None, None),
            P(),
            P(),
            P(),
        ),
        out_specs=(P(("expert", "dp"), None), P("expert", None, "dp"), P("expert", "dp", None)),
        check_vma=False,
    )
```

```python
import jax
import jax.numpy as jnp
from jax import lax
from jax.experimental import pallas as pl
from jax.experimental.pallas import tpu as pltpu
from jax.sharding import PartitionSpec as P

D = 768
H = 3072
IMG = 50
TXT = 16
E = 32
DP = 8
NX = 4
NZ = 8
TOK = 132
CAP = 9
PAIRS = 512
ROWS = E * CAP
LANES = 128
CHUNKS = D // LANES
SLAB = 56
META = CAP * CHUNKS
TAIL = 16
PACKED = E * SLAB
HB = 1024
HS = H // DP
GROUP = 4 * E

EPS = 1e-06
ROOT_HALF = 0.7071067811865476
INV_ROOT_TAU = 0.3989422804014327
BF = jnp.bfloat16
F32 = jnp.float32


def params(mib):
    return pltpu.CompilerParams(vmem_limit_bytes=mib * 1024 * 1024)


def cost(flops, moved, trans=0):
    return pl.CostEstimate(flops=int(flops), bytes_accessed=int(moved), transcendentals=int(trans))


def dot(a, b, ca=1, cb=0):
    return lax.dot_general(a, b, (((ca,), (cb,)), ((), ())), preferred_element_type=F32)


def norm(values):
    center = values - jnp.mean(values, axis=1, keepdims=True)
    inverse = lax.rsqrt(jnp.mean(center * center, axis=1, keepdims=True) + EPS)
    return center * inverse, inverse


def norm_back(grad_hat, scaled, inverse):
    return inverse * (
        grad_hat
        - jnp.mean(grad_hat, axis=1, keepdims=True)
        - scaled * jnp.mean(grad_hat * scaled, axis=1, keepdims=True)
    )


def gelu_parts(v):
    e = jnp.exp(-0.5 * v * v)
    t = pl.reciprocal(1.0 + (0.3275911 * ROOT_HALF) * jnp.abs(v))
    tail = t * (0.5 * 1.061405429) + (0.5 * -1.453152027)
    tail = t * tail + (0.5 * 1.421413741)
    tail = t * tail + (0.5 * -0.284496736)
    tail = t * tail + (0.5 * 0.254829592)
    tail = t * tail * e
    cdf = jnp.where(v < 0.0, tail, 1.0 - tail)
    return v * cdf, cdf + v * e * INV_ROOT_TAU


def three(v):
    hi = v.astype(BF).astype(F32)
    mid = (v - hi).astype(BF).astype(F32)
    return hi, mid, v - hi - mid


def iota(shape, dim):
    return lax.broadcasted_iota(jnp.int32, shape, dim)


def pack_rows(scr, rows):
    for j in range(CAP):
        for c in range(CHUNKS):
            scr[pl.ds(c * CAP + j, E, stride=SLAB), :] = rows[
                j * E : (j + 1) * E, c * LANES : (c + 1) * LANES
            ]


def unpack_rows(scr, rows):
    for j in range(CAP):
        for c in range(CHUNKS):
            rows[j * E : (j + 1) * E, c * LANES : (c + 1) * LANES] = scr[
                pl.ds(c * CAP + j, E, stride=SLAB), :
            ]


def meta_chance(meta, j):
    return meta[:, j : j + 1] + meta[:, 16 + j : 17 + j] + meta[:, 32 + j : 33 + j]


def fill_hot(hot, meta):
    s, lane = iota((E, GROUP), 0), iota((E, GROUP), 1)
    first = (s % NZ) * (4 * NX) + s // NZ
    marks = [(lane == first + NX * k).astype(F32) for k in range(4)]
    for j in range(CAP):
        rows = jnp.zeros((E, GROUP), F32)
        for k in range(4):
            at = 48 + 16 * k + j
            rows += marks[k] * meta[:, at : at + 1]
        hot[j * E : (j + 1) * E, :GROUP] = rows.astype(BF)


def two(v):
    hi = v.astype(BF)
    return hi, (v - hi.astype(F32)).astype(BF)


VM = pl.BlockSpec(memory_space=pltpu.VMEM)
IN_HBM = pl.BlockSpec(memory_space=pltpu.HBM)
MARK = jax.ShapeDtypeStruct((8, LANES), F32)


def dispatch_kernel(x, route, kind, chance, gain_in, gain_out, out, slot, gains, scr, rows):
    gains[0:1, :] = gain_in[...].reshape(1, D)
    gains[1:2, :] = gain_out[...].reshape(1, D)
    eye = iota((TOK, TOK), 0) == iota((TOK, TOK), 1)

    def column(row):
        return jnp.sum(jnp.where(eye, row, 0.0), axis=1, keepdims=True)

    onehot = (iota((E, TOK), 0) == route[...]).astype(F32)
    upper = (iota((TOK, TOK), 0) <= iota((TOK, TOK), 1)).astype(BF)
    run = dot(onehot.astype(BF), upper)
    pos = jnp.sum(onehot * run, axis=0, keepdims=True) - 1.0
    target = pos * E + route[...].astype(F32)
    placing = (iota((ROWS, TOK), 0) == target.astype(jnp.int32)).astype(F32).astype(BF)
    rows[...] = dot(placing, x[...])

    slot[...] = column(target)
    lane = iota((TOK, LANES), 1)
    field = lane // 16
    hi, mid, low = three(column(chance[...]))
    same = (column(kind[...].astype(F32)).astype(jnp.int32) == field - 3).astype(F32)
    held = jnp.where(
        field == 0, hi, jnp.where(field == 1, mid, jnp.where(field == 2, low, same))
    )
    held = jnp.where(lane % 16 == column(pos).astype(jnp.int32), held, 0.0).astype(BF)
    scr[pl.ds(META, E, stride=SLAB), :] = dot(onehot.astype(BF), held)
    scr[pl.ds(META + 1, E, stride=SLAB), :] = jnp.zeros((E, LANES), F32)
    pack_rows(scr, rows)
    out[...] = scr[...].astype(BF)


def dispatch(x, route, kind, chance, gain_in, gain_out):
    return pl.pallas_call(
        dispatch_kernel,
        out_shape=(
            jax.ShapeDtypeStruct((PACKED, LANES), BF),
            jax.ShapeDtypeStruct((TOK, 1), F32),
            jax.ShapeDtypeStruct((2, D), F32),
        ),
        scratch_shapes=[pltpu.VMEM((PACKED, LANES), F32), pltpu.VMEM((ROWS, D), F32)],
        compiler_params=params(60),
        cost_estimate=cost(2 * ROWS * TOK * D, 700000),
    )(
        x,
        route.reshape(1, TOK),
        kind.reshape(1, TOK),
        chance.reshape(1, TOK),
        gain_in,
        gain_out,
    )


def forward_kernel(
    arr, gains, w1, w2, part, bundle, slope, hot, scaled_in,
    scr, x, normed, acc, w1v, w2v, sem,
):
    cols = [slice(i * HB, (i + 1) * HB) for i in range(H // HB)]
    fetches = [
        (
            pltpu.make_async_copy(w1.at[:, at], w1v.at[:, at], sem.at[0, i]),
            pltpu.make_async_copy(w2.at[at, :], w2v.at[at, :], sem.at[1, i]),
        )
        for i, at in enumerate(cols)
    ]
    for first, second in fetches:
        first.start()
        second.start()
    scr[...] = arr[...].astype(F32)
    unpack_rows(scr, x)
    scaled, inverse = norm(x[...])
    normed[...] = (scaled * gains[0:1, :]).astype(BF)
    scaled_in[...] = scaled.astype(BF)
    for f, v in enumerate(three(inverse)):
        hot[:, GROUP + 3 + f : GROUP + 4 + f] = v.astype(BF)
    for i, at in enumerate(cols):
        fetches[i][0].wait()
        hidden, grad = gelu_parts(dot(normed[...], w1v[:, at]))
        slope[:, at] = grad.astype(BF)
        fetches[i][1].wait()
        term = dot(hidden.astype(BF), w2v[at, :])
        acc[...] = term if i == 0 else acc[...] + term
    meta = scr[pl.ds(META, E, stride=SLAB), :]
    fill_hot(hot, meta)
    lane = iota((E, LANES), 1)
    routing = jnp.where(lane >= 48, meta, 0.0)
    for j in range(CAP):
        at = slice(j * E, (j + 1) * E)
        chance = meta_chance(meta, j)
        mixed = x[at, :] + chance * acc[at, :].astype(BF).astype(F32)
        scaled, inverse = norm(mixed)
        bundle[at, :] = scaled.astype(BF)
        for f, v in enumerate(three(inverse) + three(chance)):
            lane_at = GROUP + f + (3 if f > 2 else 0)
            hot[at, lane_at : lane_at + 1] = v.astype(BF)
        acc[at, :] = scaled * gains[1:2, :]
        for f, v in enumerate(three(chance * inverse)):
            routing = jnp.where(lane == 16 * f + j, v, routing)
    bundle[ROWS:, 2 * LANES :] = jnp.zeros((TAIL, D - 2 * LANES), BF)
    for c in range(E // TAIL):
        bundle[ROWS:, c * LANES : (c + 1) * LANES] = routing[c * TAIL : (c + 1) * TAIL].astype(BF)
    hi, low = two(acc[...])
    part[...] = (dot(hot[:, :GROUP], hi, 0, 0) + dot(hot[:, :GROUP], low, 0, 0)).astype(BF)


def whole(shape):
    return pl.BlockSpec(shape, lambda *_: (0,) * len(shape))


def forward(arr, gains, w1, w2):
    return pl.pallas_call(
        forward_kernel,
        in_specs=[VM, VM, IN_HBM, IN_HBM],
        out_specs=(VM,) * 5,
        out_shape=(
            jax.ShapeDtypeStruct((GROUP, D), BF),
            jax.ShapeDtypeStruct((ROWS + TAIL, D), BF),
            jax.ShapeDtypeStruct((ROWS, H), BF),
            jax.ShapeDtypeStruct((ROWS, 2 * GROUP), BF),
            jax.ShapeDtypeStruct((ROWS, D), BF),
        ),
        scratch_shapes=[
            pltpu.VMEM((PACKED, LANES), F32),
            pltpu.VMEM((ROWS, D), F32),
            pltpu.VMEM((ROWS, D), BF),
            pltpu.VMEM((ROWS, D), F32),
            pltpu.VMEM((D, H), BF),
            pltpu.VMEM((H, D), BF),
            pltpu.SemaphoreType.DMA((2, H // HB)),
        ],
        compiler_params=params(48),
        cost_estimate=cost(4 * ROWS * D * H, 4 * D * H, 2 * ROWS * H),
    )(arr, gains, w1, w2)


HALF = PAIRS // DP


def load_units(near, far, unit, inverse, img, txt, keep):
    for i in range(DP):
        src = near if i < DP // 2 else far
        first = (i % (DP // 2)) * GROUP
        pooled = src[first : first + GROUP, :].astype(F32)
        inv = lax.rsqrt(jnp.sum(pooled * pooled, axis=1, keepdims=True) + EPS)
        u = pooled * inv
        if i < keep:
            unit[i * GROUP : (i + 1) * GROUP, :] = u
            inverse[i * GROUP : (i + 1) * GROUP, :] = inv
        u = u.reshape(NZ, 2 * NZ, D)
        img[i * HALF : (i + 1) * HALF, :] = u[:, :NZ].reshape(HALF, D).astype(BF)
        txt[i * HALF : (i + 1) * HALF, :] = u[:, NZ:].reshape(HALF, D).astype(BF)


def slopes(scalars, products):
    sharpness, shift, factor = scalars[0], scalars[1], scalars[2]
    logits = sharpness * products + shift
    diagonal = iota(products.shape, 0) == iota(products.shape, 1)
    sign = jnp.where(diagonal, 1.0, -1.0)
    return (-(factor / PAIRS) * sharpness) * sign * jax.nn.sigmoid(-sign * logits)


def pool_grads(g_img, g_txt, u, inv, gain):
    a, b = g_img.reshape(NZ, NZ, D), g_txt.reshape(NZ, NZ, D)
    grad = jnp.concatenate([a, b], axis=1).reshape(GROUP, D)
    share = jnp.where(iota((NZ, 2 * NZ, 1), 1) < NZ, 1.0 / IMG, 1.0 / TXT).reshape(GROUP, 1)
    return (inv * share) * (grad - u * jnp.sum(u * grad, axis=1, keepdims=True)) * gain


def own_loss(scalars, near, far, gains, unit, inverse, img, txt):
    load_units(near, far, unit, inverse, img, txt, 1)

    def side(mine, others):
        slope = slopes(scalars, dot(mine[:HALF, :], others[...], 1, 1))
        return dot(slope.astype(BF), others[...])

    return pool_grads(side(img, txt), side(txt, img), unit[...], inverse[...], gains[1:2, :])


def all_loss(scalars, near, far, gains, every, unit, inverse, img, txt):
    load_units(near, far, unit, inverse, img, txt, DP)
    slope = slopes(scalars, dot(img[...], txt[...], 1, 1)).astype(BF)
    g_img = dot(slope, txt[...])
    g_txt = dot(slope, img[...], 0, 0)
    for i in range(DP):
        at, half = slice(i * GROUP, (i + 1) * GROUP), slice(i * HALF, (i + 1) * HALF)
        every[i] = pool_grads(
            g_img[half], g_txt[half], unit[at, :], inverse[at, :], gains[1:2, :]
        ).astype(BF)


def merge_kernel(a, b, c, d, out):
    for i, piece in enumerate((a, b, c, d)):
        out[i * GROUP : (i + 1) * GROUP, :] = piece[...]


def merge(pieces):
    return pl.pallas_call(
        merge_kernel,
        out_shape=jax.ShapeDtypeStruct((DP // 2 * GROUP, D), BF),
        compiler_params=params(8),
    )(*pieces)


def backward_kernel(
    scalars, near, far, gains, bundle, hot, scaled_in, slope, w1, w2, out, mark,
    scr, mixed, rows, acc, unit, inverse, img, txt,
):
    hi, low = two(own_loss(scalars, near, far, gains, unit, inverse, img, txt))
    mixed[...] = dot(hot[:, :GROUP], hi) + dot(hot[:, :GROUP], low)

    def column(at, n):
        return jnp.sum(hot[at, GROUP + 3 * n : GROUP + 3 * n + 3].astype(F32), axis=1, keepdims=True)

    for j in range(CAP):
        at = slice(j * E, (j + 1) * E)
        grad = norm_back(mixed[at, :], bundle[at, :].astype(F32), column(at, 0))
        mixed[at, :] = grad
        rows[at, :] = (column(at, 2) * grad).astype(BF)
    for i in range(H // HB):
        at = slice(i * HB, (i + 1) * HB)
        hidden = (dot(rows[...], w2[at, :], 1, 1) * slope[:, at].astype(F32)).astype(BF)
        term = dot(hidden, w1[:, at], 1, 1)
        acc[...] = term if i == 0 else acc[...] + term
    for j in range(CAP):
        at = slice(j * E, (j + 1) * E)
        back = acc[at, :].astype(BF).astype(F32) * gains[0:1, :]
        mixed[at, :] += norm_back(back, scaled_in[at, :].astype(F32), column(at, 1))
    for row in (META, META + 1):
        scr[pl.ds(row, E, stride=SLAB), :] = jnp.zeros((E, LANES), F32)
    pack_rows(scr, mixed)
    out[...] = scr[...].astype(BF)
    mark[...] = jnp.zeros_like(mark)


def backward(scalars, near, far, gains, bundle, hot, scaled_in, slope, w1, w2):
    return pl.pallas_call(
        backward_kernel,
        in_specs=[pl.BlockSpec(memory_space=pltpu.SMEM)] + [VM] * 9,
        out_specs=(VM, VM),
        out_shape=(jax.ShapeDtypeStruct((PACKED, LANES), BF), MARK),
        scratch_shapes=[
            pltpu.VMEM((PACKED, LANES), F32),
            pltpu.VMEM((ROWS, D), F32),
            pltpu.VMEM((ROWS, D), BF),
            pltpu.VMEM((ROWS, D), F32),
            pltpu.VMEM((GROUP, D), F32),
            pltpu.VMEM((GROUP, 1), F32),
            pltpu.VMEM((PAIRS, D), BF),
            pltpu.VMEM((PAIRS, D), BF),
        ],
        compiler_params=params(24),
        cost_estimate=cost(4 * ROWS * D * H + 6 * GROUP * PAIRS * D, 4 * D * H + 2 * ROWS * H),
    )(scalars, near, far, gains, bundle, hot, scaled_in, slope, w1, w2)


def slice_kernel(
    dp, arr, gains, w1, pooled, normed_t, hidden_t, slope, passed, scr, x, normed, hidden, w1s, sem
):
    step = pl.program_id(0)
    at = pl.ds(pl.multiple_of(dp[0] * HS, HS), HS)
    copy = pltpu.make_async_copy(w1.at[:, at], w1s, sem)

    @pl.when(step == 0)
    def _():
        copy.start()
        passed[...] = pooled[...]

    scr[...] = arr[0].astype(F32)
    unpack_rows(scr, x)
    scaled, _inverse = norm(x[...])
    rows = (scaled * gains[0:1, :]).astype(BF)
    at = pl.ds(pl.multiple_of(step * ROWS, ROWS), ROWS)
    normed[at, :] = rows

    @pl.when(step == 0)
    def _():
        copy.wait()

    value, grad = gelu_parts(dot(rows, w1s[...]))
    hidden[at, :] = value.astype(BF)
    slope[...] = grad.astype(BF)

    @pl.when(step == pl.num_programs(0) - 1)
    def _():
        normed_t[...] = normed[...].T
        hidden_t[...] = hidden[...].T


ALL = DP * ROWS


def hidden_slice(dp, arrs, gains, w1, pooled):
    return pl.pallas_call(
        slice_kernel,
        grid_spec=pltpu.PrefetchScalarGridSpec(
            num_scalar_prefetch=1,
            grid=(DP,),
            in_specs=[
                pl.BlockSpec((1, PACKED, LANES), lambda h, dp: (h, 0, 0)),
                whole((2, D)),
                IN_HBM,
                whole((GROUP, D)),
            ],
            out_specs=(
                whole((D, ALL)),
                whole((HS, ALL)),
                pl.BlockSpec((ROWS, HS), lambda h, dp: (h, 0)),
                whole((GROUP, D)),
            ),
            scratch_shapes=[
                pltpu.VMEM((PACKED, LANES), F32),
                pltpu.VMEM((ROWS, D), F32),
                pltpu.VMEM((ALL, D), BF),
                pltpu.VMEM((ALL, HS), BF),
                pltpu.VMEM((D, HS), BF),
                pltpu.SemaphoreType.DMA,
            ],
        ),
        out_shape=(
            jax.ShapeDtypeStruct((D, ALL), BF),
            jax.ShapeDtypeStruct((HS, ALL), BF),
            jax.ShapeDtypeStruct((ALL, HS), BF),
            jax.ShapeDtypeStruct((GROUP, D), BF),
        ),
        compiler_params=params(40),
        cost_estimate=cost(2 * ALL * D * HS, 12000000, 2 * ALL * HS),
    )(dp, arrs, gains, w1, pooled)


def weights_kernel(
    dp, scalars, near, far, gains, bundle, slope, _, normed_t, hidden_t, w2, g_in, g_out, mark,
    hot, rows, hidden, normed, value, w2s, every, unit, inverse, img, txt, sem,
):
    step = pl.program_id(0)
    at = pl.ds(pl.multiple_of(dp[0] * HS, HS), HS)
    weights = pltpu.make_async_copy(w2.at[at, :], w2s, sem.at[0])
    late = [
        pltpu.make_async_copy(normed_t, normed, sem.at[1]),
        pltpu.make_async_copy(hidden_t, value, sem.at[2]),
    ]

    @pl.when(step == 0)
    def _():
        weights.start()
        for copy in late:
            copy.start()
        all_loss(scalars, near, far, gains, every, unit, inverse, img, txt)
        weights.wait()

    for b in range(2):
        meta = bundle[b, ROWS:, : 2 * LANES].astype(F32)
        meta = jnp.concatenate([meta[:, :LANES], meta[:, LANES:]], axis=0)
        fill_hot(hot, meta)
        place = (step ^ lax.div(dp[0], 2)) + 4 * (b ^ lax.rem(dp[0], 2))
        q = dot(hot[...], every[place])
        for j in range(CAP):
            at = slice(j * E, (j + 1) * E)
            grad = norm_back(q[at, :], bundle[b, at, :].astype(F32), meta_chance(meta, j))
            first = pl.multiple_of((2 * step + b) * ROWS + j * E, E)
            rows[pl.ds(first, E), :] = grad.astype(BF)
    at = pl.ds(pl.multiple_of(step * (2 * ROWS), 2 * ROWS), 2 * ROWS)
    hidden[at, :] = (dot(rows[at, :], w2s[...], 1, 1) * slope[...].astype(F32)).astype(BF)

    @pl.when(step == pl.num_programs(0) - 1)
    def _():
        for copy in late:
            copy.wait()
        g_in[...] = dot(normed[...], hidden[...]).astype(BF)
        g_out[...] = dot(value[...], rows[...]).astype(BF)
        mark[...] = jnp.zeros_like(mark)


def weight_grads(dp, scalars, near, far, gains, bundles, slope, after, normed_t, hidden_t, w2):
    return pl.pallas_call(
        weights_kernel,
        grid_spec=pltpu.PrefetchScalarGridSpec(
            num_scalar_prefetch=2,
            grid=(DP // 2,),
            in_specs=[
                whole((DP // 2 * GROUP, D)),
                whole((DP // 2 * GROUP, D)),
                whole((2, D)),
                pl.BlockSpec((2, ROWS + TAIL, D), lambda h, *_: (h, 0, 0)),
                pl.BlockSpec((2 * ROWS, HS), lambda h, *_: (h, 0)),
                whole(MARK.shape),
                IN_HBM,
                IN_HBM,
                IN_HBM,
            ],
            out_specs=(whole((D, HS)), whole((HS, D)), whole(MARK.shape)),
            scratch_shapes=[
                pltpu.VMEM((ROWS, GROUP), BF),
                pltpu.VMEM((ALL, D), BF),
                pltpu.VMEM((ALL, HS), BF),
                pltpu.VMEM((D, ALL), BF),
                pltpu.VMEM((HS, ALL), BF),
                pltpu.VMEM((HS, D), BF),
                pltpu.VMEM((DP, GROUP, D), BF),
                pltpu.VMEM((DP * GROUP, D), F32),
                pltpu.VMEM((DP * GROUP, 1), F32),
                pltpu.VMEM((PAIRS, D), BF),
                pltpu.VMEM((PAIRS, D), BF),
                pltpu.SemaphoreType.DMA((3,)),
            ],
        ),
        out_shape=(
            jax.ShapeDtypeStruct((D, HS), BF),
            jax.ShapeDtypeStruct((HS, D), BF),
            MARK,
        ),
        compiler_params=params(57),
        cost_estimate=cost(6 * ALL * D * HS + 10 * PAIRS * PAIRS * D, 15000000),
    )(dp, scalars, near, far, gains, bundles, slope, after, normed_t, hidden_t, w2)


def collect_kernel(arr, slot, _, out, scr, rows):
    scr[...] = arr[...].astype(F32)
    unpack_rows(scr, rows)
    taking = (iota((TOK, ROWS), 1) == slot[...].astype(jnp.int32)).astype(F32).astype(BF)
    out[...] = dot(taking, rows[...].astype(BF)).astype(BF)


def collect(arr, slot, after):
    return pl.pallas_call(
        collect_kernel,
        out_shape=jax.ShapeDtypeStruct((TOK, D), BF),
        scratch_shapes=[pltpu.VMEM((PACKED, LANES), F32), pltpu.VMEM((ROWS, D), F32)],
        compiler_params=params(16),
        cost_estimate=cost(2 * ROWS * TOK * D, 700000),
    )(arr, slot, after)


Z_GROUPS = [[x * NZ + z for z in range(NZ)] for x in range(NX)]


def to_experts(packed):
    slabs = packed.reshape(E, SLAB, LANES)
    slabs = lax.all_to_all(slabs, "expert", split_axis=0, concat_axis=0, tiled=True)
    return slabs.reshape(PACKED, LANES)


def along_z(values):
    return lax.all_to_all(
        values, "expert", split_axis=0, concat_axis=0, tiled=True, axis_index_groups=Z_GROUPS
    )


def swap(values, axis, size, by):
    return lax.ppermute(values, axis, [(i, i ^ by) for i in range(size)])


def on_device(
    incoming_elements,
    assigned_specialist,
    element_couple_kind,
    chosen_specialist_chance,
    specialist_layernorm_multiplier,
    final_layernorm_multiplier_vec,
    specialist_first_matrix,
    specialist_second_matrix,
    sharpness_factor,
    similarity_shift_term,
    objective_adjoint_factor,
):
    w1 = specialist_first_matrix[0]
    w2 = specialist_second_matrix[0]
    dp = lax.axis_index("dp").astype(jnp.int32).reshape(1)

    packed, slot, gains = dispatch(
        incoming_elements,
        assigned_specialist,
        element_couple_kind,
        chosen_specialist_chance,
        specialist_layernorm_multiplier,
        final_layernorm_multiplier_vec,
    )
    arr = to_experts(packed)
    arrs = lax.all_gather(arr, "dp", axis=0)
    part, bundle, slope, hot, scaled_in = forward(arr, gains, w1, w2)
    bundles = lax.all_gather(bundle, "dp", axis=0)

    part = along_z(part.reshape(NZ, 2 * NZ, D))
    part = jnp.sum(part.astype(F32), axis=0).astype(BF)
    others = [swap(part, "expert", E, NZ * m) for m in range(1, NX)]
    share = jnp.where(jnp.arange(2 * NZ) < NZ, 1.0 / IMG, 1.0 / TXT).astype(F32)
    part, others = part.astype(F32), [other.astype(F32) for other in others]
    pooled = (((part + others[0]) + (others[1] + others[2])) * share[:, None]).astype(BF)
    pooled = along_z(jnp.broadcast_to(pooled[None], (NZ, 2 * NZ, D))).reshape(GROUP, D)
    normed_t, hidden_t, grads, passed = hidden_slice(dp, arrs, gains, w1, pooled)
    near = merge([passed] + [swap(pooled, "dp", DP, m) for m in (2, 4, 6)])
    far = swap(near, "dp", DP, 1)

    scalars = jnp.concatenate([sharpness_factor, similarity_shift_term, objective_adjoint_factor])
    packed, mark = backward(scalars, near, far, gains, bundle, hot, scaled_in, slope, w1, w2)
    returned = to_experts(packed)
    grad_in, grad_out, mark = weight_grads(
        dp, scalars, near, far, gains, bundles, grads, mark, normed_t, hidden_t, w2
    )
    token_grads = collect(returned, slot, mark)
    return (token_grads, grad_in[None], grad_out[None])


def solution(mesh):
    return jax.shard_map(
        on_device,
        mesh=mesh,
        in_specs=(
            P(("expert", "dp"), None),
            P(("expert", "dp"), None),
            P(("expert", "dp")),
            P(("expert", "dp")),
            P(),
            P(),
            P("expert", None, None),
            P("expert", None, None),
            P(),
            P(),
            P(),
        ),
        out_specs=(P(("expert", "dp"), None), P("expert", None, "dp"), P("expert", "dp", None)),
        check_vma=False,
    )
```
